32 devices in a mesh: dp: 4 (over y, x), seq: 8 (over z, core).
Axes of the slice: x: 2, y: 2, z: 4, core: 2. Of those that a mesh axis runs over, the one named last changes fastest.
Arguments:
- hidden_in: bfloat16 [8192, 1024], P(('dp', 'seq')), may hold values from -6 to 6
- task_ids: int32 [4], P('dp'), may hold values from 0 to 2
- prefix_keys: bfloat16 [100, 1024], replicated, may hold values from -6 to 6
- prefix_values: bfloat16 [100, 1024], replicated, may hold values from -6 to 6
- query_weight: bfloat16 [1024, 1024], replicated, may hold values from -0.1875 to 0.1875
- query_bias: bfloat16 [1024], replicated, may hold values from -3 to 3
- key_weight: bfloat16 [1024, 1024], replicated, may hold values from -0.1875 to 0.1875
- key_bias: bfloat16 [1024], replicated, may hold values from -3 to 3
- value_weight: bfloat16 [1024, 1024], replicated, may hold values from -0.1875 to 0.1875
- value_bias: bfloat16 [1024], replicated, may hold values from -3 to 3
- out_weight: bfloat16 [1024, 1024], replicated, may hold values from -8 to 8
- out_bias: bfloat16 [1024], replicated, may hold values from -3 to 3
- norm1_gain: bfloat16 [1024], replicated, may hold values from 0.099609375 to 1.8984375
- norm1_bias: bfloat16 [1024], replicated, may hold values from -3 to 3
- up_weight: bfloat16 [1024, 4096], replicated, may hold values from -0.1875 to 0.1875
- up_bias: bfloat16 [4096], replicated, may hold values from -3 to 3
- down_weight: bfloat16 [4096, 1024], replicated, may hold values from -0.09375 to 0.09375
- down_bias: bfloat16 [1024], replicated, may hold values from -3 to 3
- norm2_gain: bfloat16 [1024], replicated, may hold values from 0.099609375 to 1.8984375
- norm2_bias: bfloat16 [1024], replicated, may hold values from -3 to 3
- out_grad: bfloat16 [8192, 1024], P(('dp', 'seq')), may hold values from -6 to 6
Outputs:
- layer_out: bfloat16 [8192, 1024], P(('dp', 'seq'))
- input_grad: bfloat16 [8192, 1024], P(('dp', 'seq'))
- prefix_key_grad: float32 [100, 1024], replicated
- prefix_value_grad: float32 [100, 1024], replicated
The draws below stay inside these ranges and needn't reach their ends.
Inputs may be any that keep to these rules, and one draw needn't show every extreme that they name: `task_ids`: task id of each sequence; ids 0, 1 and 2 keep 20, 64 and 100 prefix slots.
All inputs are finite; a program needn't handle non-finite values.
Results may differ from the reference program's by a relative error of at most 0.019.
Values may be sent and summed in bfloat16 or wider, within the bound.
No kernel may reach another device: no remote copies, remote signals or barrier semaphores. Data moves between devices by JAX's collectives and lax.ppermute only.
A program may use at most 256 MiB of HBM per device.

```python
import math
import jax
import jax.numpy as jnp
from jax import lax

D = 1024
HEADS = 16
HEAD_DIM = 64
FF = 4096
PREFIX = 100
LENGTH = 2048
SEQS = 4
TOKENS = 8192


def plant(values, key, low, top_value):
    shape = values.shape
    place = [jax.random.randint(jax.random.fold_in(key, axis), (), 0, shape[axis]) for axis in range(len(shape))]
    values = values.at[tuple(place)].set(low)
    longest = shape.index(max(shape))
    place[longest] = (place[longest] + 1) % shape[longest]
    return values.at[tuple(place)].set(top_value)


def block_scale(own_key, dims, cuts, least, high):
    loudness, own = 1.0, jax.random.fold_in(own_key, 6)
    for axis_at, shards_of in cuts:
        heights = jnp.exp(jax.random.uniform(jax.random.fold_in(own, axis_at), (shards_of,), jnp.float32, least / len(cuts), high / len(cuts)))
        loudness = loudness * jnp.repeat(heights, dims[axis_at] // shards_of).reshape([-1 if axis == axis_at else 1 for axis in range(len(dims))])
    return loudness


def bell_draw(rng, dims, scale, most, cuts=(), kind=jnp.bfloat16):
    factor_of = block_scale(rng, dims, cuts, -0.22, 0.18) if cuts else 1.0
    result = jax.random.normal(rng, dims, jnp.float32) * scale * factor_of
    return jnp.minimum(jnp.maximum(result, -most), most).astype(kind)


def setup_inputs(seed: int = 0) -> dict:
    key_of = jax.random.split(jax.random.key(seed), 22)
    return {
        "hidden_in": bell_draw(key_of[0], (TOKENS, D), 1.0, 6.0, ((0, 32),)),
        "task_ids": plant(jax.random.randint(key_of[1], (SEQS,), 0, 3), jax.random.fold_in(key_of[1], 1), 0, 2).astype(jnp.int32),
        "prefix_keys": bell_draw(key_of[2], (PREFIX, D), 1.0, 6.0),
        "prefix_values": bell_draw(key_of[3], (PREFIX, D), 1.0, 6.0),
        "query_weight": bell_draw(key_of[4], (D, D), D ** -0.5, 0.1875),
        "query_bias": bell_draw(key_of[5], (D,), 0.5, 3.0),
        "key_weight": bell_draw(key_of[6], (D, D), D ** -0.5, 0.1875),
        "key_bias": bell_draw(key_of[7], (D,), 0.5, 3.0),
        "value_weight": bell_draw(key_of[8], (D, D), D ** -0.5, 0.1875),
        "value_bias": bell_draw(key_of[9], (D,), 0.5, 3.0),
        "out_weight": bell_draw(key_of[10], (D, D), ((LENGTH // D) ** 0.5), 8.0),
        "out_bias": bell_draw(key_of[11], (D,), 0.5, 3.0),
        "norm1_gain": jnp.clip(1.0 + 0.18 * jax.random.normal(key_of[12], (D,), jnp.float32), 0.099609375, 1.8984375).astype(jnp.bfloat16),
        "norm1_bias": bell_draw(key_of[13], (D,), 0.5, 3.0),
        "up_weight": bell_draw(key_of[14], (D, FF), D ** -0.5, 0.1875),
        "up_bias": bell_draw(key_of[15], (FF,), 0.5, 3.0),
        "down_weight": bell_draw(key_of[16], (FF, D), FF ** -0.5, 0.09375),
        "down_bias": bell_draw(key_of[17], (D,), 0.5, 3.0),
        "norm2_gain": jnp.clip(1.0 + 0.18 * jax.random.normal(key_of[18], (D,), jnp.float32), 0.099609375, 1.8984375).astype(jnp.bfloat16),
        "norm2_bias": bell_draw(key_of[19], (D,), 0.5, 3.0),
        "out_grad": bell_draw(key_of[20], (TOKENS, D), 1.0, 6.0, ((0, 32),)),
    }


@jax.custom_vjp
def low(v):
    return lax.optimization_barrier(v.astype(jnp.bfloat16)).astype(jnp.float32)

@jax.custom_vjp
def low_back(v):
    return v

def low_keep(v):
    return (low(v), None)

def low_pass(kept, grad):
    return (grad,)

def back_keep(v):
    return (v, None)

def back_low(kept, grad):
    return (low(grad),)
low.defvjp(low_keep, low_pass)
low_back.defvjp(back_keep, back_low)
eps_norm = 1e-05
masked_score = -1e+30

def matmul_hi(left, right):
    return jnp.dot(left, right, precision=lax.Precision.HIGHEST)

def heads_of(matrix):
    return matrix.reshape(matrix.shape[0], HEADS, HEAD_DIM)

def layer_norm(values, gain, shift):
    center = values - lax.optimization_barrier(jnp.mean(values, axis=-1, keepdims=True))
    spread = lax.optimization_barrier(jnp.mean(center * center, axis=-1, keepdims=True))
    return center * lax.rsqrt(spread + eps_norm) * gain + shift

def attend(query_block, all_keys, all_values, keep_all):
    query_heads = heads_of(query_block)
    raw_scores = jnp.einsum('qhd,khd->hqk', query_heads, heads_of(all_keys), precision=lax.Precision.HIGHEST)
    scores = low_back(raw_scores * 0.125)
    scores = jnp.where(keep_all[None, None, :], scores, masked_score)
    largest = lax.optimization_barrier(jnp.max(scores, axis=-1, keepdims=True))
    exp_scores = jnp.exp(scores - largest)
    probs = exp_scores / lax.optimization_barrier(jnp.sum(exp_scores, axis=-1, keepdims=True))
    attended = jnp.einsum('hqk,khd->qhd', low(probs), heads_of(all_values), precision=lax.Precision.HIGHEST)
    return attended.reshape(query_block.shape[0], HEADS * HEAD_DIM)

def encoder_layer(seq_in, prefix_len, prefix_keys, prefix_values, weights):
    query_weight, query_bias, key_weight, key_bias, value_weight, value_bias, out_weight, out_bias, norm1_gain, norm1_bias, up_weight, up_bias, down_weight, down_bias, norm2_gain, norm2_bias = weights
    queries = low_back(low(matmul_hi(seq_in, query_weight) + query_bias))
    keys = low_back(low(matmul_hi(seq_in, key_weight) + key_bias))
    values = low_back(low(matmul_hi(seq_in, value_weight) + value_bias))
    keep_all = jnp.concatenate([jnp.arange(PREFIX) < prefix_len, jnp.ones((LENGTH,), dtype=jnp.bool_)])
    all_keys = jnp.concatenate([prefix_keys, keys], axis=0)
    all_values = jnp.concatenate([prefix_values, values], axis=0)
    block_size = math.gcd(LENGTH, 512)
    attend_block = jax.checkpoint(lambda query_block: attend(query_block, all_keys, all_values, keep_all))
    attended = lax.map(attend_block, queries.reshape(LENGTH // block_size, block_size, D)).reshape(LENGTH, D)
    attended = low_back(low(attended))
    branch = low_back(matmul_hi(attended, out_weight) + out_bias)
    first_norm = layer_norm(seq_in + branch, norm1_gain, norm1_bias)
    pre_act = low_back(matmul_hi(low(first_norm), up_weight) + up_bias)
    activation = low(jax.nn.gelu(pre_act, approximate=False))
    ffn_out = low_back(matmul_hi(activation, down_weight) + down_bias)
    return layer_norm(first_norm + ffn_out, norm2_gain, norm2_bias)

def reference(hidden_in, task_ids, prefix_keys, prefix_values, query_weight, query_bias, key_weight, key_bias, value_weight, value_bias, out_weight, out_bias, norm1_gain, norm1_bias, up_weight, up_bias, down_weight, down_bias, norm2_gain, norm2_bias, out_grad):
    weights = tuple((item.astype(jnp.float32) for item in (query_weight, query_bias, key_weight, key_bias, value_weight, value_bias, out_weight, out_bias, norm1_gain, norm1_bias, up_weight, up_bias, down_weight, down_bias, norm2_gain, norm2_bias)))
    seq_inputs = hidden_in.astype(jnp.float32).reshape(SEQS, LENGTH, D)
    lengths = jnp.where(task_ids == 0, 20, jnp.where(task_ids == 1, 64, PREFIX)).astype(jnp.int32)

    def forward(seq_all, prefix_key_rows, prefix_value_rows):

        def per_seq(seq_item):
            return encoder_layer(seq_item[0], seq_item[1], prefix_key_rows, prefix_value_rows, weights)
        return lax.map(per_seq, (seq_all, lengths))
    layer_rows, pullback = jax.vjp(forward, seq_inputs, prefix_keys.astype(jnp.float32), prefix_values.astype(jnp.float32))
    grad_input, grad_keys, grad_values = pullback(out_grad.astype(jnp.float32).reshape(SEQS, LENGTH, D))
    return (layer_rows.reshape(TOKENS, D).astype(jnp.bfloat16), grad_input.reshape(TOKENS, D).astype(jnp.bfloat16), grad_keys, grad_values)
```

```python
import functools
from typing import Any, NamedTuple

import jax
import jax.numpy as jnp
from jax import lax
from jax.experimental import pallas as pl
from jax.experimental.pallas import tpu as pltpu
from jax.sharding import PartitionSpec as P

HEAD_DIM = 64
LANES = 128
F32 = jnp.float32
BF16 = jnp.bfloat16
eps_norm = 1e-05
masked_score = -1e30
root_half = 0.7071067811865476
inv_root_tau = 0.3989422804014327
MARGIN = 8 * 1024 * 1024
COST = 0.05
NT = (((1,), (1,)), ((), ()))
NN = (((1,), (0,)), ((), ()))


def dot(left, right, dims=NN):
    return lax.dot_general(left, right, dims, preferred_element_type=F32)


def lane_iota(rows):
    return lax.broadcasted_iota(jnp.int32, (rows, LANES), 1)


def stack_pair(block, low_half):
    zero = jnp.zeros_like(block)
    return jnp.concatenate(
        [jnp.where(low_half, block, zero), jnp.where(low_half, zero, block)], axis=0
    )


def lanes_of(p):
    return slice(p * LANES, (p + 1) * LANES)


def row_of(ref):
    return ref[...].astype(F32).reshape(1, -1)


def kept_slots(task_ref, slot_count):
    task = task_ref[0]
    return jnp.where(task == 0, 20, jnp.where(task == 1, 64, slot_count))


def start_copies(pairs_of_refs, sems, at=0):
    copies = [
        pltpu.make_async_copy(src, dst, sems.at[at + i]) for i, (src, dst) in enumerate(pairs_of_refs)
    ]
    for copy in copies:
        copy.start()
    return copies


def piece_of(ref, piece):
    axis, at, count = piece
    return ref.at[:, pl.ds(at, count)] if axis else ref.at[pl.ds(at, count), :]


def fwd_kernel(n_parts, first, far, pairs, pieces, *refs):
    refs = list(refs)

    def take(count):
        got = refs[:count]
        del refs[:count]
        return got

    parts = take(n_parts)
    if first:
        weights_far, vectors, (prefix_keys, prefix_values, task) = take(3), take(3), take(3)
    else:
        weights, (biases,), (stacked_in, top_in, sum_in, acc_in) = take(3), take(1), take(4)
    ahead_far = take(len(pieces))
    rows_out = take(3)
    if first:
        stacked_out, prefix_k, prefix_v = take(3)
        weights, (biases,) = take(3), take(1)
    top_out, sum_out, acc_out = take(3)
    ahead = take(len(pieces))
    q_out, k_out, v_out = take(3) if far else rows_out
    (sems,) = take(1)
    rows = acc_out.shape[0]
    low_half = lane_iota(rows) < HEAD_DIM
    arriving = []
    if first:
        wide = weights[0].shape[1] // 2
        for i, (src, dst) in enumerate(zip(weights_far, weights)):
            moves = [
                (src.at[:, pl.ds(n * wide, wide)], dst.at[:, pl.ds(n * wide, wide)])
                for n in range(2)
            ]
            arriving.append(start_copies(moves, sems, 3 + 2 * i))
    coming = [(piece_of(src, piece), dst) for src, piece, dst in zip(ahead_far, pieces, ahead)]
    coming = start_copies(coming, sems, 9)
    if first:
        for i, vector in enumerate(vectors):
            biases[i : i + 1, :] = row_of(vector)
    leaving = []
    for i, (weight, out) in enumerate(zip(weights, (q_out, k_out, v_out))):
        width = weight.shape[1]
        split = 2 if arriving else 1
        for n in range(split):
            if arriving:
                arriving[i][n].wait()
            cols = slice(n * width // split, (n + 1) * width // split)
            at = 0
            for part in parts:
                here = slice(at, at + part.shape[0])
                at += part.shape[0]
                block = (dot(part[...], weight[:, cols]) + biases[i : i + 1, cols]).astype(BF16)
                out[here, cols] = block * jnp.asarray(0.125, BF16) if i == 0 else block
        if far:
            leaving += start_copies([(out, rows_out[i])], sems, i)
    if first:
        slot_count = prefix_keys.shape[0]
        prefix_k[...] = jnp.zeros_like(prefix_k)
        prefix_v[...] = jnp.zeros_like(prefix_v)
        prefix_k[0:slot_count, :] = prefix_keys[...]
        prefix_v[0:slot_count, :] = prefix_values[...]
        slot = lax.broadcasted_iota(jnp.int32, (1, prefix_k.shape[0]), 1)
        slot_bias = jnp.where(slot < kept_slots(task, slot_count), 0.0, masked_score)
    for p in range(pairs):
        cols = lanes_of(p)
        sources = [(k_out[:, cols], v_out[:, cols], None)]
        if first:
            stacked = stack_pair(q_out[:, cols], low_half)
            stacked_out[p] = stacked
            sources.append((prefix_k[:, cols], prefix_v[:, cols], slot_bias))
        else:
            stacked = stacked_in[p]
        tiles = []
        for key, value, bias in sources:
            score = dot(stacked, key, NT)
            if bias is not None:
                score = score + bias
            tiles.append([score[:, i : i + LANES] for i in range(0, score.shape[1], LANES)])
        top = functools.reduce(jnp.maximum, sum(tiles, []))
        top = jnp.broadcast_to(jnp.max(top, axis=1, keepdims=True), top.shape)
        if not first:
            top = jnp.maximum(top, top_in[p])
        top_out[p] = top
        total = None
        for (key, value, bias), group in zip(sources, tiles):
            probs = jnp.concatenate([jnp.exp(tile - top).astype(BF16) for tile in group], axis=1)
            wide = jnp.concatenate([value, jnp.ones_like(value)], axis=1)
            term = dot(probs, wide)
            total = term if total is None else total + term
        acc = jnp.where(low_half, total[0:rows, 0:LANES], total[rows:, 0:LANES])
        sums = jnp.where(low_half, total[0:rows, LANES:], total[rows:, LANES:])
        if not first:
            alpha = jnp.exp(top_in[p] - top)
            alpha = jnp.where(low_half, alpha[0:rows], alpha[rows:])
            sums = sums + sum_in[:, cols] * alpha
            acc = acc + acc_in[:, cols] * alpha
        sum_out[:, cols] = sums
        acc_out[:, cols] = acc
    for copy in leaving + coming:
        copy.wait()


def size_of(shape, kind):
    n = jnp.dtype(kind).itemsize
    for dim in shape:
        n *= dim
    return n


class Arg(NamedTuple):
    array: Any
    how: str = "copy"


class Out(NamedTuple):
    shape: tuple
    kind: Any
    how: str = "vmem"


def call(kernel, outs, args, flops, name, scratch=(), side=None, spare=MARGIN):
    outs, args, scratch = list(outs), list(args), list(scratch)
    n_args, n_outs = len(args), len(outs)
    if side is not None:
        side_kernel, side_outs, side_args = side
        args += side_args
        outs += side_outs
    copied = [i for i, a in enumerate(args) if a.how == "copy"]
    held = sum(size_of(a.array.shape, a.array.dtype) for a in args if a.how in ("copy", "auto"))
    held += sum(size_of(o.shape, o.kind) for o in outs if o.how == "auto")
    held += sum(size_of(*o) for o in scratch if isinstance(o, tuple))
    spaces = {
        "vmem": pltpu.VMEM,
        "auto": pltpu.VMEM,
        "copy": pltpu.HBM,
        "hbm": pltpu.HBM,
        "smem": pltpu.SMEM,
    }

    def placed(arg):
        if arg.how in ("vmem", "hbm", "copy"):
            return pltpu.with_memory_space_constraint(arg.array, spaces[arg.how])
        return arg.array

    own = [(args[i].array.shape, args[i].array.dtype) for i in copied]
    if copied:
        own.append(pltpu.SemaphoreType.DMA((len(copied),)))

    def body(*refs):
        ins = list(refs[: len(args)])
        results = refs[len(args) : len(args) + len(outs)]
        extra = refs[len(args) + len(outs) :]
        if copied:
            sems = extra[len(copied)]
            copies = start_copies([(ins[i], extra[n]) for n, i in enumerate(copied)], sems)
            for n, i in enumerate(copied):
                ins[i] = extra[n]
            for copy in copies:
                copy.wait()
        if side is not None:
            side_kernel(*ins[n_args:], *results[n_outs:])
        kernel(*ins[:n_args], *results[:n_outs], *extra[len(own) :])

    n_bytes = sum(size_of(a.array.shape, a.array.dtype) for a in args if a.how != "vmem")
    got = pl.pallas_call(
        body,
        out_shape=[
            (pltpu.VMEM if o.how == "vmem" else pltpu.HBM)(o.shape, o.kind) for o in outs
        ],
        in_specs=[pl.BlockSpec(memory_space=spaces[a.how]) for a in args],
        out_specs=[pl.BlockSpec(memory_space=spaces[o.how]) for o in outs],
        scratch_shapes=[pltpu.VMEM(*o) if isinstance(o, tuple) else o for o in own + scratch],
        compiler_params=pltpu.CompilerParams(vmem_limit_bytes=held + spare),
        cost_estimate=pl.CostEstimate(
            flops=int(flops * COST), bytes_accessed=int(n_bytes * COST), transcendentals=0
        ),
        name=name,
    )(*[placed(a) for a in args])
    return (got[:n_outs], got[n_outs:]) if side is not None else got


def norm_forward(values, gain, shift):
    center = values - jnp.mean(values, axis=-1, keepdims=True)
    inv_spread = lax.rsqrt(jnp.mean(center * center, axis=-1, keepdims=True) + eps_norm)
    normed = center * inv_spread
    return (normed * gain + shift, normed, inv_spread)


def norm_backward(upstream, normed, inv_spread, gain):
    scaled = upstream * gain
    return inv_spread * (
        scaled
        - jnp.mean(scaled, axis=-1, keepdims=True)
        - normed * jnp.mean(scaled * normed, axis=-1, keepdims=True)
    )


def middle_kernel(
    pairs, n_up, hidden, m_in, l_in, acc_in, grad, bo, g1, s1, up_bias, down_bias, g2, s2, wo, *refs
):
    up, down = refs[:n_up], refs[n_up : 2 * n_up]
    layer_out, res_out, *pay_outs, slope_ref = refs[2 * n_up :]
    rows, width = hidden.shape
    chunk = up[0].shape[1]
    low_half = lane_iota(rows) < HEAD_DIM
    lane = lane_iota(rows)
    vec = row_of
    sums = l_in[...]
    attended = acc_in[...] / sums
    residual = hidden[...].astype(F32) + dot(attended.astype(BF16), wo[...]) + vec(bo)
    first_norm, first_normed, first_spread = norm_forward(residual, vec(g1), vec(s1))
    first_low = first_norm.astype(BF16)
    ffn = jnp.zeros((rows, width), F32)
    up_row = row_of(up_bias)
    for c in range(n_up):
        cols = slice(c * chunk, (c + 1) * chunk)
        pre = dot(first_low, up[c][...]) + up_row[:, cols]
        phi = 0.5 * (1.0 + lax.erf(pre * root_half))
        slope_ref[:, cols] = (phi + pre * jnp.exp(-0.5 * pre * pre) * inv_root_tau).astype(BF16)
        ffn = ffn + dot((pre * phi).astype(BF16), down[c][...])
    layer, second_normed, second_spread = norm_forward(
        first_norm + ffn + vec(down_bias), vec(g2), vec(s2)
    )
    layer_out[...] = layer.astype(BF16)
    sum_grad = norm_backward(grad[...].astype(F32), second_normed, second_spread, vec(g2))
    sum_low = sum_grad.astype(BF16)
    first_grad = sum_grad
    for c in range(n_up):
        cols = slice(c * chunk, (c + 1) * chunk)
        pre_grad = dot(sum_low, down[c][...], NT) * slope_ref[:, cols]
        first_grad = first_grad + dot(pre_grad.astype(BF16), up[c][...], NT)
    res_grad = norm_backward(first_grad, first_normed, first_spread, vec(g1))
    res_out[...] = res_grad
    upstream = dot(res_grad.astype(BF16), wo[...], NT).astype(BF16)
    log_sums = jnp.log(sums)
    lse = jnp.zeros((rows, LANES), F32)
    product = upstream.astype(F32) * attended
    delta = jnp.zeros((rows, LANES), F32)
    for p in range(pairs):
        block = product[:, lanes_of(p)]
        for e in range(2):
            keep = low_half if e == 0 else jnp.logical_not(low_half)
            part = jnp.sum(jnp.where(keep, block, 0.0), axis=1, keepdims=True)
            delta = jnp.where(lane == p + 8 * e, part, delta)
            at = p * LANES + e * HEAD_DIM
            head_lse = m_in[p, e * rows : (e + 1) * rows, :] + log_sums[:, at : at + 1]
            lse = jnp.where(lane == p + 8 * e, head_lse, lse)

    def pieces(values, count):
        got = []
        for _ in range(count):
            low = values.astype(BF16).astype(F32)
            got.append(low)
            values = values - low
        return got

    aux = jnp.where(lane == LANES - 1, 1.0, 0.0)
    for i, piece in enumerate(pieces(lse, 3) + pieces(delta, 2)):
        moved = piece if i == 0 else pltpu.roll(piece, 16 * i, 1)
        aux = jnp.where((lane >= 16 * i) & (lane < 16 * i + 16), moved, aux)
    payload = jnp.concatenate([upstream, aux.astype(BF16)], axis=1)
    half = rows // 2
    for i, out in enumerate(pay_outs):
        out[...] = payload[i * half : (i + 1) * half, :]


def aux_masks(rows, p):
    lane = lane_iota(2 * rows)
    side = jnp.where(lax.broadcasted_iota(jnp.int32, (2 * rows, LANES), 0) < rows, 0, 8)
    own = lax.rem(lane, 16) == p + side
    return own & (lane < 48), own & (lane >= 48) & (lane < 80), lane == LANES - 1


def query_grad_kernel(n_blocks, far, slot_count, chosen, *refs):
    task, queries, pay_a, pay_b, base, wq, prefix_k, prefix_v = refs[:8]
    all_keys = refs[8 : 8 + n_blocks]
    all_values = refs[8 + n_blocks : 8 + 2 * n_blocks]
    out, grad_ref, wq_cols, wq_sem, *own = refs[8 + 2 * n_blocks :]
    rows, width = queries.shape
    span = pl.ds(chosen[0] * LANES, len(chosen) * LANES)
    coming = start_copies([(wq.at[:, span], wq_cols)], wq_sem)
    arriving = []
    if far:
        keys, values, sems = own
        for b in range(n_blocks):
            moves = [
                (all_keys[b].at[:, span], keys.at[b]),
                (all_values[b].at[:, span], values.at[b]),
            ]
            arriving.append(start_copies(moves, sems, 2 * b))
    slots = prefix_k.shape[0]
    low_half = lane_iota(rows) < HEAD_DIM
    aux = [pay[:, width : width + LANES] for pay in (pay_a, pay_b)]
    aux2 = jnp.concatenate(aux + aux, axis=0)
    zero = jnp.zeros_like(aux2)

    def minus_ones(count):
        return jnp.where(lane_iota(count) < 80, -1.0, 0.0)

    slot = lax.broadcasted_iota(jnp.int32, (slots, LANES), 0)
    left_out = (lane_iota(slots) == LANES - 1) & (slot >= kept_slots(task, slot_count))
    prefix_tail = jnp.where(left_out, masked_score, minus_ones(slots)).astype(BF16)
    tail = minus_ones(rows).astype(BF16)
    for n, p in enumerate(chosen):
        cols, here = lanes_of(p), lanes_of(n)
        for_scores, for_delta, for_bias = aux_masks(rows, p)
        q_wide = jnp.concatenate(
            [
                stack_pair(queries[:, cols], low_half),
                jnp.where(for_scores | for_bias, aux2, zero),
            ],
            axis=1,
        )
        d_wide = jnp.concatenate(
            [
                stack_pair(jnp.concatenate([pay_a[:, cols], pay_b[:, cols]], axis=0), low_half),
                jnp.where(for_delta, aux2, zero),
            ],
            axis=1,
        )
        total = None
        for b in range(-1, n_blocks):
            if b < 0:
                key, value, ends = prefix_k[:, cols], prefix_v[:, cols], prefix_tail
            elif far:
                if n == 0:
                    for copy in arriving[b]:
                        copy.wait()
                key, value, ends = keys[b, :, here], values[b, :, here], tail
            else:
                key, value, ends = all_keys[b][:, cols], all_values[b][:, cols], tail
            probs = jnp.exp(dot(q_wide, jnp.concatenate([key, ends], axis=1), NT))
            products = dot(d_wide, jnp.concatenate([value, ends], axis=1), NT)
            term = dot((probs * products).astype(BF16), key)
            total = term if total is None else total + term
        both = jnp.where(low_half, total[0:rows], total[rows : 2 * rows])
        grad_ref[:, here] = (both * 0.125).astype(BF16)
    coming[0].wait()
    out[...] = base[...] + dot(grad_ref[...], wq_cols[...], NT)


def tall(parts, cols):
    return jnp.concatenate([part[:, cols] for part in parts], axis=0)


def key_terms(key, value, left_out, q_block, d_block, aux, p, low_half):
    rows = key.shape[0]
    for_scores, for_delta, for_bias = aux_masks(rows, p)
    score_tail = jnp.where(for_scores, -1.0, 0.0)
    if left_out is not None:
        score_tail = jnp.where(for_bias & left_out, masked_score, score_tail)
    k_wide = jnp.concatenate([stack_pair(key, low_half), score_tail.astype(BF16)], axis=1)
    v_wide = jnp.concatenate(
        [stack_pair(value, low_half), jnp.where(for_delta, -1.0, 0.0).astype(BF16)], axis=1
    )
    probs = jnp.exp(dot(k_wide, jnp.concatenate([q_block, aux], axis=1), NT))
    products = dot(v_wide, jnp.concatenate([d_block, aux], axis=1), NT)
    value_total = dot(probs.astype(BF16), d_block)
    key_total = dot((probs * products).astype(BF16), q_block)
    return (
        jnp.where(low_half, key_total[0:rows], key_total[rows : 2 * rows]),
        jnp.where(low_half, value_total[0:rows], value_total[rows : 2 * rows]),
    )


def prefix_grad_kernel(pairs, slot_count, queries, pay_a, pay_b, prefix_k, prefix_v, task, out, sent):
    width = queries.shape[1]
    slots = prefix_k.shape[0]
    low_half = lane_iota(slots) < HEAD_DIM
    aux = tall((pay_a, pay_b), slice(width, width + LANES))
    slot = lax.rem(lax.broadcasted_iota(jnp.int32, (2 * slots, LANES), 0), slots)
    left_out = slot >= kept_slots(task, slot_count)
    for p in range(pairs):
        cols = lanes_of(p)
        key_term, value_term = key_terms(
            prefix_k[:, cols], prefix_v[:, cols], left_out,
            queries[:, cols], tall((pay_a, pay_b), cols), aux, p, low_half,
        )
        out[0:slots, cols] = key_term.astype(BF16)
        out[slots : 2 * slots, cols] = value_term.astype(BF16)
    sent[...] = out[part_of(out.shape[0], "seq", 2, 1), :]


def part_of(height, axis, parts, flip):
    at = lax.rem(lax.axis_index(axis), parts)
    other = jnp.int32(0)
    for bit in range(parts.bit_length() - 1):
        digit = lax.rem(at // (1 << bit), 2)
        other = other + (1 << bit) * (1 - digit if (flip >> bit) % 2 else digit)
    return pl.ds(pl.multiple_of(other * (height // parts), 16), height // parts)


def scatter_kernel(axis, parts, then, terms, *refs):
    got, out, sent = refs[: parts - 1], refs[parts - 1], refs[parts:]
    total = terms[part_of(terms.shape[0], axis, parts, 0), :].astype(F32)
    for ref in got:
        total = total + ref[...].astype(F32)
    out[...] = total.astype(BF16)
    for i, ref in enumerate(sent):
        ref[...] = out[part_of(out.shape[0], then, len(sent) + 1, i + 1), :]


def add_kernel(terms, *refs):
    total = terms[...].astype(F32)
    for ref in refs[:-1]:
        total = total + ref[...].astype(F32)
    refs[-1][...] = total.astype(BF16)


def join_kernel(axis, parts, terms, *refs):
    out = refs[-1]
    for flip, ref in enumerate((terms,) + refs[:-1]):
        out[part_of(out.shape[0], axis, parts, flip), :] = ref[...]


def join_last_kernel(slot_count, terms, got, key_out, value_out):
    lower = lax.rem(lax.axis_index("seq"), 2) == 0
    for out, mine in ((key_out, lower), (value_out, jnp.logical_not(lower))):
        rows = jnp.where(mine, terms[...].astype(F32), got[...].astype(F32))
        out[...] = rows[0:slot_count, :]


def key_grad_kernel(pairs, count, first, last, *refs):
    refs = list(refs)

    def take(count):
        got = refs[:count]
        del refs[:count]
        return got

    keys, values, queries = take(3)
    pay_refs = take(count)
    if not first:
        key_in, value_in = take(2)
    if last:
        partial, wk_far, wv_far = take(3)
        (out,) = take(1)
        key_low, value_low, wk, wv, sems = take(5)
        coming = start_copies([(wk_far, wk), (wv_far, wv)], sems)
    else:
        key_out, value_out = take(2)
    rows, width = keys.shape
    low_half = lane_iota(rows) < HEAD_DIM
    aux = tall(pay_refs, slice(width, width + LANES))
    for p in range(pairs):
        cols = lanes_of(p)
        key_term, value_term = key_terms(
            keys[:, cols], values[:, cols], None,
            queries[:, cols], tall(pay_refs, cols), aux, p, low_half,
        )
        if not first:
            key_term = key_term + key_in[:, cols]
            value_term = value_term + value_in[:, cols]
        if last:
            key_low[:, cols] = key_term.astype(BF16)
            value_low[:, cols] = value_term.astype(BF16)
        else:
            key_out[:, cols] = key_term
            value_out[:, cols] = value_term
    if last:
        for copy in coming:
            copy.wait()
        out[...] = (
            partial[...] + dot(key_low[...], wk[...], NT) + dot(value_low[...], wv[...], NT)
        ).astype(BF16)


def after(value, *others):
    return lax.optimization_barrier((value, *others))[0]


def sum_steps(dp, seq, slots, width, slot_count):
    height = slots

    def rows_out(count):
        return Out((count, width), BF16)

    last = [Out((slot_count, width), F32, "auto")] * 2
    dp_flips, chip_flips = range(1, dp), [2 * i for i in range(1, seq // 2)]
    return [
        (
            ("seq", [1]),
            functools.partial(scatter_kernel, "seq", 2, "dp"),
            [rows_out(height)] + [rows_out(height // dp)] * (dp - 1),
        ),
        (("dp", dp_flips), functools.partial(scatter_kernel, "dp", dp, ""), [rows_out(height // dp)]),
        (("seq", chip_flips), add_kernel, [rows_out(height // dp)]),
        (("dp", dp_flips), functools.partial(join_kernel, "dp", dp), [rows_out(height)]),
        (("seq", [1]), functools.partial(join_last_kernel, slot_count), last),
    ]


def per_device(
    hidden_in,
    task_ids,
    prefix_keys,
    prefix_values,
    query_weight,
    query_bias,
    key_weight,
    key_bias,
    value_weight,
    value_bias,
    out_weight,
    out_bias,
    norm1_gain,
    norm1_bias,
    up_weight,
    up_bias,
    down_weight,
    down_bias,
    norm2_gain,
    norm2_bias,
    out_grad,
):
    rows, width = hidden_in.shape
    pairs = width // LANES
    ff = up_weight.shape[1]
    seq = lax.axis_size("seq")
    chips = seq // 2
    slot_count = prefix_keys.shape[0]
    slots = -(-slot_count // LANES) * LANES
    ring = [(2 * z + c, 2 * ((z + 1) % chips) + c) for z in range(chips) for c in range(2)]
    swap = [(i, i ^ 1) for i in range(seq)]

    half = rows // 2

    wide = (rows, width)

    def ring_hop(block):
        return lax.ppermute(block, "seq", ring)

    def swapped(block):
        return lax.ppermute(block, "seq", swap)

    def walk(halves, block, use, done, lag):
        others = [swapped(block)] if block is not None else [swapped(part) for part in halves]
        flying = [ring_hop(part) for part in halves]
        hops = 2 * chips - 2
        use(0, [block] if block is not None else halves)
        use(1, others)
        for step in range(hops):
            here = after(flying.pop(0), done[step + lag])
            if step < hops - 2:
                flying.append(ring_hop(here))
            use(step + 2, [here, swapped(here)])

    piece = ff // 4
    ahead = [(out_weight, (0, 0, width))]
    ahead += [(up_weight, (1, i * piece, piece)) for i in range(4)]
    ahead += [(down_weight, (0, i * piece, piece)) for i in range(4)]
    shares = [ahead[:0], ahead[0:2], ahead[2:4], ahead[4:6], ahead[6:8], ahead[8:9], [], []]

    state = [Out((pairs, 2 * rows, LANES), F32), Out(wide, F32), Out(wide, F32)]
    far = seq > 8
    q_list, k_list, v_list, attended, near_weights, fetched = [], [], [], [], [], []
    held = []

    def attend(step, parts):
        share = shares[step] if step < len(shares) else []
        rows_out = [Out(wide, BF16, "hbm" if far else "vmem")] * 3
        fetch_in = [Arg(w, "hbm") for w, _ in share]
        fetch_out = [
            Out((width, n) if axis else (n, width), BF16, "vmem") for _, (axis, _, n) in share
        ]
        scratch = [(wide, BF16)] * 3 if far else []
        scratch += [pltpu.SemaphoreType.DMA((9 + len(share),))]
        kernel = functools.partial(
            fwd_kernel, len(parts), step == 0, far, pairs, tuple(p for _, p in share)
        )
        if step == 0:
            got = call(
                kernel,
                rows_out
                + [Out((pairs, 2 * rows, LANES), BF16, "vmem")]
                + [Out((slots, width), BF16)] * 2
                + [Out((width, width), BF16, "vmem")] * 3
                + [Out((3, width), F32, "vmem")]
                + state
                + fetch_out,
                [Arg(part) for part in parts]
                + [Arg(w, "hbm") for w in (query_weight, key_weight, value_weight)]
                + [Arg(v) for v in (query_bias, key_bias, value_bias, prefix_keys, prefix_values)]
                + [Arg(task_ids, "smem")]
                + fetch_in,
                10 * rows * width * width, "attend_first", scratch,
            )
            held[:] = got[3:13]
            now = got[10:13]
        else:
            got = call(
                kernel,
                rows_out + state + fetch_out,
                [Arg(part, "auto") for part in parts]
                + [Arg(w, "vmem") for w in held[3:7] + held[0:1] + held[7:10]]
                + fetch_in,
                8 * rows * width * width, "attend_%d" % len(parts), scratch,
            )
            now = got[3:6]
            held[7:10] = now
        if share:
            fetched.extend(got[-len(share) :])
        q_list.append(got[0])
        k_list.append(got[1])
        v_list.append(got[2])
        attended.append(now[2])

    walk([hidden_in[0:half], hidden_in[half:rows]], hidden_in, attend, attended, 0)
    prefix_k, prefix_v, state_now = held[1], held[2], held[7:10]
    q0, k0, v0 = q_list[0], k_list[0], v_list[0]
    layer_out, res_grad, *payload = call(
        functools.partial(middle_kernel, pairs, 4),
        [Out(wide, BF16, "auto"), Out(wide, F32)] + [Out((half, width + LANES), BF16)] * 2,
        [Arg(hidden_in)]
        + [Arg(a, "vmem") for a in state_now]
        + [Arg(a) for a in (out_grad, out_bias, norm1_gain, norm1_bias)]
        + [Arg(a) for a in (up_bias, down_bias, norm2_gain, norm2_bias)]
        + [Arg(a, "vmem") for a in fetched],
        8 * rows * width * ff, "middle", [((rows, ff), BF16)], spare=12 * 1024 * 1024,
    )
    near_rows = "copy" if far else "vmem"
    own = [Arg(q0, near_rows)] + [Arg(a, "vmem") for a in payload]
    prefix = [Arg(prefix_k, "vmem"), Arg(prefix_v, "vmem")]
    terms, sent = call(
        functools.partial(prefix_grad_kernel, pairs, slot_count),
        [Out((2 * slots, width), BF16), Out((slots, width), BF16)],
        own + prefix + [Arg(task_ids, "smem")],
        8 * rows * slots * width, "prefix_grads",
    )
    sums = sum_steps(lax.axis_size("dp"), seq, slots, width, slot_count)
    trading = [terms, sent]
    done = [terms]

    def exchange(slot):
        if not sums or slot < times[0]:
            return None
        (axis, flips), job, outs = sums.pop(0)
        times.pop(0)
        kept, sent = trading[0], trading[1:] or trading[:1] * len(flips)
        args = [Arg(kept, "vmem")]
        for flip, block in zip(flips, sent):
            partners = [(i, i ^ flip) for i in range(lax.axis_size(axis))]
            args.append(Arg(after(lax.ppermute(block, axis, partners), done[-1]), "auto"))
        return job, outs, args

    times = [1, 3, 7, 9, 11]

    partial = res_grad
    each = 2
    for first_pair in range(0, pairs, each):
        chosen = tuple(range(first_pair, first_pair + each))
        side = exchange(first_pair // each)
        got = call(
            functools.partial(query_grad_kernel, seq, far, slot_count, chosen),
            [Out(wide, F32)],
            [Arg(task_ids, "smem"), Arg(after(q0, done[-1]), near_rows)] + own[1:]
            + [Arg(partial, "vmem"), Arg(query_weight, "hbm")]
            + prefix
            + [Arg(a, "hbm" if far else "vmem") for a in k_list + v_list],
            24 * rows * rows * seq * each * LANES, "query_grad_%d" % first_pair,
            [((rows, each * LANES), BF16), ((width, each * LANES), BF16), pltpu.SemaphoreType.DMA((1,))]
            + ([((seq, rows, each * LANES), BF16)] * 2 + [pltpu.SemaphoreType.DMA((2 * seq,))] if far else []),
            side,
        )
        if side is None:
            (partial,) = got
        else:
            (partial,) = got[0]
            trading[:] = got[1]
        done.append(partial)
    key_state = []

    def key_grads(step, parts):
        count, last = len(parts), step == seq - 1
        if step == 0:
            parts = [after(parts[0], partial)] + parts[1:]
        args = [Arg(a, near_rows) for a in (k0, v0, q_list[step])]
        args += [Arg(a, "auto" if step else "vmem") for a in parts]
        args += [Arg(a, "vmem") for a in key_state]
        if last:
            args += [Arg(partial, "vmem"), Arg(key_weight, "hbm"), Arg(value_weight, "hbm")]
        side = exchange(pairs // each + step)
        got = call(
            functools.partial(key_grad_kernel, pairs, count, step == 0, last),
            [Out(wide, BF16, "auto")] if last else [Out(wide, F32)] * 2,
            args,
            32 * rows * rows * width, "key_grad_%d%s" % (count, "_last" if last else ""),
            [(wide, BF16)] * 2 + [((width, width), BF16)] * 2 + [pltpu.SemaphoreType.DMA((2,))]
            if last
            else [],
            side,
        )
        if side is None:
            key_state[:] = got
        else:
            key_state[:] = got[0]
            trading[:] = got[1]
        done.append(key_state[0])

    walk(payload, None, key_grads, done, 2)
    (result,) = key_state
    return (layer_out, result, *trading)


def solution(mesh):
    rows = P(("dp", "seq"), None)
    return jax.shard_map(
        per_device,
        mesh=mesh,
        in_specs=(rows, P("dp")) + (P(),) * 18 + (rows,),
        out_specs=(rows, rows, P(), P()),
        check_vma=False,
    )
```

```python
import functools
from typing import Any, NamedTuple

import jax
import jax.numpy as jnp
from jax import lax
from jax.experimental import pallas as pl
from jax.experimental.pallas import tpu as pltpu
from jax.sharding import PartitionSpec as P

HEAD_DIM = 64
LANES = 128
F32 = jnp.float32
BF16 = jnp.bfloat16
eps_norm = 1e-05
masked_score = -1e30
root_half = 0.7071067811865476
inv_root_tau = 0.3989422804014327
MARGIN = 4 * 1024 * 1024
COST = 0.05
NT = (((1,), (1,)), ((), ()))
NN = (((1,), (0,)), ((), ()))


def dot(left, right, dims=NN):
    return lax.dot_general(left, right, dims, preferred_element_type=F32)


def lane_iota(rows):
    return lax.broadcasted_iota(jnp.int32, (rows, LANES), 1)


def stack_pair(block, low_half):
    zero = jnp.zeros_like(block)
    return jnp.concatenate(
        [jnp.where(low_half, block, zero), jnp.where(low_half, zero, block)], axis=0
    )


def lanes_of(p):
    return slice(p * LANES, (p + 1) * LANES)


def row_of(ref):
    return ref[...].astype(F32).reshape(1, -1)


def kept_slots(task_ref, slot_count):
    task = task_ref[0]
    return jnp.where(task == 0, 20, jnp.where(task == 1, 64, slot_count))


def start_copies(pairs_of_refs, sems, at=0):
    copies = [
        pltpu.make_async_copy(src, dst, sems.at[at + i]) for i, (src, dst) in enumerate(pairs_of_refs)
    ]
    for copy in copies:
        copy.start()
    return copies


def piece_of(ref, piece):
    axis, at, count = piece
    return ref.at[:, pl.ds(at, count)] if axis else ref.at[pl.ds(at, count), :]


def fwd_kernel(n_parts, first, far, pairs, pieces, ready, *refs):
    refs = list(refs)

    def take(count):
        got = refs[:count]
        del refs[:count]
        return got

    parts = take(n_parts)
    if first:
        weights_far, vectors, (prefix_keys, prefix_values, task) = take(3), take(3), take(3)
    else:
        weights, (biases,), (stacked_in, top_in, sum_in, acc_in) = take(3), take(1), take(4)
    ahead_far = take(len(pieces))
    rows_out = take(3)
    if first:
        stacked_out, prefix_k, prefix_v = take(3)
        weights, (biases,) = take(3), take(1)
    top_out, sum_out, acc_out = take(3)
    ahead = take(len(pieces))
    q_out, k_out, v_out = take(3) if far else rows_out
    (sems,) = take(1)
    rows = acc_out.shape[0]
    low_half = lane_iota(rows) < HEAD_DIM
    coming = [(piece_of(src, piece), dst) for src, piece, dst in zip(ahead_far, pieces, ahead)]
    coming = start_copies(coming, sems, 9)
    groups = 2 if first else 1
    span = acc_out.shape[1] // groups
    arriving = []
    if first:
        for n in range(groups):
            cols = pl.ds(n * span, span)
            moves = [(src.at[:, cols], dst.at[:, cols]) for src, dst in zip(weights_far, weights)]
            arriving.append(start_copies(moves, sems, 3 + 3 * n))
    ready()
    if first:
        for i, vector in enumerate(vectors):
            biases[i : i + 1, :] = row_of(vector)
        slot_count = prefix_keys.shape[0]
        prefix_k[...] = jnp.zeros_like(prefix_k)
        prefix_v[...] = jnp.zeros_like(prefix_v)
        prefix_k[0:slot_count, :] = prefix_keys[...]
        prefix_v[0:slot_count, :] = prefix_values[...]
        slot = lax.broadcasted_iota(jnp.int32, (1, prefix_k.shape[0]), 1)
        slot_bias = jnp.where(slot < kept_slots(task, slot_count), 0.0, masked_score)

    def project(cols, copies):
        for i, (weight, out) in enumerate(zip(weights, (q_out, k_out, v_out))):
            if copies:
                copies[i].wait()
            at = 0
            for part in parts:
                here = slice(at, at + part.shape[0])
                at += part.shape[0]
                block = (dot(part[...], weight[:, cols]) + biases[i : i + 1, cols]).astype(BF16)
                out[here, cols] = block * jnp.asarray(0.125, BF16) if i == 0 else block

    def attend(p):
        cols = lanes_of(p)
        sources = [(k_out[:, cols], v_out[:, cols], None)]
        if first:
            stacked = stack_pair(q_out[:, cols], low_half)
            stacked_out[p] = stacked
            sources.append((prefix_k[:, cols], prefix_v[:, cols], slot_bias))
        else:
            stacked = stacked_in[p]
        tiles = []
        for key, value, bias in sources:
            score = dot(stacked, key, NT)
            if bias is not None:
                score = score + bias
            tiles.append([score[:, i : i + LANES] for i in range(0, score.shape[1], LANES)])
        top = functools.reduce(jnp.maximum, sum(tiles, []))
        top = jnp.broadcast_to(jnp.max(top, axis=1, keepdims=True), top.shape)
        if not first:
            old = top_in[p]
            top = jnp.maximum(top, old)
        top_out[p] = top
        total = None
        for (key, value, bias), group in zip(sources, tiles):
            probs = jnp.concatenate([jnp.exp(tile - top).astype(BF16) for tile in group], axis=1)
            wide = jnp.concatenate([value, jnp.ones_like(value)], axis=1)
            term = dot(probs, wide)
            total = term if total is None else total + term
        acc = jnp.where(low_half, total[0:rows, 0:LANES], total[rows:, 0:LANES])
        sums = jnp.where(low_half, total[0:rows, LANES:], total[rows:, LANES:])
        if not first:
            alpha = jnp.exp(old - top)
            alpha = jnp.where(low_half, alpha[0:rows], alpha[rows:])
            sums = sums + sum_in[:, cols] * alpha
            acc = acc + acc_in[:, cols] * alpha
        sum_out[:, cols] = sums
        acc_out[:, cols] = acc

    leaving = []
    for n in range(groups):
        project(slice(n * span, (n + 1) * span), arriving[n] if first else None)
        if far and n == groups - 1:
            leaving = start_copies(zip((q_out, k_out, v_out), rows_out), sems)
        for p in range(n * pairs // groups, (n + 1) * pairs // groups):
            attend(p)
    for copy in leaving + coming:
        copy.wait()


def size_of(shape, kind):
    n = jnp.dtype(kind).itemsize
    for dim in shape:
        n *= dim
    return n


class Arg(NamedTuple):
    array: Any
    how: str = "copy"


class Out(NamedTuple):
    shape: tuple
    kind: Any
    how: str = "vmem"


def call(kernel, outs, args, flops, name, scratch=(), side=None, spare=MARGIN, lazy=False, alias=None):
    outs, args, scratch = list(outs), list(args), list(scratch)
    n_args, n_outs = len(args), len(outs)
    if side is not None:
        side_kernel, side_outs, side_args = side
        args += side_args
        outs += side_outs
    copied = [i for i, a in enumerate(args) if a.how == "copy"]
    held = sum(size_of(a.array.shape, a.array.dtype) for a in args if a.how in ("copy", "auto"))
    held += sum(size_of(o.shape, o.kind) for o in outs if o.how == "auto")
    held += sum(size_of(*o) for o in scratch if isinstance(o, tuple))
    spaces = {
        "vmem": pltpu.VMEM,
        "auto": pltpu.VMEM,
        "copy": pltpu.HBM,
        "hbm": pltpu.HBM,
        "smem": pltpu.SMEM,
    }

    def placed(arg):
        if arg.how in ("vmem", "hbm", "copy"):
            return pltpu.with_memory_space_constraint(arg.array, spaces[arg.how])
        return arg.array

    own = [(args[i].array.shape, args[i].array.dtype) for i in copied]
    if copied:
        own.append(pltpu.SemaphoreType.DMA((len(copied),)))

    def body(*refs):
        ins = list(refs[: len(args)])
        results = refs[len(args) : len(args) + len(outs)]
        extra = refs[len(args) + len(outs) :]
        if copied:
            sems = extra[len(copied)]
            copies = start_copies([(ins[i], extra[n]) for n, i in enumerate(copied)], sems)
            for n, i in enumerate(copied):
                ins[i] = extra[n]

        def ready():
            if copied:
                for copy in copies:
                    copy.wait()

        if side is not None:
            side_kernel(*ins[n_args:], *results[n_outs:])
        if lazy:
            kernel(ready, *ins[:n_args], *results[:n_outs], *extra[len(own) :])
        else:
            ready()
            kernel(*ins[:n_args], *results[:n_outs], *extra[len(own) :])

    n_bytes = sum(size_of(a.array.shape, a.array.dtype) for a in args if a.how != "vmem")
    got = pl.pallas_call(
        body,
        out_shape=[
            (pltpu.VMEM if o.how == "vmem" else pltpu.HBM)(o.shape, o.kind) for o in outs
        ],
        in_specs=[pl.BlockSpec(memory_space=spaces[a.how]) for a in args],
        out_specs=[pl.BlockSpec(memory_space=spaces[o.how]) for o in outs],
        scratch_shapes=[pltpu.VMEM(*o) if isinstance(o, tuple) else o for o in own + scratch],
        input_output_aliases=alias or {},
        compiler_params=pltpu.CompilerParams(vmem_limit_bytes=held + spare),
        cost_estimate=pl.CostEstimate(
            flops=int(flops * COST), bytes_accessed=int(n_bytes * COST), transcendentals=0
        ),
        name=name,
    )(*[placed(a) for a in args])
    return (got[:n_outs], got[n_outs:]) if side is not None else got


def norm_forward(values, gain, shift):
    center = values - jnp.mean(values, axis=-1, keepdims=True)
    inv_spread = lax.rsqrt(jnp.mean(center * center, axis=-1, keepdims=True) + eps_norm)
    normed = center * inv_spread
    return (normed * gain + shift, normed, inv_spread)


def norm_backward(upstream, normed, inv_spread, gain):
    scaled = upstream * gain
    return inv_spread * (
        scaled
        - jnp.mean(scaled, axis=-1, keepdims=True)
        - normed * jnp.mean(scaled * normed, axis=-1, keepdims=True)
    )


def middle_kernel(
    pairs, n_up, ready, hidden, m_in, l_in, acc_in, grad, bo, g1, s1, up_bias, down_bias, g2, s2,
    wo, *refs,
):
    up, down, layer_out, res_out, pay_out, slope_ref = refs
    rows, width = hidden.shape
    chunk = up.shape[1] // n_up
    low_half = lane_iota(rows) < HEAD_DIM
    lane = lane_iota(rows)
    vec = row_of
    sums = l_in[...]
    attended = acc_in[...] / sums
    branch = dot(attended.astype(BF16), wo[...])
    ready()
    residual = hidden[...].astype(F32) + branch + vec(bo)
    first_norm, first_normed, first_spread = norm_forward(residual, vec(g1), vec(s1))
    first_low = first_norm.astype(BF16)
    ffn = jnp.zeros((rows, width), F32)
    up_row = row_of(up_bias)
    for c in range(n_up):
        cols = slice(c * chunk, (c + 1) * chunk)
        pre = dot(first_low, up[:, cols]) + up_row[:, cols]
        phi = 0.5 * (1.0 + lax.erf(pre * root_half))
        slope_ref[:, cols] = (phi + pre * jnp.exp(-0.5 * pre * pre) * inv_root_tau).astype(BF16)
        ffn = ffn + dot((pre * phi).astype(BF16), down[cols, :])
    layer, second_normed, second_spread = norm_forward(
        first_norm + ffn + vec(down_bias), vec(g2), vec(s2)
    )
    layer_out[...] = layer.astype(BF16)
    sum_grad = norm_backward(grad[...].astype(F32), second_normed, second_spread, vec(g2))
    sum_low = sum_grad.astype(BF16)
    first_grad = sum_grad
    for c in range(n_up):
        cols = slice(c * chunk, (c + 1) * chunk)
        pre_grad = dot(sum_low, down[cols, :], NT) * slope_ref[:, cols]
        first_grad = first_grad + dot(pre_grad.astype(BF16), up[:, cols], NT)
    res_grad = norm_backward(first_grad, first_normed, first_spread, vec(g1))
    res_out[...] = res_grad
    upstream = dot(res_grad.astype(BF16), wo[...], NT).astype(BF16)
    log_sums = jnp.log(sums)
    lse = jnp.zeros((rows, LANES), F32)
    product = upstream.astype(F32) * attended
    delta = jnp.zeros((rows, LANES), F32)
    for p in range(pairs):
        block = product[:, lanes_of(p)]
        for e in range(2):
            keep = low_half if e == 0 else jnp.logical_not(low_half)
            part = jnp.sum(jnp.where(keep, block, 0.0), axis=1, keepdims=True)
            delta = jnp.where(lane == p + 8 * e, part, delta)
            at = p * LANES + e * HEAD_DIM
            head_lse = m_in[p, e * rows : (e + 1) * rows, :] + log_sums[:, at : at + 1]
            lse = jnp.where(lane == p + 8 * e, head_lse, lse)

    def pieces(values, count):
        got = []
        for _ in range(count):
            low = values.astype(BF16).astype(F32)
            got.append(low)
            values = values - low
        return got

    aux = jnp.where(lane == LANES - 1, 1.0, 0.0)
    for i, piece in enumerate(pieces(lse, 3) + pieces(delta, 2)):
        moved = piece if i == 0 else pltpu.roll(piece, 16 * i, 1)
        aux = jnp.where((lane >= 16 * i) & (lane < 16 * i + 16), moved, aux)
    payload = jnp.concatenate([upstream, aux.astype(BF16)], axis=1)
    pay_out[...] = payload


def aux_masks(rows, p):
    lane = lane_iota(2 * rows)
    side = jnp.where(lax.broadcasted_iota(jnp.int32, (2 * rows, LANES), 0) < rows, 0, 8)
    own = lax.rem(lane, 16) == p + side
    return own & (lane < 48), own & (lane >= 48) & (lane < 80), lane == LANES - 1


def query_grad_kernel(n_blocks, far, slot_count, chosen, *refs):
    task, queries, payload, base, wq, prefix_k, prefix_v = refs[:7]
    all_keys = refs[7 : 7 + n_blocks]
    all_values = refs[7 + n_blocks : 7 + 2 * n_blocks]
    out, grad_ref, *own = refs[7 + 2 * n_blocks :]
    rows, width = queries.shape
    span = pl.ds(chosen[0] * LANES, len(chosen) * LANES)
    arriving = []
    if far:
        keys, values, sems = own
        for b in range(n_blocks):
            moves = [
                (all_keys[b].at[:, span], keys.at[b]),
                (all_values[b].at[:, span], values.at[b]),
            ]
            arriving.append(start_copies(moves, sems, 2 * b))
    slots = prefix_k.shape[0]
    low_half = lane_iota(rows) < HEAD_DIM
    aux = payload[:, width : width + LANES]
    aux2 = jnp.concatenate([aux, aux], axis=0)
    zero = jnp.zeros_like(aux2)

    def minus_ones(count):
        return jnp.where(lane_iota(count) < 80, -1.0, 0.0)

    slot = lax.broadcasted_iota(jnp.int32, (slots, LANES), 0)
    left_out = (lane_iota(slots) == LANES - 1) & (slot >= kept_slots(task, slot_count))
    prefix_tail = jnp.where(left_out, masked_score, minus_ones(slots)).astype(BF16)
    tail = minus_ones(rows).astype(BF16)
    for n, p in enumerate(chosen):
        cols, here = lanes_of(p), lanes_of(n)
        for_scores, for_delta, for_bias = aux_masks(rows, p)
        q_wide = jnp.concatenate(
            [
                stack_pair(queries[:, cols], low_half),
                jnp.where(for_scores | for_bias, aux2, zero),
            ],
            axis=1,
        )
        d_wide = jnp.concatenate(
            [
                stack_pair(payload[:, cols], low_half),
                jnp.where(for_delta, aux2, zero),
            ],
            axis=1,
        )
        total = None
        for b in range(-1, n_blocks):
            if b < 0:
                key, value, ends = prefix_k[:, cols], prefix_v[:, cols], prefix_tail
            elif far:
                if n == 0:
                    for copy in arriving[b]:
                        copy.wait()
                key, value, ends = keys[b, :, here], values[b, :, here], tail
            else:
                key, value, ends = all_keys[b][:, cols], all_values[b][:, cols], tail
            probs = jnp.exp(dot(q_wide, jnp.concatenate([key, ends], axis=1), NT))
            products = dot(d_wide, jnp.concatenate([value, ends], axis=1), NT)
            term = dot((probs * products).astype(BF16), key)
            total = term if total is None else total + term
        both = jnp.where(low_half, total[0:rows], total[rows : 2 * rows])
        grad_ref[:, here] = (both * 0.125).astype(BF16)
    chosen_cols = slice(chosen[0] * LANES, (chosen[-1] + 1) * LANES)
    out[...] = base[...] + dot(grad_ref[...], wq[:, chosen_cols], NT)


def tall(parts, cols):
    return jnp.concatenate([part[:, cols] for part in parts], axis=0)


def key_terms(key, value, left_out, q_block, d_block, aux, p, low_half):
    rows = key.shape[0]
    for_scores, for_delta, for_bias = aux_masks(rows, p)
    score_tail = jnp.where(for_scores, -1.0, 0.0)
    if left_out is not None:
        score_tail = jnp.where(for_bias & left_out, masked_score, score_tail)
    k_wide = jnp.concatenate([stack_pair(key, low_half), score_tail.astype(BF16)], axis=1)
    v_wide = jnp.concatenate(
        [stack_pair(value, low_half), jnp.where(for_delta, -1.0, 0.0).astype(BF16)], axis=1
    )
    probs = jnp.exp(dot(k_wide, jnp.concatenate([q_block, aux], axis=1), NT))
    products = dot(v_wide, jnp.concatenate([d_block, aux], axis=1), NT)
    value_total = dot(probs.astype(BF16), d_block)
    key_total = dot((probs * products).astype(BF16), q_block)
    return (
        jnp.where(low_half, key_total[0:rows], key_total[rows : 2 * rows]),
        jnp.where(low_half, value_total[0:rows], value_total[rows : 2 * rows]),
    )


def prefix_grad_kernel(pairs, slot_count, queries, payload, prefix_k, prefix_v, task, out, sent):
    width = queries.shape[1]
    slots = prefix_k.shape[0]
    low_half = lane_iota(slots) < HEAD_DIM
    aux = payload[:, width : width + LANES]
    slot = lax.rem(lax.broadcasted_iota(jnp.int32, (2 * slots, LANES), 0), slots)
    left_out = slot >= kept_slots(task, slot_count)
    for p in range(pairs):
        cols = lanes_of(p)
        key_term, value_term = key_terms(
            prefix_k[:, cols], prefix_v[:, cols], left_out,
            queries[:, cols], payload[:, cols], aux, p, low_half,
        )
        out[0:slots, cols] = key_term.astype(BF16)
        out[slots : 2 * slots, cols] = value_term.astype(BF16)
    sent[...] = out[part_of(out.shape[0], "seq", 2, 1), :]


def part_of(height, axis, parts, flip):
    at = lax.rem(lax.axis_index(axis), parts)
    other = jnp.int32(0)
    for bit in range(parts.bit_length() - 1):
        digit = lax.rem(at // (1 << bit), 2)
        other = other + (1 << bit) * (1 - digit if (flip >> bit) % 2 else digit)
    return pl.ds(pl.multiple_of(other * (height // parts), 16), height // parts)


def scatter_kernel(axis, parts, then, terms, *refs):
    got, out, sent = refs[: parts - 1], refs[parts - 1], refs[parts:]
    total = terms[part_of(terms.shape[0], axis, parts, 0), :].astype(F32)
    for ref in got:
        total = total + ref[...].astype(F32)
    out[...] = total.astype(out.dtype)
    for i, ref in enumerate(sent):
        ref[...] = out[part_of(out.shape[0], then, len(sent) + 1, i + 1), :]


def add_kernel(terms, *refs):
    total = terms[...].astype(F32)
    for ref in refs[:-1]:
        total = total + ref[...].astype(F32)
    refs[-1][...] = total.astype(BF16)


def join_kernel(axis, parts, terms, *refs):
    out = refs[-1]
    for flip, ref in enumerate((terms,) + refs[:-1]):
        out[part_of(out.shape[0], axis, parts, flip), :] = ref[...]


def join_last_kernel(slot_count, terms, got, key_out, value_out):
    lower = lax.rem(lax.axis_index("seq"), 2) == 0
    for out, mine in ((key_out, lower), (value_out, jnp.logical_not(lower))):
        rows = jnp.where(mine, terms[...].astype(F32), got[...].astype(F32))
        out[...] = rows[0:slot_count, :]


def key_grad_kernel(pairs, count, first, last, *refs):
    refs = list(refs)

    def take(count):
        got = refs[:count]
        del refs[:count]
        return got

    keys, values, queries = take(3)
    pay_refs = take(count)
    if not first:
        key_in, value_in = take(2)
    if last:
        partial, wk, wv = take(3)
        (out,) = take(1)
        key_low, value_low = take(2)
    else:
        key_out, value_out = take(2)
    rows, width = keys.shape
    low_half = lane_iota(rows) < HEAD_DIM
    aux = tall(pay_refs, slice(width, width + LANES))
    for p in range(pairs):
        cols = lanes_of(p)
        key_term, value_term = key_terms(
            keys[:, cols], values[:, cols], None,
            queries[:, cols], tall(pay_refs, cols), aux, p, low_half,
        )
        if not first:
            key_term = key_term + key_in[:, cols]
            value_term = value_term + value_in[:, cols]
        if last:
            key_low[:, cols] = key_term.astype(BF16)
            value_low[:, cols] = value_term.astype(BF16)
        else:
            key_out[:, cols] = key_term
            value_out[:, cols] = value_term
    if last:
        out[...] = (
            partial[...] + dot(key_low[...], wk[...], NT) + dot(value_low[...], wv[...], NT)
        ).astype(BF16)


def after(value, *others):
    return lax.optimization_barrier((value, *others))[0]


def sum_steps(dp, seq, slots, width, slot_count):
    def rows_out(count):
        return Out((count, width), BF16)

    dp_flips, part = range(1, dp), slots // dp
    last = [Out((slot_count, width), F32, "auto")] * 2
    return [
        (
            ("seq", [1]),
            functools.partial(scatter_kernel, "seq", 2, "dp"),
            [rows_out(slots)] + [rows_out(part)] * (dp - 1),
        ),
        (("dp", dp_flips), functools.partial(scatter_kernel, "dp", dp, ""), [rows_out(part)]),
        (("seq", range(2, seq, 2)), add_kernel, [rows_out(part)]),
        (("dp", dp_flips), functools.partial(join_kernel, "dp", dp), [rows_out(slots)]),
        (("seq", [1]), functools.partial(join_last_kernel, slot_count), last),
    ]


def per_device(
    hidden_in,
    task_ids,
    prefix_keys,
    prefix_values,
    query_weight,
    query_bias,
    key_weight,
    key_bias,
    value_weight,
    value_bias,
    out_weight,
    out_bias,
    norm1_gain,
    norm1_bias,
    up_weight,
    up_bias,
    down_weight,
    down_bias,
    norm2_gain,
    norm2_bias,
    out_grad,
):
    rows, width = hidden_in.shape
    pairs = width // LANES
    ff = up_weight.shape[1]
    seq = lax.axis_size("seq")
    chips = seq // 2
    slot_count = prefix_keys.shape[0]
    slots = -(-slot_count // LANES) * LANES
    loop = [*range(0, chips, 2), *range(1, chips, 2)[::-1]]
    ring = [
        (2 * loop[i] + c, 2 * loop[(i + 1) % chips] + c) for i in range(chips) for c in range(2)
    ]
    swap = [(i, i ^ 1) for i in range(seq)]

    half = rows // 2

    wide = (rows, width)

    def ring_hop(block):
        return lax.ppermute(block, "seq", ring)

    def swapped(block):
        return lax.ppermute(block, "seq", swap)

    def walk(block, use, done, between=(), ahead=lambda step: []):
        between = dict(between)

        def turn(step, part, *others):
            use(step, [after(part, *done[-1:], *others)])
            between.get(step, lambda: None)()

        flying = ring_hop(block)
        other = swapped(block)
        between.get(-1, lambda: None)()
        turn(0, block)
        turn(1, other)
        for step in range(2, 2 * chips, 2):
            here = after(flying, done[-1], *ahead(step))
            if step < 2 * chips - 2:
                flying = ring_hop(here)
            other = swapped(here)
            turn(step, here)
            turn(step + 1, other)

    piece = ff // 4
    up_pieces = [(up_weight, (1, i * piece, piece)) for i in range(4)]
    ahead = [(out_weight, (0, 0, width))] + up_pieces
    shares = []

    state = [Out((pairs, 2 * rows, LANES), F32), Out(wide, F32), Out(wide, F32)]
    far = seq > 8
    q_list, k_list, v_list, attended, held, fetched = [], [], [], [], [], []

    def attend(step, parts):
        rows_out = [Out(wide, BF16, "hbm" if far else "vmem")] * 3
        scratch = [(wide, BF16)] * 3 if far else []
        share = shares[step] if step < len(shares) else []
        scratch += [pltpu.SemaphoreType.DMA((9 + len(share),))]
        fetch_in = [Arg(w, "hbm") for w, _ in share]
        fetch_out = [Out((width, n) if axis else (n, width), BF16) for _, (axis, _, n) in share]
        kernel = functools.partial(
            fwd_kernel, len(parts), step == 0, far, pairs, tuple(p for _, p in share)
        )
        if step == 0:
            got = call(
                kernel,
                rows_out
                + [Out((pairs, 2 * rows, LANES), BF16, "vmem")]
                + [Out((slots, width), BF16)] * 2
                + [Out((width, width), BF16, "vmem")] * 3
                + [Out((3, width), F32, "vmem")]
                + state
                + fetch_out,
                [Arg(part) for part in parts]
                + [Arg(w, "hbm") for w in (query_weight, key_weight, value_weight)]
                + [Arg(v) for v in (query_bias, key_bias, value_bias, prefix_keys, prefix_values)]
                + [Arg(task_ids, "smem")]
                + fetch_in,
                10 * rows * width * width, "attend_first", scratch, lazy=True,
            )
            held[:] = got[3:13]
            now = got[10:13]
        else:
            got = call(
                kernel,
                rows_out + state + fetch_out,
                [Arg(part, "auto") for part in parts]
                + [Arg(w, "vmem") for w in held[3:7] + held[0:1] + held[7:10]]
                + fetch_in,
                8 * rows * width * width, "attend_%d" % len(parts), scratch, lazy=True,
            )
            now = got[3:6]
            held[7:10] = now
        if share:
            fetched.extend(got[-len(share) :])
        q_list.append(got[0])
        k_list.append(got[1])
        v_list.append(got[2])
        attended.append(got[1])

    walk(hidden_in, attend, attended)
    prefix_k, prefix_v, state_now = held[1], held[2], held[7:10]
    q0, k0, v0 = q_list[0], k_list[0], v_list[0]
    layer_out, res_grad, payload = call(
        functools.partial(middle_kernel, pairs, 4),
        [Out(wide, BF16, "auto"), Out(wide, F32), Out((rows, width + LANES), BF16)],
        [Arg(hidden_in)]
        + [Arg(a, "vmem") for a in state_now]
        + [Arg(a) for a in (out_grad, out_bias, norm1_gain, norm1_bias)]
        + [Arg(a) for a in (up_bias, down_bias, norm2_gain, norm2_bias)]
        + [Arg(a, "vmem") for a in (out_weight, up_weight, down_weight)],
        8 * rows * width * ff, "middle", [((rows, ff), BF16)], spare=12 * 1024 * 1024, lazy=True,
    )
    near_rows = "copy" if far else "vmem"
    own = [Arg(q0, near_rows), Arg(payload, "vmem")]
    prefix = [Arg(prefix_k, "vmem"), Arg(prefix_v, "vmem")]
    terms, sent = call(
        functools.partial(prefix_grad_kernel, pairs, slot_count),
        [Out((2 * slots, width), BF16), Out((slots, width), BF16)],
        own + prefix + [Arg(task_ids, "smem")],
        8 * rows * slots * width, "prefix_grads",
    )
    sums = sum_steps(lax.axis_size("dp"), seq, slots, width, slot_count)
    trading = [terms, sent]
    done = [terms]

    def trade():
        if sums:
            (axis, flips), _, _ = sums[0]
            kept, sent = trading[0], trading[1:] or trading[:1] * len(flips)
            partners = [[(i, i ^ f) for i in range(lax.axis_size(axis))] for f in flips]
            pending[:] = [lax.ppermute(b, axis, p) for b, p in zip(sent, partners)]

    def exchange(slot):
        if not sums or times and slot < times[0]:
            return None
        _, job, outs = sums.pop(0)
        times[:1] = []
        got = [trading[0]] + [after(g, done[-1]) for g in pending]
        pending[:] = []
        return job, outs, [Arg(a, "auto") for a in got]

    pending = []
    trade()
    times = [2, 4, 9, 11, 13]

    def run(*args, **more):
        side = exchange(len(done))
        got = call(*args, side=side, **more)
        if side is not None:
            got, trading[:] = got
            trade()
        return got

    partial_now = [res_grad]
    each = 2

    def query_grads(first_pair):
        chosen = tuple(range(first_pair, first_pair + each))
        scratch = [((rows, each * LANES), BF16)]
        if far:
            scratch += [((seq, rows, each * LANES), BF16)] * 2 + [pltpu.SemaphoreType.DMA((2 * seq,))]
        partial_now[:] = run(
            functools.partial(query_grad_kernel, seq, far, slot_count, chosen),
            [Out(wide, F32)],
            [Arg(task_ids, "smem"), Arg(q0, near_rows), Arg(after(payload, done[-1]), "vmem")]
            + [Arg(partial_now[0], "vmem"), Arg(query_weight, "vmem")]
            + prefix
            + [Arg(a, "hbm" if far else "vmem") for a in k_list + v_list],
            24 * rows * rows * seq * each * LANES, "query_grad_%d" % first_pair, scratch,
        )
        done.append(partial_now[0])

    key_state = []

    def key_grads(step, parts):
        count, last = len(parts), step == seq - 1
        args = [Arg(a, near_rows) for a in (k0, v0, q_list[step])]
        args += [Arg(a, "auto" if step else "vmem") for a in parts]
        args += [Arg(a, "vmem") for a in key_state]
        if last:
            args += [Arg(a, "vmem") for a in (partial_now[0], key_weight, value_weight)]
        key_state[:] = run(
            functools.partial(key_grad_kernel, pairs, count, step == 0, last),
            [Out(wide, BF16, "auto")] if last else [Out(wide, F32)] * 2,
            args,
            32 * rows * rows * width, "key_grad_%d%s" % (count, "_last" if last else ""),
            [(wide, BF16)] * 2 if last else [],
        )
        done.append(key_state[0])

    def settle():
        job, outs, args = exchange(len(done))
        trading[:] = call(job, outs, args, 0, "settle")
        done.append(trading[0])
        trade()

    between = {
        1: lambda: (query_grads(0), settle()),
        2: lambda: query_grads(2),
        3: lambda: query_grads(4),
        5: lambda: query_grads(6),
    }
    walk(payload, key_grads, done, between, lambda step: pending if step == 4 else [])
    (result,) = key_state
    return (layer_out, result, *trading)


def solution(mesh):
    rows = P(("dp", "seq"), None)
    return jax.shard_map(
        per_device,
        mesh=mesh,
        in_specs=(rows, P("dp")) + (P(),) * 18 + (rows,),
        out_specs=(rows, rows, P(), P()),
        check_vma=False,
    )
```

```python
import functools
from typing import Any, NamedTuple

import jax
import jax.numpy as jnp
from jax import lax
from jax.experimental import pallas as pl
from jax.experimental.pallas import tpu as pltpu
from jax.sharding import PartitionSpec as P

HEAD_DIM = 64
LANES = 128
F32 = jnp.float32
BF16 = jnp.bfloat16
eps_norm = 1e-05
masked_score = -1e30
root_half = 0.7071067811865476
inv_root_tau = 0.3989422804014327
MARGIN = 4 * 1024 * 1024
COST = 0.05
NT = (((1,), (1,)), ((), ()))
NN = (((1,), (0,)), ((), ()))


def dot(left, right, dims=NN):
    return lax.dot_general(left, right, dims, preferred_element_type=F32)


def lane_iota(rows):
    return lax.broadcasted_iota(jnp.int32, (rows, LANES), 1)


def stack_pair(block, low_half):
    zero = jnp.zeros_like(block)
    return jnp.concatenate(
        [jnp.where(low_half, block, zero), jnp.where(low_half, zero, block)], axis=0
    )


def lanes_of(p):
    return slice(p * LANES, (p + 1) * LANES)


def row_of(ref):
    return ref[...].astype(F32).reshape(1, -1)


def start_copies(pairs_of_refs, sems, at=0):
    copies = [
        pltpu.make_async_copy(src, dst, sems.at[at + i]) for i, (src, dst) in enumerate(pairs_of_refs)
    ]
    for copy in copies:
        copy.start()
    return copies


def fwd_kernel(n_parts, first, far, pairs, unused, ready, *refs):
    refs = list(refs)

    def take(count):
        got = refs[:count]
        del refs[:count]
        return got

    parts = take(n_parts)
    if first:
        weights_far, vectors, (prefix_keys, prefix_values, task) = take(3), take(3), take(3)
    else:
        weights, (biases,), (stacked_in, top_in, sum_in, acc_in) = take(3), take(1), take(4)
    take(unused)
    rows_out = take(3)
    if first:
        stacked_out, prefix_k, prefix_v, left_out = take(4)
        weights, (biases,) = take(3), take(1)
    top_out, sum_out, acc_out = take(3)
    q_out, k_out, v_out = take(3) if far else rows_out
    (sems,) = take(1)
    rows = acc_out.shape[0]
    low_half = lane_iota(rows) < HEAD_DIM
    groups = 2 if first else 1
    span = acc_out.shape[1] // groups
    arriving = []
    if first:
        for n in range(groups):
            cols = pl.ds(n * span, span)
            moves = [(src.at[:, cols], dst.at[:, cols]) for src, dst in zip(weights_far, weights)]
            arriving.append(start_copies(moves, sems, 3 + 3 * n))
    ready()
    if first:
        for i, vector in enumerate(vectors):
            biases[i : i + 1, :] = row_of(vector)
        slot_count = prefix_keys.shape[0]
        prefix_k[...] = jnp.zeros_like(prefix_k)
        prefix_v[...] = jnp.zeros_like(prefix_v)
        prefix_k[0:slot_count, :] = prefix_keys[...]
        prefix_v[0:slot_count, :] = prefix_values[...]
        kept = jnp.where(task[0] == 0, 20, jnp.where(task[0] == 1, 64, slot_count))
        slot = lax.broadcasted_iota(jnp.int32, (1, prefix_k.shape[0]), 1)
        slot_bias = jnp.where(slot < kept, 0.0, masked_score)
        slot = lax.broadcasted_iota(jnp.int32, left_out.shape, 0)
        left_out[...] = jnp.where(slot < kept, 0.0, 1.0)

    def project(cols, copies):
        for i, (weight, out) in enumerate(zip(weights, (q_out, k_out, v_out))):
            if copies:
                copies[i].wait()
            at = 0
            for part in parts:
                here = slice(at, at + part.shape[0])
                at += part.shape[0]
                block = (dot(part[...], weight[:, cols]) + biases[i : i + 1, cols]).astype(BF16)
                out[here, cols] = block * jnp.asarray(0.125, BF16) if i == 0 else block

    def attend(p):
        cols = lanes_of(p)
        sources = [(k_out[:, cols], v_out[:, cols], None)]
        if first:
            stacked = stack_pair(q_out[:, cols], low_half)
            stacked_out[p] = stacked
            sources.append((prefix_k[:, cols], prefix_v[:, cols], slot_bias))
        else:
            stacked = stacked_in[p]
        tiles = []
        for key, value, bias in sources:
            score = dot(stacked, key, NT)
            if bias is not None:
                score = score + bias
            tiles.append([score[:, i : i + LANES] for i in range(0, score.shape[1], LANES)])
        top = functools.reduce(jnp.maximum, sum(tiles, []))
        top = jnp.broadcast_to(jnp.max(top, axis=1, keepdims=True), top.shape)
        if not first:
            old = top_in[p]
            top = jnp.maximum(top, old)
        top_out[p] = top
        total = None
        for (key, value, bias), group in zip(sources, tiles):
            probs = jnp.concatenate([jnp.exp(tile - top).astype(BF16) for tile in group], axis=1)
            wide = jnp.concatenate([value, jnp.ones_like(value)], axis=1)
            term = dot(probs, wide)
            total = term if total is None else total + term
        acc = jnp.where(low_half, total[0:rows, 0:LANES], total[rows:, 0:LANES])
        sums = jnp.where(low_half, total[0:rows, LANES:], total[rows:, LANES:])
        if not first:
            alpha = jnp.exp(old - top)
            alpha = jnp.where(low_half, alpha[0:rows], alpha[rows:])
            sums = sums + sum_in[:, cols] * alpha
            acc = acc + acc_in[:, cols] * alpha
        sum_out[:, cols] = sums
        acc_out[:, cols] = acc

    leaving = []
    for n in range(groups):
        project(slice(n * span, (n + 1) * span), arriving[n] if first else None)
        if far and n == groups - 1:
            leaving = start_copies(zip((q_out, k_out, v_out), rows_out), sems)
        for p in range(n * pairs // groups, (n + 1) * pairs // groups):
            attend(p)
    for copy in leaving:
        copy.wait()


def size_of(shape, kind):
    n = jnp.dtype(kind).itemsize
    for dim in shape:
        n *= dim
    return n


class Arg(NamedTuple):
    array: Any
    how: str = "copy"


class Out(NamedTuple):
    shape: tuple
    kind: Any
    how: str = "vmem"


def call(kernel, outs, args, flops, name, scratch=(), side=None, spare=MARGIN, lazy=False, alias=None):
    outs, args, scratch = list(outs), list(args), list(scratch)
    n_args, n_outs = len(args), len(outs)
    if side is not None:
        side_kernel, side_outs, side_args = side
        args += side_args
        outs += side_outs
    copied = [i for i, a in enumerate(args) if a.how == "copy"]
    held = sum(size_of(a.array.shape, a.array.dtype) for a in args if a.how in ("copy", "auto"))
    held += sum(size_of(o.shape, o.kind) for o in outs if o.how == "auto")
    held += sum(size_of(*o) for o in scratch if isinstance(o, tuple))
    spaces = {
        "vmem": pltpu.VMEM,
        "auto": pltpu.VMEM,
        "copy": pltpu.HBM,
        "hbm": pltpu.HBM,
        "smem": pltpu.SMEM,
    }

    def placed(arg):
        if arg.how in ("vmem", "hbm", "copy"):
            return pltpu.with_memory_space_constraint(arg.array, spaces[arg.how])
        return arg.array

    own = [(args[i].array.shape, args[i].array.dtype) for i in copied]
    if copied:
        own.append(pltpu.SemaphoreType.DMA((len(copied),)))

    def body(*refs):
        ins = list(refs[: len(args)])
        results = refs[len(args) : len(args) + len(outs)]
        extra = refs[len(args) + len(outs) :]
        if copied:
            sems = extra[len(copied)]
            copies = start_copies([(ins[i], extra[n]) for n, i in enumerate(copied)], sems)
            for n, i in enumerate(copied):
                ins[i] = extra[n]

        def ready():
            if copied:
                for copy in copies:
                    copy.wait()

        if side is not None:
            side_kernel(*ins[n_args:], *results[n_outs:])
        if lazy:
            kernel(ready, *ins[:n_args], *results[:n_outs], *extra[len(own) :])
        else:
            ready()
            kernel(*ins[:n_args], *results[:n_outs], *extra[len(own) :])

    n_bytes = sum(size_of(a.array.shape, a.array.dtype) for a in args if a.how != "vmem")
    got = pl.pallas_call(
        body,
        out_shape=[
            (pltpu.VMEM if o.how == "vmem" else pltpu.HBM)(o.shape, o.kind) for o in outs
        ],
        in_specs=[pl.BlockSpec(memory_space=spaces[a.how]) for a in args],
        out_specs=[pl.BlockSpec(memory_space=spaces[o.how]) for o in outs],
        scratch_shapes=[pltpu.VMEM(*o) if isinstance(o, tuple) else o for o in own + scratch],
        input_output_aliases=alias or {},
        compiler_params=pltpu.CompilerParams(vmem_limit_bytes=held + spare),
        cost_estimate=pl.CostEstimate(
            flops=int(flops * COST), bytes_accessed=int(n_bytes * COST), transcendentals=0
        ),
        name=name,
    )(*[placed(a) for a in args])
    return (got[:n_outs], got[n_outs:]) if side is not None else got


def norm_forward(values, gain, shift):
    center = values - jnp.mean(values, axis=-1, keepdims=True)
    inv_spread = lax.rsqrt(jnp.mean(center * center, axis=-1, keepdims=True) + eps_norm)
    normed = center * inv_spread
    return (normed * gain + shift, normed, inv_spread)


def norm_backward(upstream, normed, inv_spread, gain):
    scaled = upstream * gain
    return inv_spread * (
        scaled
        - jnp.mean(scaled, axis=-1, keepdims=True)
        - normed * jnp.mean(scaled * normed, axis=-1, keepdims=True)
    )


def middle_kernel(
    pairs, n_up, ready, hidden, m_in, l_in, acc_in, grad, bo, g1, s1, up_bias, down_bias, g2, s2,
    wo, *refs,
):
    up, down, layer_out, res_out, pay_out, slope_ref = refs
    rows, width = hidden.shape
    chunk = up.shape[1] // n_up
    low_half = lane_iota(rows) < HEAD_DIM
    lane = lane_iota(rows)
    vec = row_of
    sums = l_in[...]
    attended = acc_in[...] / sums
    branch = dot(attended.astype(BF16), wo[...])
    ready()
    residual = hidden[...].astype(F32) + branch + vec(bo)
    first_norm, first_normed, first_spread = norm_forward(residual, vec(g1), vec(s1))
    first_low = first_norm.astype(BF16)
    ffn = jnp.zeros((rows, width), F32)
    up_row = row_of(up_bias)
    for c in range(n_up):
        cols = slice(c * chunk, (c + 1) * chunk)
        pre = dot(first_low, up[:, cols]) + up_row[:, cols]
        phi = 0.5 * (1.0 + lax.erf(pre * root_half))
        slope_ref[:, cols] = (phi + pre * jnp.exp(-0.5 * pre * pre) * inv_root_tau).astype(BF16)
        ffn = ffn + dot((pre * phi).astype(BF16), down[cols, :])
    layer, second_normed, second_spread = norm_forward(
        first_norm + ffn + vec(down_bias), vec(g2), vec(s2)
    )
    layer_out[...] = layer.astype(BF16)
    sum_grad = norm_backward(grad[...].astype(F32), second_normed, second_spread, vec(g2))
    sum_low = sum_grad.astype(BF16)
    first_grad = sum_grad
    for c in range(n_up):
        cols = slice(c * chunk, (c + 1) * chunk)
        pre_grad = dot(sum_low, down[cols, :], NT) * slope_ref[:, cols]
        first_grad = first_grad + dot(pre_grad.astype(BF16), up[:, cols], NT)
    res_grad = norm_backward(first_grad, first_normed, first_spread, vec(g1))
    res_out[...] = res_grad
    upstream = dot(res_grad.astype(BF16), wo[...], NT).astype(BF16)
    log_sums = jnp.log(sums)
    lse = jnp.zeros((rows, LANES), F32)
    product = upstream.astype(F32) * attended
    delta = jnp.zeros((rows, LANES), F32)
    for p in range(pairs):
        block = product[:, lanes_of(p)]
        for e in range(2):
            keep = low_half if e == 0 else jnp.logical_not(low_half)
            part = jnp.sum(jnp.where(keep, block, 0.0), axis=1, keepdims=True)
            delta = jnp.where(lane == p + 8 * e, part, delta)
            at = p * LANES + e * HEAD_DIM
            head_lse = m_in[p, e * rows : (e + 1) * rows, :] + log_sums[:, at : at + 1]
            lse = jnp.where(lane == p + 8 * e, head_lse, lse)

    def pieces(values, count):
        got = []
        for _ in range(count):
            low = values.astype(BF16).astype(F32)
            got.append(low)
            values = values - low
        return got

    aux = jnp.where(lane == LANES - 1, 1.0, 0.0)
    for i, piece in enumerate(pieces(lse, 3) + pieces(delta, 2)):
        moved = piece if i == 0 else pltpu.roll(piece, 16 * i, 1)
        aux = jnp.where((lane >= 16 * i) & (lane < 16 * i + 16), moved, aux)
    payload = jnp.concatenate([upstream, aux.astype(BF16)], axis=1)
    pay_out[...] = payload


def aux_masks(rows, p):
    lane = lane_iota(2 * rows)
    side = jnp.where(lax.broadcasted_iota(jnp.int32, (2 * rows, LANES), 0) < rows, 0, 8)
    own = lax.rem(lane, 16) == p + side
    return own & (lane < 48), own & (lane >= 48) & (lane < 80), lane == LANES - 1


def query_grad_kernel(n_blocks, far, chosen, *refs):
    mask, queries, payload, base, wq, prefix_k, prefix_v = refs[:7]
    all_keys = refs[7 : 7 + n_blocks]
    all_values = refs[7 + n_blocks : 7 + 2 * n_blocks]
    out, grad_ref, *own = refs[7 + 2 * n_blocks :]
    rows, width = queries.shape
    span = pl.ds(chosen[0] * LANES, len(chosen) * LANES)
    arriving = []
    if far:
        keys, values, sems = own
        for b in range(n_blocks):
            moves = [
                (all_keys[b].at[:, span], keys.at[b]),
                (all_values[b].at[:, span], values.at[b]),
            ]
            arriving.append(start_copies(moves, sems, 2 * b))
    slots = prefix_k.shape[0]
    low_half = lane_iota(rows) < HEAD_DIM
    aux = payload[:, width : width + LANES]
    aux2 = jnp.concatenate([aux, aux], axis=0)
    zero = jnp.zeros_like(aux2)

    def minus_ones(count):
        return jnp.where(lane_iota(count) < 80, -1.0, 0.0)

    left_out = (lane_iota(slots) == LANES - 1) & (mask[...] > 0.5)
    prefix_tail = jnp.where(left_out, masked_score, minus_ones(slots)).astype(BF16)
    tail = minus_ones(rows).astype(BF16)
    for n, p in enumerate(chosen):
        cols, here = lanes_of(p), lanes_of(n)
        for_scores, for_delta, for_bias = aux_masks(rows, p)
        q_wide = jnp.concatenate(
            [
                stack_pair(queries[:, cols], low_half),
                jnp.where(for_scores | for_bias, aux2, zero),
            ],
            axis=1,
        )
        d_wide = jnp.concatenate(
            [
                stack_pair(payload[:, cols], low_half),
                jnp.where(for_delta, aux2, zero),
            ],
            axis=1,
        )
        total = None
        for b in range(-1, n_blocks):
            if b < 0:
                key, value, ends = prefix_k[:, cols], prefix_v[:, cols], prefix_tail
            elif far:
                if n == 0:
                    for copy in arriving[b]:
                        copy.wait()
                key, value, ends = keys[b, :, here], values[b, :, here], tail
            else:
                key, value, ends = all_keys[b][:, cols], all_values[b][:, cols], tail
            probs = jnp.exp(dot(q_wide, jnp.concatenate([key, ends], axis=1), NT))
            products = dot(d_wide, jnp.concatenate([value, ends], axis=1), NT)
            term = dot((probs * products).astype(BF16), key)
            total = term if total is None else total + term
        both = jnp.where(low_half, total[0:rows], total[rows : 2 * rows])
        grad_ref[:, here] = (both * 0.125).astype(BF16)
    chosen_cols = slice(chosen[0] * LANES, (chosen[-1] + 1) * LANES)
    out[...] = base[...] + dot(grad_ref[...], wq[:, chosen_cols], NT)


def tall(parts, cols):
    return jnp.concatenate([part[:, cols] for part in parts], axis=0)


def key_terms(key, value, left_out, q_block, d_block, aux, p, low_half):
    rows = key.shape[0]
    for_scores, for_delta, for_bias = aux_masks(rows, p)
    score_tail = jnp.where(for_scores, -1.0, 0.0)
    if left_out is not None:
        score_tail = jnp.where(for_bias & left_out, masked_score, score_tail)
    k_wide = jnp.concatenate([stack_pair(key, low_half), score_tail.astype(BF16)], axis=1)
    v_wide = jnp.concatenate(
        [stack_pair(value, low_half), jnp.where(for_delta, -1.0, 0.0).astype(BF16)], axis=1
    )
    probs = jnp.exp(dot(k_wide, jnp.concatenate([q_block, aux], axis=1), NT))
    products = dot(v_wide, jnp.concatenate([d_block, aux], axis=1), NT)
    value_total = dot(probs.astype(BF16), d_block)
    key_total = dot((probs * products).astype(BF16), q_block)
    return (
        jnp.where(low_half, key_total[0:rows], key_total[rows : 2 * rows]),
        jnp.where(low_half, value_total[0:rows], value_total[rows : 2 * rows]),
    )


def prefix_grad_kernel(pairs, queries, payload, prefix_k, prefix_v, mask, out, sent):
    width = queries.shape[1]
    slots = prefix_k.shape[0]
    low_half = lane_iota(slots) < HEAD_DIM
    aux = payload[:, width : width + LANES]
    left_out = jnp.concatenate([mask[...], mask[...]], axis=0) > 0.5
    for p in range(pairs):
        cols = lanes_of(p)
        key_term, value_term = key_terms(
            prefix_k[:, cols], prefix_v[:, cols], left_out,
            queries[:, cols], payload[:, cols], aux, p, low_half,
        )
        out[0:slots, cols] = key_term.astype(BF16)
        out[slots : 2 * slots, cols] = value_term.astype(BF16)
    sent[...] = out[part_of(out.shape[0], "seq", 2, 1), :]


def part_of(height, axis, parts, flip):
    at = lax.rem(lax.axis_index(axis), parts)
    other = jnp.int32(0)
    for bit in range(parts.bit_length() - 1):
        digit = lax.rem(at // (1 << bit), 2)
        other = other + (1 << bit) * (1 - digit if (flip >> bit) % 2 else digit)
    return pl.ds(pl.multiple_of(other * (height // parts), 16), height // parts)


def scatter_kernel(axis, parts, then, terms, *refs):
    got, out, sent = refs[: parts - 1], refs[parts - 1], refs[parts:]
    total = terms[part_of(terms.shape[0], axis, parts, 0), :].astype(F32)
    for ref in got:
        total = total + ref[...].astype(F32)
    out[...] = total.astype(out.dtype)
    for i, ref in enumerate(sent):
        ref[...] = out[part_of(out.shape[0], then, len(sent) + 1, i + 1), :]


def add_kernel(terms, *refs):
    total = terms[...].astype(F32)
    for ref in refs[:-1]:
        total = total + ref[...].astype(F32)
    refs[-1][...] = total.astype(BF16)


def join_kernel(axis, parts, terms, *refs):
    out = refs[-1]
    for flip, ref in enumerate((terms,) + refs[:-1]):
        out[part_of(out.shape[0], axis, parts, flip), :] = ref[...]


def join_last_kernel(slot_count, terms, got, key_out, value_out):
    lower = lax.rem(lax.axis_index("seq"), 2) == 0
    for out, mine in ((key_out, lower), (value_out, jnp.logical_not(lower))):
        rows = jnp.where(mine, terms[...].astype(F32), got[...].astype(F32))
        out[...] = rows[0:slot_count, :]


def key_grad_kernel(pairs, count, at, first, last, *refs):
    refs = list(refs)

    def take(count):
        got = refs[:count]
        del refs[:count]
        return got

    keys, values = take(2)
    q_refs = take(len(at))
    pay_refs = take(count)
    if not first:
        key_in, value_in = take(2)
    if last:
        partial, wk, wv = take(3)
        (out,) = take(1)
        key_low, value_low = take(2)
    else:
        key_out, value_out = take(2)
    rows, width = keys.shape
    low_half = lane_iota(rows) < HEAD_DIM
    aux = tall(pay_refs, slice(width, width + LANES))
    for p in range(pairs):
        cols = lanes_of(p)
        key_term, value_term = key_terms(
            keys[:, cols], values[:, cols], None,
            jnp.concatenate([q[here, cols] for q, here in zip(q_refs, at)], axis=0),
            tall(pay_refs, cols), aux, p, low_half,
        )
        if not first:
            key_term = key_term + key_in[:, cols]
            value_term = value_term + value_in[:, cols]
        if last:
            key_low[:, cols] = key_term.astype(BF16)
            value_low[:, cols] = value_term.astype(BF16)
        else:
            key_out[:, cols] = key_term
            value_out[:, cols] = value_term
    if last:
        out[...] = (
            partial[...] + dot(key_low[...], wk[...], NT) + dot(value_low[...], wv[...], NT)
        ).astype(BF16)


def after(value, *others):
    return lax.optimization_barrier((value, *others))[0]


def sum_steps(dp, seq, slots, width, slot_count):
    def rows_out(count):
        return Out((count, width), BF16)

    dp_flips, part = range(1, dp), slots // dp
    last = [Out((slot_count, width), F32, "auto")] * 2
    return [
        (
            ("seq", [1]),
            functools.partial(scatter_kernel, "seq", 2, "dp"),
            [rows_out(slots)] + [rows_out(part)] * (dp - 1),
        ),
        (("dp", dp_flips), functools.partial(scatter_kernel, "dp", dp, ""), [rows_out(part)]),
        (("seq", range(2, seq, 2)), add_kernel, [rows_out(part)]),
        (("dp", dp_flips), functools.partial(join_kernel, "dp", dp), [rows_out(slots)]),
        (("seq", [1]), functools.partial(join_last_kernel, slot_count), last),
    ]


def per_device(
    hidden_in,
    task_ids,
    prefix_keys,
    prefix_values,
    query_weight,
    query_bias,
    key_weight,
    key_bias,
    value_weight,
    value_bias,
    out_weight,
    out_bias,
    norm1_gain,
    norm1_bias,
    up_weight,
    up_bias,
    down_weight,
    down_bias,
    norm2_gain,
    norm2_bias,
    out_grad,
):
    rows, width = hidden_in.shape
    pairs = width // LANES
    ff = up_weight.shape[1]
    seq = lax.axis_size("seq")
    chips = seq // 2
    slot_count = prefix_keys.shape[0]
    slots = -(-slot_count // LANES) * LANES
    loop = [*range(0, chips, 2), *range(1, chips, 2)[::-1]]
    ring = [
        (2 * loop[i] + c, 2 * loop[(i + 1) % chips] + c) for i in range(chips) for c in range(2)
    ]
    swap = [(i, i ^ 1) for i in range(seq)]

    half = rows // 2

    wide = (rows, width)

    def ring_hop(block):
        return lax.ppermute(block, "seq", ring)

    def swapped(block):
        return lax.ppermute(block, "seq", swap)

    def walk(block, use, done, between=(), ahead=lambda step: []):
        between = dict(between)

        def turn(step, part, *others):
            use(step, [after(part, *done[-1:], *others)])
            between.get(step, lambda: None)()

        flying = ring_hop(block)
        other = swapped(block)
        between.get(-1, lambda: None)()
        turn(0, block)
        turn(1, other)
        for step in range(2, 2 * chips, 2):
            here = after(flying, done[-1], *ahead(step))
            if step < 2 * chips - 2:
                flying = ring_hop(here)
            other = swapped(here)
            turn(step, here)
            turn(step + 1, other)

    def walk_in_halves(block, use, done):
        flying = [ring_hop(block[0 : rows // 2]), ring_hop(block[rows // 2 : rows])]
        other = swapped(block)
        hops = 2 * chips - 2
        use(0, [block])
        parts = [other]
        for step in range(hops):
            here = after(flying.pop(0), done[-1])
            if step < hops - 2:
                flying.append(ring_hop(here))
            use(step + 1, [after(part, done[-1], here) for part in parts])
            parts = [here, swapped(here)]
        use(hops + 1, [after(part, done[-1]) for part in parts])

    state = [Out((pairs, 2 * rows, LANES), F32), Out(wide, F32), Out(wide, F32)]
    far = seq > 8
    q_list, k_list, v_list, attended, held, masks = [], [], [], [], [], []

    def attend(step, parts):
        rows_out = [Out(wide, BF16, "hbm" if far else "vmem")] * 3
        scratch = [(wide, BF16)] * 3 if far else []
        scratch += [pltpu.SemaphoreType.DMA((9,))]
        early = {2: [out_weight, up_weight], 4: [down_weight]}.get(step, [])
        kernel = functools.partial(fwd_kernel, len(parts), step == 0, far, pairs, len(early))
        if step == 0:
            got = call(
                kernel,
                rows_out
                + [Out((pairs, 2 * rows, LANES), BF16, "vmem")]
                + [Out((slots, width), BF16)] * 2
                + [Out((slots, LANES), F32)]
                + [Out((width, width), BF16, "vmem")] * 3
                + [Out((3, width), F32, "vmem")]
                + state,
                [Arg(part) for part in parts]
                + [Arg(w, "hbm") for w in (query_weight, key_weight, value_weight)]
                + [Arg(v) for v in (query_bias, key_bias, value_bias, prefix_keys, prefix_values)]
                + [Arg(task_ids, "smem")],
                10 * rows * width * width, "attend_first", scratch, lazy=True,
            )
            masks[:] = got[6:7]
            held[:] = got[3:6] + got[7:14]
            now = got[11:14]
        else:
            got = call(
                kernel,
                rows_out + state,
                [Arg(part, "auto") for part in parts]
                + [Arg(w, "vmem") for w in held[3:7] + held[0:1] + held[7:10] + early],
                8 * rows * width * width, "attend_%d" % len(parts), scratch, lazy=True,
            )
            now = got[3:6]
            held[7:10] = now
        q_list.append(got[0])
        k_list.append(got[1])
        v_list.append(got[2])
        attended.append(got[1])

    walk_in_halves(hidden_in, attend, attended)
    prefix_k, prefix_v, state_now = held[1], held[2], held[7:10]
    q0, k0, v0 = q_list[0], k_list[0], v_list[0]
    layer_out, res_grad, payload = call(
        functools.partial(middle_kernel, pairs, 4),
        [Out(wide, BF16, "auto"), Out(wide, F32), Out((rows, width + LANES), BF16)],
        [Arg(hidden_in)]
        + [Arg(a, "vmem") for a in state_now]
        + [Arg(a) for a in (out_grad, out_bias, norm1_gain, norm1_bias)]
        + [Arg(a) for a in (up_bias, down_bias, norm2_gain, norm2_bias)]
        + [Arg(a, "vmem") for a in (out_weight, up_weight, down_weight)],
        8 * rows * width * ff, "middle", [((rows, ff), BF16)], spare=12 * 1024 * 1024, lazy=True,
    )
    near_rows = "copy" if far else "vmem"
    own = [Arg(q0, near_rows), Arg(payload, "vmem")]
    prefix = [Arg(prefix_k, "vmem"), Arg(prefix_v, "vmem")]
    terms, sent = call(
        functools.partial(prefix_grad_kernel, pairs),
        [Out((2 * slots, width), BF16), Out((slots, width), BF16)],
        own + prefix + [Arg(masks[0], "vmem")],
        8 * rows * slots * width, "prefix_grads",
    )
    sums = sum_steps(lax.axis_size("dp"), seq, slots, width, slot_count)
    trading = [terms, sent]
    done = [terms]

    def trade():
        if sums:
            (axis, flips), _, _ = sums[0]
            kept, sent = trading[0], trading[1:] or trading[:1] * len(flips)
            partners = [[(i, i ^ f) for i in range(lax.axis_size(axis))] for f in flips]
            pending[:] = [lax.ppermute(b, axis, p) for b, p in zip(sent, partners)]

    def exchange(slot):
        if not sums or times and slot < times[0]:
            return None
        _, job, outs = sums.pop(0)
        times[:1] = []
        got = [trading[0]] + [after(g, done[-1]) for g in pending]
        pending[:] = []
        return job, outs, [Arg(a, "auto") for a in got]

    pending = []
    trade()
    times = [2, 4, 8, 10, 12]

    def run(*args, **more):
        side = exchange(len(done))
        got = call(*args, side=side, **more)
        if side is not None:
            got, trading[:] = got
            trade()
        return got

    partial_now = [res_grad]

    def query_grads(first_pair, each):
        chosen = tuple(range(first_pair, first_pair + each))
        scratch = [((rows, each * LANES), BF16)]
        if far:
            scratch += [((seq, rows, each * LANES), BF16)] * 2 + [pltpu.SemaphoreType.DMA((2 * seq,))]
        partial_now[:] = run(
            functools.partial(query_grad_kernel, seq, far, chosen),
            [Out(wide, F32)],
            [Arg(masks[0], "vmem"), Arg(q0, near_rows), Arg(after(payload, done[-1]), "vmem")]
            + [Arg(partial_now[0], "vmem"), Arg(query_weight, "vmem")]
            + prefix
            + [Arg(a, "hbm" if far else "vmem") for a in k_list + v_list],
            24 * rows * rows * seq * each * LANES, "query_grad_%d" % first_pair, scratch,
        )
        done.append(partial_now[0])

    key_state = []

    def key_grads(step, parts):
        count, last = len(parts), step == seq - 1
        if step < 2:
            q_blocks, at = q_list[step : step + 1], (slice(0, rows),)
        else:
            q_blocks = q_list[step - step % 2 :][:2]
            at = (slice(0, rows // 2) if step % 2 == 0 else slice(rows // 2, rows),) * 2
        args = [Arg(a, near_rows) for a in (k0, v0, *q_blocks)]
        args += [Arg(a, "auto" if step else "vmem") for a in parts]
        args += [Arg(a, "vmem") for a in key_state]
        if last:
            args += [Arg(a, "vmem") for a in (partial_now[0], key_weight, value_weight)]
        key_state[:] = run(
            functools.partial(key_grad_kernel, pairs, count, at, step == 0, last),
            [Out(wide, BF16, "auto")] if last else [Out(wide, F32)] * 2,
            args,
            32 * rows * rows * width, "key_grad_%d%s" % (count, "_last" if last else ""),
            [(wide, BF16)] * 2 if last else [],
        )
        done.append(key_state[0])

    def settle():
        job, outs, args = exchange(len(done))
        trading[:] = call(job, outs, args, 0, "settle")
        done.append(trading[0])
        trade()

    between = {
        1: lambda: (query_grads(0, 1), settle()),
        2: lambda: query_grads(1, 4),
        5: lambda: query_grads(5, 3),
    }
    walk(payload, key_grads, done, between, lambda step: pending if step == 4 else [])
    (result,) = key_state
    return (layer_out, result, *trading)


def solution(mesh):
    rows = P(("dp", "seq"), None)
    return jax.shard_map(
        per_device,
        mesh=mesh,
        in_specs=(rows, P("dp")) + (P(),) * 18 + (rows,),
        out_specs=(rows, rows, P(), P()),
        check_vma=False,
    )
```

```python
import functools
from typing import Any, NamedTuple

import jax
import jax.numpy as jnp
from jax import lax
from jax.experimental import pallas as pl
from jax.experimental.pallas import tpu as pltpu
from jax.sharding import PartitionSpec as P

HEAD_DIM = 64
LANES = 128
F32 = jnp.float32
BF16 = jnp.bfloat16
eps_norm = 1e-05
masked_score = -1e30
root_half = 0.7071067811865476
inv_root_tau = 0.3989422804014327
MARGIN = 4 * 1024 * 1024
COST = 0.05
NT = (((1,), (1,)), ((), ()))
NN = (((1,), (0,)), ((), ()))


def dot(left, right, dims=NN):
    return lax.dot_general(left, right, dims, preferred_element_type=F32)


def lane_iota(rows):
    return lax.broadcasted_iota(jnp.int32, (rows, LANES), 1)


def stack_pair(block, low_half):
    zero = jnp.zeros_like(block)
    return jnp.concatenate(
        [jnp.where(low_half, block, zero), jnp.where(low_half, zero, block)], axis=0
    )


def lanes_of(p):
    return slice(p * LANES, (p + 1) * LANES)


def row_of(ref):
    return ref[...].astype(F32).reshape(1, -1)


def start_copies(pairs_of_refs, sems, at=0):
    copies = [
        pltpu.make_async_copy(src, dst, sems.at[at + i]) for i, (src, dst) in enumerate(pairs_of_refs)
    ]
    for copy in copies:
        copy.start()
    return copies


def project_rows(parts, weights, biases, kinds, outs, cols=slice(None), arriving=()):
    for n, (i, weight, out) in enumerate(zip(kinds, weights, outs)):
        if arriving:
            arriving[n].wait()
        at = 0
        for part in parts:
            here = slice(at, at + part.shape[0])
            at += part.shape[0]
            block = (dot(part[...], weight[:, cols]) + biases[i : i + 1, cols]).astype(BF16)
            out[here, cols] = block * jnp.asarray(0.125, BF16) if i == 0 else block


def late_queries_kernel(n_parts, *refs):
    project_rows(refs[:n_parts], refs[n_parts : n_parts + 1], refs[n_parts + 1], (0,), refs[n_parts + 2 :])


def fwd_kernel(n_parts, first, far, kinds, pairs, unused, ready, *refs):
    refs = list(refs)

    def take(count):
        got = refs[:count]
        del refs[:count]
        return got

    parts = take(n_parts)
    if first:
        weights_far, vectors, (prefix_keys, prefix_values, task) = take(3), take(3), take(3)
    else:
        weights, (biases,) = take(len(kinds)), take(1)
        stacked_in, top_in, sum_in, acc_in = take(4)
    take(unused)
    rows_out = take(len(kinds))
    if first:
        stacked_out, prefix_k, prefix_v, left_out = take(4)
        weights, (biases,) = take(3), take(1)
    top_out, sum_out, acc_out = take(3)
    here_out = take(len(kinds)) if far else rows_out
    q_out, k_out, v_out = here_out if first else ([None] + list(here_out))[-3:]
    (sems,) = take(1)
    rows = acc_out.shape[0]
    low_half = lane_iota(rows) < HEAD_DIM
    groups = 1
    span = acc_out.shape[1] // groups
    arriving = []
    if first:
        for n in range(groups):
            cols = pl.ds(n * span, span)
            moves = [(src.at[:, cols], dst.at[:, cols]) for src, dst in zip(weights_far, weights)]
            arriving.append(start_copies(moves, sems, 3 + 3 * n))
    ready()
    if first:
        for i, vector in enumerate(vectors):
            biases[i : i + 1, :] = row_of(vector)
        slot_count = prefix_keys.shape[0]
        prefix_k[...] = jnp.zeros_like(prefix_k)
        prefix_v[...] = jnp.zeros_like(prefix_v)
        prefix_k[0:slot_count, :] = prefix_keys[...]
        prefix_v[0:slot_count, :] = prefix_values[...]
        kept = jnp.where(task[0] == 0, 20, jnp.where(task[0] == 1, 64, slot_count))
        slot = lax.broadcasted_iota(jnp.int32, (1, prefix_k.shape[0]), 1)
        slot_bias = jnp.where(slot < kept, 0.0, masked_score)
        slot = lax.broadcasted_iota(jnp.int32, left_out.shape, 0)
        left_out[...] = jnp.where(slot < kept, 0.0, 1.0)

    def attend(p):
        cols = lanes_of(p)
        sources = [(k_out[:, cols], v_out[:, cols], None)]
        if first:
            stacked = stack_pair(q_out[:, cols], low_half)
            stacked_out[p] = stacked
            sources.append((prefix_k[:, cols], prefix_v[:, cols], slot_bias))
        else:
            stacked = stacked_in[p]
        tiles = []
        for key, value, bias in sources:
            score = dot(stacked, key, NT)
            if bias is not None:
                score = score + bias
            tiles.append([score[:, i : i + LANES] for i in range(0, score.shape[1], LANES)])
        top = functools.reduce(jnp.maximum, sum(tiles, []))
        top = jnp.broadcast_to(jnp.max(top, axis=1, keepdims=True), top.shape)
        if not first:
            old = top_in[p]
            top = jnp.maximum(top, old)
        top_out[p] = top
        total = None
        for (key, value, bias), group in zip(sources, tiles):
            probs = jnp.concatenate([jnp.exp(tile - top).astype(BF16) for tile in group], axis=1)
            wide = jnp.concatenate([value, jnp.ones_like(value)], axis=1)
            term = dot(probs, wide)
            total = term if total is None else total + term
        acc = jnp.where(low_half, total[0:rows, 0:LANES], total[rows:, 0:LANES])
        sums = jnp.where(low_half, total[0:rows, LANES:], total[rows:, LANES:])
        if not first:
            alpha = jnp.exp(old - top)
            alpha = jnp.where(low_half, alpha[0:rows], alpha[rows:])
            sums = sums + sum_in[:, cols] * alpha
            acc = acc + acc_in[:, cols] * alpha
        sum_out[:, cols] = sums
        acc_out[:, cols] = acc

    leaving = []
    for n in range(groups):
        cols = slice(n * span, (n + 1) * span)
        project_rows(parts, weights, biases, kinds, here_out, cols, arriving[n] if first else ())
        if far and n == groups - 1:
            leaving = start_copies(zip(here_out, rows_out), sems)
        for p in range(n * pairs // groups, (n + 1) * pairs // groups):
            attend(p)
    for copy in leaving:
        copy.wait()


def size_of(shape, kind):
    n = jnp.dtype(kind).itemsize
    for dim in shape:
        n *= dim
    return n


class Arg(NamedTuple):
    array: Any
    how: str = "copy"


class Out(NamedTuple):
    shape: tuple
    kind: Any
    how: str = "vmem"


def call(kernel, outs, args, flops, name, scratch=(), side=None, spare=MARGIN, lazy=False, alias=None):
    outs, args, scratch = list(outs), list(args), list(scratch)
    n_args, n_outs = len(args), len(outs)
    if side is not None:
        side_kernel, side_outs, side_args = side
        args += side_args
        outs += side_outs
    copied = [i for i, a in enumerate(args) if a.how == "copy"]
    held = sum(size_of(a.array.shape, a.array.dtype) for a in args if a.how in ("copy", "auto"))
    held += sum(size_of(o.shape, o.kind) for o in outs if o.how == "auto")
    held += sum(size_of(*o) for o in scratch if isinstance(o, tuple))
    spaces = {
        "vmem": pltpu.VMEM,
        "auto": pltpu.VMEM,
        "copy": pltpu.HBM,
        "hbm": pltpu.HBM,
        "smem": pltpu.SMEM,
    }

    def placed(arg):
        if arg.how in ("vmem", "hbm", "copy"):
            return pltpu.with_memory_space_constraint(arg.array, spaces[arg.how])
        return arg.array

    own = [(args[i].array.shape, args[i].array.dtype) for i in copied]
    if copied:
        own.append(pltpu.SemaphoreType.DMA((len(copied),)))

    def body(*refs):
        ins = list(refs[: len(args)])
        results = refs[len(args) : len(args) + len(outs)]
        extra = refs[len(args) + len(outs) :]
        if copied:
            sems = extra[len(copied)]
            copies = start_copies([(ins[i], extra[n]) for n, i in enumerate(copied)], sems)
            for n, i in enumerate(copied):
                ins[i] = extra[n]

        def ready():
            if copied:
                for copy in copies:
                    copy.wait()

        if side is not None:
            side_kernel(*ins[n_args:], *results[n_outs:])
        if lazy:
            kernel(ready, *ins[:n_args], *results[:n_outs], *extra[len(own) :])
        else:
            ready()
            kernel(*ins[:n_args], *results[:n_outs], *extra[len(own) :])

    n_bytes = sum(size_of(a.array.shape, a.array.dtype) for a in args if a.how != "vmem")
    got = pl.pallas_call(
        body,
        out_shape=[
            (pltpu.VMEM if o.how == "vmem" else pltpu.HBM)(o.shape, o.kind) for o in outs
        ],
        in_specs=[pl.BlockSpec(memory_space=spaces[a.how]) for a in args],
        out_specs=[pl.BlockSpec(memory_space=spaces[o.how]) for o in outs],
        scratch_shapes=[pltpu.VMEM(*o) if isinstance(o, tuple) else o for o in own + scratch],
        input_output_aliases=alias or {},
        compiler_params=pltpu.CompilerParams(vmem_limit_bytes=held + spare),
        cost_estimate=pl.CostEstimate(
            flops=int(flops * COST), bytes_accessed=int(n_bytes * COST), transcendentals=0
        ),
        name=name,
    )(*[placed(a) for a in args])
    return (got[:n_outs], got[n_outs:]) if side is not None else got


def norm_forward(values, gain, shift):
    center = values - jnp.mean(values, axis=-1, keepdims=True)
    inv_spread = lax.rsqrt(jnp.mean(center * center, axis=-1, keepdims=True) + eps_norm)
    normed = center * inv_spread
    return (normed * gain + shift, normed, inv_spread)


def norm_backward(upstream, normed, inv_spread, gain):
    scaled = upstream * gain
    return inv_spread * (
        scaled
        - jnp.mean(scaled, axis=-1, keepdims=True)
        - normed * jnp.mean(scaled * normed, axis=-1, keepdims=True)
    )


def middle_kernel(
    pairs, n_up, ready, hidden, m_in, l_in, acc_in, grad, bo, g1, s1, up_bias, down_bias, g2, s2,
    wo, *refs,
):
    up, down, layer_out, res_out, pay_out, slope_ref = refs
    rows, width = hidden.shape
    chunk = up.shape[1] // n_up
    low_half = lane_iota(rows) < HEAD_DIM
    lane = lane_iota(rows)
    vec = row_of
    sums = l_in[...]
    attended = acc_in[...] / sums
    branch = dot(attended.astype(BF16), wo[...])
    ready()
    residual = hidden[...].astype(F32) + branch + vec(bo)
    first_norm, first_normed, first_spread = norm_forward(residual, vec(g1), vec(s1))
    first_low = first_norm.astype(BF16)
    ffn = jnp.zeros((rows, width), F32)
    up_row = row_of(up_bias)
    for c in range(n_up):
        cols = slice(c * chunk, (c + 1) * chunk)
        pre = dot(first_low, up[:, cols]) + up_row[:, cols]
        phi = 0.5 * (1.0 + lax.erf(pre * root_half))
        slope_ref[:, cols] = (phi + pre * jnp.exp(-0.5 * pre * pre) * inv_root_tau).astype(BF16)
        ffn = ffn + dot((pre * phi).astype(BF16), down[cols, :])
    layer, second_normed, second_spread = norm_forward(
        first_norm + ffn + vec(down_bias), vec(g2), vec(s2)
    )
    layer_out[...] = layer.astype(BF16)
    sum_grad = norm_backward(grad[...].astype(F32), second_normed, second_spread, vec(g2))
    sum_low = sum_grad.astype(BF16)
    first_grad = sum_grad
    for c in range(n_up):
        cols = slice(c * chunk, (c + 1) * chunk)
        pre_grad = dot(sum_low, down[cols, :], NT) * slope_ref[:, cols]
        first_grad = first_grad + dot(pre_grad.astype(BF16), up[:, cols], NT)
    res_grad = norm_backward(first_grad, first_normed, first_spread, vec(g1))
    res_out[...] = res_grad
    upstream = dot(res_grad.astype(BF16), wo[...], NT).astype(BF16)
    log_sums = jnp.log(sums)
    lse = jnp.zeros((rows, LANES), F32)
    product = upstream.astype(F32) * attended
    delta = jnp.zeros((rows, LANES), F32)
    for p in range(pairs):
        block = product[:, lanes_of(p)]
        for e in range(2):
            keep = low_half if e == 0 else jnp.logical_not(low_half)
            part = jnp.sum(jnp.where(keep, block, 0.0), axis=1, keepdims=True)
            delta = jnp.where(lane == p + 8 * e, part, delta)
            at = p * LANES + e * HEAD_DIM
            head_lse = m_in[p, e * rows : (e + 1) * rows, :] + log_sums[:, at : at + 1]
            lse = jnp.where(lane == p + 8 * e, head_lse, lse)

    def pieces(values, count):
        got = []
        for _ in range(count):
            low = values.astype(BF16).astype(F32)
            got.append(low)
            values = values - low
        return got

    aux = jnp.where(lane == LANES - 1, 1.0, 0.0)
    for i, piece in enumerate(pieces(lse, 3) + pieces(delta, 2)):
        moved = piece if i == 0 else pltpu.roll(piece, 16 * i, 1)
        aux = jnp.where((lane >= 16 * i) & (lane < 16 * i + 16), moved, aux)
    payload = jnp.concatenate([upstream, aux.astype(BF16)], axis=1)
    pay_out[...] = payload


def aux_masks(rows, p):
    lane = lane_iota(2 * rows)
    side = jnp.where(lax.broadcasted_iota(jnp.int32, (2 * rows, LANES), 0) < rows, 0, 8)
    own = lax.rem(lane, 16) == p + side
    return own & (lane < 48), own & (lane >= 48) & (lane < 80), lane == LANES - 1


def query_grad_kernel(n_blocks, far, chosen, *refs):
    mask, queries, payload, base, wq, prefix_k, prefix_v = refs[:7]
    all_keys = refs[7 : 7 + n_blocks]
    all_values = refs[7 + n_blocks : 7 + 2 * n_blocks]
    out, grad_ref, *own = refs[7 + 2 * n_blocks :]
    rows, width = queries.shape
    span = pl.ds(chosen[0] * LANES, len(chosen) * LANES)
    arriving = []
    if far:
        keys, values, sems = own
        for b in range(n_blocks):
            moves = [
                (all_keys[b].at[:, span], keys.at[b]),
                (all_values[b].at[:, span], values.at[b]),
            ]
            arriving.append(start_copies(moves, sems, 2 * b))
    slots = prefix_k.shape[0]
    low_half = lane_iota(rows) < HEAD_DIM
    aux = payload[:, width : width + LANES]
    aux2 = jnp.concatenate([aux, aux], axis=0)
    zero = jnp.zeros_like(aux2)

    def minus_ones(count):
        return jnp.where(lane_iota(count) < 80, -1.0, 0.0)

    left_out = (lane_iota(slots) == LANES - 1) & (mask[...] > 0.5)
    prefix_tail = jnp.where(left_out, masked_score, minus_ones(slots)).astype(BF16)
    tail = minus_ones(rows).astype(BF16)
    for n, p in enumerate(chosen):
        cols, here = lanes_of(p), lanes_of(n)
        for_scores, for_delta, for_bias = aux_masks(rows, p)
        q_wide = jnp.concatenate(
            [
                stack_pair(queries[:, cols], low_half),
                jnp.where(for_scores | for_bias, aux2, zero),
            ],
            axis=1,
        )
        d_wide = jnp.concatenate(
            [
                stack_pair(payload[:, cols], low_half),
                jnp.where(for_delta, aux2, zero),
            ],
            axis=1,
        )
        total = None
        for b in range(-1, n_blocks):
            if b < 0:
                key, value, ends = prefix_k[:, cols], prefix_v[:, cols], prefix_tail
            elif far:
                if n == 0:
                    for copy in arriving[b]:
                        copy.wait()
                key, value, ends = keys[b, :, here], values[b, :, here], tail
            else:
                key, value, ends = all_keys[b][:, cols], all_values[b][:, cols], tail
            probs = jnp.exp(dot(q_wide, jnp.concatenate([key, ends], axis=1), NT))
            products = dot(d_wide, jnp.concatenate([value, ends], axis=1), NT)
            term = dot((probs * products).astype(BF16), key)
            total = term if total is None else total + term
        both = jnp.where(low_half, total[0:rows], total[rows : 2 * rows])
        grad_ref[:, here] = (both * 0.125).astype(BF16)
    chosen_cols = slice(chosen[0] * LANES, (chosen[-1] + 1) * LANES)
    out[...] = base[...] + dot(grad_ref[...], wq[:, chosen_cols], NT)


def tall(parts, cols):
    return jnp.concatenate([part[:, cols] for part in parts], axis=0)


def key_terms(key, value, left_out, q_block, d_block, aux, p, low_half):
    rows = key.shape[0]
    for_scores, for_delta, for_bias = aux_masks(rows, p)
    score_tail = jnp.where(for_scores, -1.0, 0.0)
    if left_out is not None:
        score_tail = jnp.where(for_bias & left_out, masked_score, score_tail)
    k_wide = jnp.concatenate([stack_pair(key, low_half), score_tail.astype(BF16)], axis=1)
    v_wide = jnp.concatenate(
        [stack_pair(value, low_half), jnp.where(for_delta, -1.0, 0.0).astype(BF16)], axis=1
    )
    probs = jnp.exp(dot(k_wide, jnp.concatenate([q_block, aux], axis=1), NT))
    products = dot(v_wide, jnp.concatenate([d_block, aux], axis=1), NT)
    value_total = dot(probs.astype(BF16), d_block)
    key_total = dot((probs * products).astype(BF16), q_block)
    return (
        jnp.where(low_half, key_total[0:rows], key_total[rows : 2 * rows]),
        jnp.where(low_half, value_total[0:rows], value_total[rows : 2 * rows]),
    )


def prefix_grad_kernel(pairs, queries, payload, prefix_k, prefix_v, mask, out, sent):
    width = queries.shape[1]
    slots = prefix_k.shape[0]
    low_half = lane_iota(slots) < HEAD_DIM
    aux = payload[:, width : width + LANES]
    left_out = jnp.concatenate([mask[...], mask[...]], axis=0) > 0.5
    for p in range(pairs):
        cols = lanes_of(p)
        key_term, value_term = key_terms(
            prefix_k[:, cols], prefix_v[:, cols], left_out,
            queries[:, cols], payload[:, cols], aux, p, low_half,
        )
        out[0:slots, cols] = key_term.astype(BF16)
        out[slots : 2 * slots, cols] = value_term.astype(BF16)
    sent[...] = out[part_of(out.shape[0], "seq", 2, 1), :]


def part_of(height, axis, parts, flip):
    at = lax.rem(lax.axis_index(axis), parts)
    other = jnp.int32(0)
    for bit in range(parts.bit_length() - 1):
        digit = lax.rem(at // (1 << bit), 2)
        other = other + (1 << bit) * (1 - digit if (flip >> bit) % 2 else digit)
    return pl.ds(pl.multiple_of(other * (height // parts), 16), height // parts)


def scatter_kernel(axis, parts, then, terms, *refs):
    got, out, sent = refs[: parts - 1], refs[parts - 1], refs[parts:]
    total = terms[part_of(terms.shape[0], axis, parts, 0), :].astype(F32)
    for ref in got:
        total = total + ref[...].astype(F32)
    out[...] = total.astype(out.dtype)
    for i, ref in enumerate(sent):
        ref[...] = out[part_of(out.shape[0], then, len(sent) + 1, i + 1), :]


def add_kernel(terms, *refs):
    total = terms[...].astype(F32)
    for ref in refs[:-1]:
        total = total + ref[...].astype(F32)
    refs[-1][...] = total.astype(BF16)


def join_kernel(axis, parts, terms, *refs):
    out = refs[-1]
    for flip, ref in enumerate((terms,) + refs[:-1]):
        out[part_of(out.shape[0], axis, parts, flip), :] = ref[...]


def join_last_kernel(slot_count, terms, got, key_out, value_out):
    lower = lax.rem(lax.axis_index("seq"), 2) == 0
    for out, mine in ((key_out, lower), (value_out, jnp.logical_not(lower))):
        rows = jnp.where(mine, terms[...].astype(F32), got[...].astype(F32))
        out[...] = rows[0:slot_count, :]


def key_grad_kernel(pairs, count, at, first, last, *refs):
    refs = list(refs)

    def take(count):
        got = refs[:count]
        del refs[:count]
        return got

    keys, values = take(2)
    q_refs = take(len(at))
    pay_refs = take(count)
    if not first:
        key_in, value_in = take(2)
    if last:
        partial, wk, wv = take(3)
        (out,) = take(1)
        key_low, value_low = take(2)
    else:
        key_out, value_out = take(2)
    rows, width = keys.shape
    low_half = lane_iota(rows) < HEAD_DIM
    aux = tall(pay_refs, slice(width, width + LANES))
    for p in range(pairs):
        cols = lanes_of(p)
        key_term, value_term = key_terms(
            keys[:, cols], values[:, cols], None,
            jnp.concatenate([q[here, cols] for q, here in zip(q_refs, at)], axis=0),
            tall(pay_refs, cols), aux, p, low_half,
        )
        if not first:
            key_term = key_term + key_in[:, cols]
            value_term = value_term + value_in[:, cols]
        if last:
            key_low[:, cols] = key_term.astype(BF16)
            value_low[:, cols] = value_term.astype(BF16)
        else:
            key_out[:, cols] = key_term
            value_out[:, cols] = value_term
    if last:
        out[...] = (
            partial[...] + dot(key_low[...], wk[...], NT) + dot(value_low[...], wv[...], NT)
        ).astype(BF16)


def after(value, *others):
    return lax.optimization_barrier((value, *others))[0]


def sum_steps(dp, seq, slots, width, slot_count):
    def rows_out(count):
        return Out((count, width), BF16)

    dp_flips, part = range(1, dp), slots // dp
    last = [Out((slot_count, width), F32, "auto")] * 2
    return [
        (
            ("seq", [1]),
            functools.partial(scatter_kernel, "seq", 2, "dp"),
            [rows_out(slots)] + [rows_out(part)] * (dp - 1),
        ),
        (("dp", dp_flips), functools.partial(scatter_kernel, "dp", dp, ""), [rows_out(part)]),
        (("seq", range(2, seq, 2)), add_kernel, [rows_out(part)]),
        (("dp", dp_flips), functools.partial(join_kernel, "dp", dp), [rows_out(slots)]),
        (("seq", [1]), functools.partial(join_last_kernel, slot_count), last),
    ]


def per_device(
    hidden_in,
    task_ids,
    prefix_keys,
    prefix_values,
    query_weight,
    query_bias,
    key_weight,
    key_bias,
    value_weight,
    value_bias,
    out_weight,
    out_bias,
    norm1_gain,
    norm1_bias,
    up_weight,
    up_bias,
    down_weight,
    down_bias,
    norm2_gain,
    norm2_bias,
    out_grad,
):
    rows, width = hidden_in.shape
    pairs = width // LANES
    ff = up_weight.shape[1]
    seq = lax.axis_size("seq")
    chips = seq // 2
    slot_count = prefix_keys.shape[0]
    slots = -(-slot_count // LANES) * LANES
    loop = [*range(0, chips, 2), *range(1, chips, 2)[::-1]]
    ring = [
        (2 * loop[i] + c, 2 * loop[(i + 1) % chips] + c) for i in range(chips) for c in range(2)
    ]
    swap = [(i, i ^ 1) for i in range(seq)]

    half = rows // 2

    wide = (rows, width)

    def ring_hop(block):
        return lax.ppermute(block, "seq", ring)

    def swapped(block):
        return lax.ppermute(block, "seq", swap)

    def walk(block, use, done, between=(), ahead=lambda step: []):
        between = dict(between)

        def turn(step, part, *others):
            use(step, [after(part, *done[-1:], *others)])
            between.get(step, lambda: None)()

        flying = ring_hop(block)
        other = swapped(block)
        between.get(-1, lambda: None)()
        turn(0, block)
        turn(1, other)
        for step in range(2, 2 * chips, 2):
            here = after(flying, done[-1], *ahead(step))
            if step < 2 * chips - 2:
                flying = ring_hop(here)
            other = swapped(here)
            turn(step, here)
            turn(step + 1, other)

    def walk_in_halves(block, use, done):
        flying = [ring_hop(block[0 : rows // 2]), ring_hop(block[rows // 2 : rows])]
        other = swapped(block)
        hops = 2 * chips - 2
        use(0, [block])
        parts = [other]
        for step in range(hops):
            here = after(flying.pop(0), done[-1])
            if step < hops - 2:
                flying.append(ring_hop(here))
            use(step + 1, [after(part, done[-1], here) for part in parts])
            parts = [here, swapped(here)]
        use(hops + 1, [after(part, done[-1]) for part in parts])

    state = [Out((pairs, 2 * rows, LANES), F32), Out(wide, F32), Out(wide, F32)]
    far = seq > 8
    q_list, k_list, v_list, attended, held, masks, late_parts = [], [], [], [], [], [], []
    near_weights = []

    def attend(step, parts):
        late = step >= seq // 2
        kinds = (1, 2) if late else (0, 1, 2)
        weights = [near_weights[i] for i in kinds] if step else []
        rows_out = [Out(wide, BF16, "hbm" if far else "vmem")] * len(kinds)
        scratch = [(wide, BF16)] * len(kinds) if far else []
        scratch += [pltpu.SemaphoreType.DMA((9,))]
        early = {2: [out_weight, up_weight], 4: [down_weight]}.get(step, [])
        kernel = functools.partial(fwd_kernel, len(parts), step == 0, far, kinds, pairs, len(early))
        if step == 0:
            got = call(
                kernel,
                rows_out
                + [Out((pairs, 2 * rows, LANES), BF16, "vmem")]
                + [Out((slots, width), BF16)] * 2
                + [Out((slots, LANES), F32)]
                + [Out((width, width), BF16)] * 3
                + [Out((3, width), F32)]
                + state,
                [Arg(part) for part in parts]
                + [Arg(w, "hbm") for w in (query_weight, key_weight, value_weight)]
                + [Arg(v) for v in (query_bias, key_bias, value_bias, prefix_keys, prefix_values)]
                + [Arg(task_ids, "smem")],
                10 * rows * width * width, "attend_first", scratch, lazy=True,
            )
            masks[:] = got[6:7]
            near_weights[:] = got[7:10]
            held[:] = got[3:6] + got[10:14]
        else:
            got = call(
                kernel,
                rows_out + state,
                [Arg(part, "auto") for part in parts]
                + [Arg(w, "vmem") for w in weights + held[3:4] + held[0:1] + held[4:7] + early],
                8 * rows * width * width, "attend_%d" % len(parts), scratch, lazy=True,
            )
            held[4:7] = got[len(kinds) : len(kinds) + 3]
        if late:
            late_parts.append(parts)
        else:
            q_list.append(got[0])
        k_list.append(got[len(kinds) - 2])
        v_list.append(got[len(kinds) - 1])
        attended.append(k_list[-1])

    walk_in_halves(hidden_in, attend, attended)
    prefix_k, prefix_v, state_now = held[1], held[2], held[4:7]
    q0, k0, v0 = q_list[0], k_list[0], v_list[0]
    layer_out, res_grad, payload = call(
        functools.partial(middle_kernel, pairs, 4),
        [Out(wide, BF16, "auto"), Out(wide, F32), Out((rows, width + LANES), BF16)],
        [Arg(hidden_in)]
        + [Arg(a, "vmem") for a in state_now]
        + [Arg(a) for a in (out_grad, out_bias, norm1_gain, norm1_bias)]
        + [Arg(a) for a in (up_bias, down_bias, norm2_gain, norm2_bias)]
        + [Arg(a, "vmem") for a in (out_weight, up_weight, down_weight)],
        8 * rows * width * ff, "middle", [((rows, ff), BF16)], spare=12 * 1024 * 1024, lazy=True,
    )
    near_rows = "copy" if far else "vmem"
    own = [Arg(q0, near_rows), Arg(payload, "vmem")]
    prefix = [Arg(prefix_k, "vmem"), Arg(prefix_v, "vmem")]
    terms, sent = call(
        functools.partial(prefix_grad_kernel, pairs),
        [Out((2 * slots, width), BF16), Out((slots, width), BF16)],
        own + prefix + [Arg(masks[0], "vmem")],
        8 * rows * slots * width, "prefix_grads",
    )
    sums = sum_steps(lax.axis_size("dp"), seq, slots, width, slot_count)
    trading = [terms, sent]
    done = [terms]

    def trade():
        if sums:
            (axis, flips), _, _ = sums[0]
            kept, sent = trading[0], trading[1:] or trading[:1] * len(flips)
            partners = [[(i, i ^ f) for i in range(lax.axis_size(axis))] for f in flips]
            pending[:] = [lax.ppermute(b, axis, p) for b, p in zip(sent, partners)]

    def exchange(slot):
        if not sums or times and slot < times[0]:
            return None
        _, job, outs = sums.pop(0)
        times[:1] = []
        got = [trading[0]] + [after(g, done[-1]) for g in pending]
        pending[:] = []
        return job, outs, [Arg(a, "auto") for a in got]

    pending = []
    trade()
    times = [2, 4, 8 + seq // 2, 10 + seq // 2, 13 + seq // 2]

    def run(*args, **more):
        side = exchange(len(done))
        got = call(*args, side=side, **more)
        if side is not None:
            got, trading[:] = got
            trade()
        return got

    partial_now = [res_grad]

    def query_grads(first_pair, each):
        chosen = tuple(range(first_pair, first_pair + each))
        scratch = [((rows, each * LANES), BF16)]
        if far:
            scratch += [((seq, rows, each * LANES), BF16)] * 2 + [pltpu.SemaphoreType.DMA((2 * seq,))]
        partial_now[:] = run(
            functools.partial(query_grad_kernel, seq, far, chosen),
            [Out(wide, F32)],
            [Arg(masks[0], "vmem"), Arg(q0, near_rows), Arg(after(payload, done[-1]), "vmem")]
            + [Arg(partial_now[0], "vmem"), Arg(query_weight, "vmem")]
            + prefix
            + [Arg(a, "hbm" if far else "vmem") for a in k_list + v_list],
            24 * rows * rows * seq * each * LANES, "query_grad_%d" % first_pair, scratch,
        )
        done.append(partial_now[0])

    key_state = []

    def key_grads(step, parts):
        count, last = len(parts), step == seq - 1
        if step < 2:
            q_blocks, at = q_list[step : step + 1], (slice(0, rows),)
        else:
            q_blocks = q_list[step - step % 2 :][:2]
            at = (slice(0, rows // 2) if step % 2 == 0 else slice(rows // 2, rows),) * 2
        args = [Arg(a, near_rows) for a in (k0, v0, *q_blocks)]
        args += [Arg(a, "auto" if step else "vmem") for a in parts]
        args += [Arg(a, "vmem") for a in key_state]
        if last:
            args += [Arg(a, "vmem") for a in (partial_now[0], key_weight, value_weight)]
        key_state[:] = run(
            functools.partial(key_grad_kernel, pairs, count, at, step == 0, last),
            [Out(wide, BF16, "auto")] if last else [Out(wide, F32)] * 2,
            args,
            32 * rows * rows * width, "key_grad_%d%s" % (count, "_last" if last else ""),
            [(wide, BF16)] * 2 if last else [],
        )
        done.append(key_state[0])

    def settle():
        job, outs, args = exchange(len(done))
        trading[:] = call(job, outs, args, 0, "settle")
        done.append(trading[0])
        trade()

    def late_queries():
        for parts in late_parts:
            (block,) = call(
                functools.partial(late_queries_kernel, len(parts)),
                [Out(wide, BF16)],
                [Arg(after(part, done[-1]), "auto") for part in parts]
                + [Arg(query_weight, "vmem"), Arg(held[3], "vmem")],
                2 * rows * width * width, "late_queries",
            )
            q_list.append(block)
            done.append(block)

    between = {
        1: lambda: (query_grads(0, 1), settle()),
        2: lambda: query_grads(1, 4),
        3: late_queries,
        4: lambda: query_grads(5, 2),
        5: lambda: query_grads(7, 1),
    }
    walk(payload, key_grads, done, between, lambda step: pending if step == 4 else [])
    (result,) = key_state
    return (layer_out, result, *trading)


def solution(mesh):
    rows = P(("dp", "seq"), None)
    return jax.shard_map(
        per_device,
        mesh=mesh,
        in_specs=(rows, P("dp")) + (P(),) * 18 + (rows,),
        out_specs=(rows, rows, P(), P()),
        check_vma=False,
    )
```

```python
import functools
from typing import Any, NamedTuple

import jax
import jax.numpy as jnp
from jax import lax
from jax.experimental import pallas as pl
from jax.experimental.pallas import tpu as pltpu
from jax.sharding import PartitionSpec as P

HEAD_DIM = 64
LANES = 128
F32 = jnp.float32
BF16 = jnp.bfloat16
eps_norm = 1e-05
masked_score = -1e30
root_half = 0.7071067811865476
inv_root_tau = 0.3989422804014327
MARGIN = 4 * 1024 * 1024
COST = 0.05
NT = (((1,), (1,)), ((), ()))
NN = (((1,), (0,)), ((), ()))


def dot(left, right, dims=NN):
    return lax.dot_general(left, right, dims, preferred_element_type=F32)


def lane_iota(rows):
    return lax.broadcasted_iota(jnp.int32, (rows, LANES), 1)


def stack_pair(block, low_half):
    zero = jnp.zeros_like(block)
    return jnp.concatenate(
        [jnp.where(low_half, block, zero), jnp.where(low_half, zero, block)], axis=0
    )


def lanes_of(p):
    return slice(p * LANES, (p + 1) * LANES)


def row_of(ref):
    return ref[...].astype(F32).reshape(1, -1)


def start_copies(pairs_of_refs, sems, at=0):
    copies = [
        pltpu.make_async_copy(src, dst, sems.at[at + i]) for i, (src, dst) in enumerate(pairs_of_refs)
    ]
    for copy in copies:
        copy.start()
    return copies


def project_rows(parts, weights, biases, kinds, outs, arriving=()):
    for n, (i, weight, out) in enumerate(zip(kinds, weights, outs)):
        if arriving:
            arriving[n].wait()
        at = 0
        for part in parts[:1] if i == 0 else parts:
            here = slice(at, at + part.shape[0])
            at += part.shape[0]
            block = (dot(part[...], weight[...]) + biases[i : i + 1, :]).astype(BF16)
            out[here, :] = block * jnp.asarray(0.125, BF16) if i == 0 else block


def late_queries_kernel(upper, lower, weight, biases, out):
    half = upper.shape[0]
    project_rows([upper], [weight], biases, (0,), [out.at[0:half, :]])
    project_rows([lower], [weight], biases, (0,), [out.at[half : 2 * half, :]])


def fwd_kernel(n_parts, first, far, kinds, pairs, unused, ready, *refs):
    refs = list(refs)

    def take(count):
        got = refs[:count]
        del refs[:count]
        return got

    parts = take(n_parts)
    if first:
        weights_far, vectors, (prefix_keys, prefix_values, task) = take(3), take(3), take(3)
    else:
        weights, (biases,) = take(len(kinds)), take(1)
        stacked_in, top_in, sum_in, acc_in = take(4)
    take(unused)
    rows_out = take(len(kinds))
    if first:
        stacked_out, prefix_k, prefix_v, left_out = take(4)
        weights, (biases,) = take(3), take(1)
    top_out, sum_out, acc_out = take(3)
    here_out = take(len(kinds)) if far else rows_out
    q_out, k_out, v_out = here_out if first else ([None] + list(here_out))[-3:]
    (sems,) = take(1)
    rows = acc_out.shape[0]
    low_half = lane_iota(rows) < HEAD_DIM
    arriving = start_copies(zip(weights_far, weights), sems, 3) if first else []
    ready()
    if first:
        for i, vector in enumerate(vectors):
            biases[i : i + 1, :] = row_of(vector)
        slot_count = prefix_keys.shape[0]
        prefix_k[...] = jnp.zeros_like(prefix_k)
        prefix_v[...] = jnp.zeros_like(prefix_v)
        prefix_k[0:slot_count, :] = prefix_keys[...]
        prefix_v[0:slot_count, :] = prefix_values[...]
        kept = jnp.where(task[0] == 0, 20, jnp.where(task[0] == 1, 64, slot_count))
        slot = lax.broadcasted_iota(jnp.int32, (1, prefix_k.shape[0]), 1)
        slot_bias = jnp.where(slot < kept, 0.0, masked_score)
        slot = lax.broadcasted_iota(jnp.int32, left_out.shape, 0)
        left_out[...] = jnp.where(slot < kept, 0.0, 1.0)

    def attend(p, stacked, sources, before):
        cols = lanes_of(p)
        tiles = []
        for key, value, bias in sources:
            score = dot(stacked, key, NT)
            if bias is not None:
                score = score + bias
            tiles.append([score[:, i : i + LANES] for i in range(0, score.shape[1], LANES)])
        top = functools.reduce(jnp.maximum, sum(tiles, []))
        top = jnp.broadcast_to(jnp.max(top, axis=1, keepdims=True), top.shape)
        if before is not None:
            old = before[0][p]
            top = jnp.maximum(top, old)
        top_out[p] = top
        total = None
        for (key, value, bias), group in zip(sources, tiles):
            probs = jnp.concatenate([jnp.exp(tile - top).astype(BF16) for tile in group], axis=1)
            wide = jnp.concatenate([value, jnp.ones_like(value)], axis=1)
            term = dot(probs, wide)
            total = term if total is None else total + term
        acc = jnp.where(low_half, total[0:rows, 0:LANES], total[rows:, 0:LANES])
        sums = jnp.where(low_half, total[0:rows, LANES:], total[rows:, LANES:])
        if before is not None:
            alpha = jnp.exp(old - top)
            alpha = jnp.where(low_half, alpha[0:rows], alpha[rows:])
            sums = sums + before[1][:, cols] * alpha
            acc = acc + before[2][:, cols] * alpha
        sum_out[:, cols] = sums
        acc_out[:, cols] = acc

    project_rows(parts, weights, biases, kinds, here_out, arriving)
    leaving = start_copies(zip(here_out, rows_out), sems) if far else []
    for p in range(pairs):
        cols = lanes_of(p)
        sources = [(k_out[:, cols], v_out[:, cols], None)]
        if first:
            stacked = stack_pair(q_out[:, cols], low_half)
            stacked_out[p] = stacked
            sources.append((prefix_k[:, cols], prefix_v[:, cols], slot_bias))
            attend(p, stacked, sources, None)
        else:
            attend(p, stacked_in[p], sources, (top_in, sum_in, acc_in))
    for copy in leaving:
        copy.wait()


def size_of(shape, kind):
    n = jnp.dtype(kind).itemsize
    for dim in shape:
        n *= dim
    return n


class Arg(NamedTuple):
    array: Any
    how: str = "copy"


class Out(NamedTuple):
    shape: tuple
    kind: Any
    how: str = "vmem"


def call(kernel, outs, args, flops, name, scratch=(), side=None, spare=MARGIN, lazy=False, alias=None):
    outs, args, scratch = list(outs), list(args), list(scratch)
    n_args, n_outs = len(args), len(outs)
    if side is not None:
        side_kernel, side_outs, side_args = side
        args += side_args
        outs += side_outs
    copied = [i for i, a in enumerate(args) if a.how == "copy"]
    held = sum(size_of(a.array.shape, a.array.dtype) for a in args if a.how in ("copy", "auto"))
    held += sum(size_of(o.shape, o.kind) for o in outs if o.how == "auto")
    held += sum(size_of(*o) for o in scratch if isinstance(o, tuple))
    spaces = {
        "vmem": pltpu.VMEM,
        "auto": pltpu.VMEM,
        "copy": pltpu.HBM,
        "hbm": pltpu.HBM,
        "smem": pltpu.SMEM,
    }

    def placed(arg):
        if arg.how in ("vmem", "hbm", "copy"):
            return pltpu.with_memory_space_constraint(arg.array, spaces[arg.how])
        return arg.array

    own = [(args[i].array.shape, args[i].array.dtype) for i in copied]
    if copied:
        own.append(pltpu.SemaphoreType.DMA((len(copied),)))

    def body(*refs):
        ins = list(refs[: len(args)])
        results = refs[len(args) : len(args) + len(outs)]
        extra = refs[len(args) + len(outs) :]
        if copied:
            sems = extra[len(copied)]
            copies = start_copies([(ins[i], extra[n]) for n, i in enumerate(copied)], sems)
            for n, i in enumerate(copied):
                ins[i] = extra[n]

        def ready():
            if copied:
                for copy in copies:
                    copy.wait()

        if side is not None:
            side_kernel(*ins[n_args:], *results[n_outs:])
        if lazy:
            kernel(ready, *ins[:n_args], *results[:n_outs], *extra[len(own) :])
        else:
            ready()
            kernel(*ins[:n_args], *results[:n_outs], *extra[len(own) :])

    n_bytes = sum(size_of(a.array.shape, a.array.dtype) for a in args if a.how != "vmem")
    got = pl.pallas_call(
        body,
        out_shape=[
            (pltpu.VMEM if o.how == "vmem" else pltpu.HBM)(o.shape, o.kind) for o in outs
        ],
        in_specs=[pl.BlockSpec(memory_space=spaces[a.how]) for a in args],
        out_specs=[pl.BlockSpec(memory_space=spaces[o.how]) for o in outs],
        scratch_shapes=[pltpu.VMEM(*o) if isinstance(o, tuple) else o for o in own + scratch],
        input_output_aliases=alias or {},
        compiler_params=pltpu.CompilerParams(vmem_limit_bytes=held + spare),
        cost_estimate=pl.CostEstimate(
            flops=int(flops * COST), bytes_accessed=int(n_bytes * COST), transcendentals=0
        ),
        name=name,
    )(*[placed(a) for a in args])
    return (got[:n_outs], got[n_outs:]) if side is not None else got


def norm_forward(values, gain, shift):
    center = values - jnp.mean(values, axis=-1, keepdims=True)
    inv_spread = lax.rsqrt(jnp.mean(center * center, axis=-1, keepdims=True) + eps_norm)
    normed = center * inv_spread
    return (normed * gain + shift, normed, inv_spread)


def norm_backward(upstream, normed, inv_spread, gain):
    scaled = upstream * gain
    return inv_spread * (
        scaled
        - jnp.mean(scaled, axis=-1, keepdims=True)
        - normed * jnp.mean(scaled * normed, axis=-1, keepdims=True)
    )


def middle_kernel(
    pairs, n_up, ready, hidden, m_in, l_in, acc_in, grad, bo, g1, s1, up_bias, down_bias, g2, s2,
    wo, *refs,
):
    up, down, layer_out, res_out, pay_out, slope_ref = refs
    rows, width = hidden.shape
    chunk = up.shape[1] // n_up
    low_half = lane_iota(rows) < HEAD_DIM
    lane = lane_iota(rows)
    vec = row_of
    sums = l_in[...]
    attended = acc_in[...] / sums
    branch = dot(attended.astype(BF16), wo[...])
    ready()
    residual = hidden[...].astype(F32) + branch + vec(bo)
    first_norm, first_normed, first_spread = norm_forward(residual, vec(g1), vec(s1))
    first_low = first_norm.astype(BF16)
    ffn = jnp.zeros((rows, width), F32)
    up_row = row_of(up_bias)
    for c in range(n_up):
        cols = slice(c * chunk, (c + 1) * chunk)
        pre = dot(first_low, up[:, cols]) + up_row[:, cols]
        phi = 0.5 * (1.0 + lax.erf(pre * root_half))
        slope_ref[:, cols] = (phi + pre * jnp.exp(-0.5 * pre * pre) * inv_root_tau).astype(BF16)
        ffn = ffn + dot((pre * phi).astype(BF16), down[cols, :])
    layer, second_normed, second_spread = norm_forward(
        first_norm + ffn + vec(down_bias), vec(g2), vec(s2)
    )
    layer_out[...] = layer.astype(BF16)
    sum_grad = norm_backward(grad[...].astype(F32), second_normed, second_spread, vec(g2))
    sum_low = sum_grad.astype(BF16)
    first_grad = sum_grad
    for c in range(n_up):
        cols = slice(c * chunk, (c + 1) * chunk)
        pre_grad = dot(sum_low, down[cols, :], NT) * slope_ref[:, cols]
        first_grad = first_grad + dot(pre_grad.astype(BF16), up[:, cols], NT)
    res_grad = norm_backward(first_grad, first_normed, first_spread, vec(g1))
    res_out[...] = res_grad
    upstream = dot(res_grad.astype(BF16), wo[...], NT).astype(BF16)
    log_sums = jnp.log(sums)
    lse = jnp.zeros((rows, LANES), F32)
    product = upstream.astype(F32) * attended
    delta = jnp.zeros((rows, LANES), F32)
    for p in range(pairs):
        block = product[:, lanes_of(p)]
        for e in range(2):
            keep = low_half if e == 0 else jnp.logical_not(low_half)
            part = jnp.sum(jnp.where(keep, block, 0.0), axis=1, keepdims=True)
            delta = jnp.where(lane == p + 8 * e, part, delta)
            at = p * LANES + e * HEAD_DIM
            head_lse = m_in[p, e * rows : (e + 1) * rows, :] + log_sums[:, at : at + 1]
            lse = jnp.where(lane == p + 8 * e, head_lse, lse)

    def pieces(values, count):
        got = []
        for _ in range(count):
            low = values.astype(BF16).astype(F32)
            got.append(low)
            values = values - low
        return got

    aux = jnp.where(lane == LANES - 1, 1.0, 0.0)
    for i, piece in enumerate(pieces(lse, 3) + pieces(delta, 2)):
        moved = piece if i == 0 else pltpu.roll(piece, 16 * i, 1)
        aux = jnp.where((lane >= 16 * i) & (lane < 16 * i + 16), moved, aux)
    payload = jnp.concatenate([upstream, aux.astype(BF16)], axis=1)
    pay_out[...] = payload


def aux_masks(rows, p):
    lane = lane_iota(2 * rows)
    side = jnp.where(lax.broadcasted_iota(jnp.int32, (2 * rows, LANES), 0) < rows, 0, 8)
    own = lax.rem(lane, 16) == p + side
    return own & (lane < 48), own & (lane >= 48) & (lane < 80), lane == LANES - 1


def query_grad_kernel(n_blocks, far, chosen, *refs):
    mask, queries, payload, base, wq, prefix_k, prefix_v = refs[:7]
    all_keys = refs[7 : 7 + n_blocks]
    all_values = refs[7 + n_blocks : 7 + 2 * n_blocks]
    out, grad_ref, *own = refs[7 + 2 * n_blocks :]
    rows, width = queries.shape
    span = pl.ds(chosen[0] * LANES, len(chosen) * LANES)
    arriving = []
    if far:
        keys, values, sems = own
        for b in range(n_blocks):
            moves = [
                (all_keys[b].at[:, span], keys.at[b]),
                (all_values[b].at[:, span], values.at[b]),
            ]
            arriving.append(start_copies(moves, sems, 2 * b))
    slots = prefix_k.shape[0]
    low_half = lane_iota(rows) < HEAD_DIM
    aux = payload[:, width : width + LANES]
    aux2 = jnp.concatenate([aux, aux], axis=0)
    zero = jnp.zeros_like(aux2)

    def minus_ones(count):
        return jnp.where(lane_iota(count) < 80, -1.0, 0.0)

    left_out = (lane_iota(slots) == LANES - 1) & (mask[...] > 0.5)
    prefix_tail = jnp.where(left_out, masked_score, minus_ones(slots)).astype(BF16)
    tail = minus_ones(rows).astype(BF16)
    for n, p in enumerate(chosen):
        cols, here = lanes_of(p), lanes_of(n)
        for_scores, for_delta, for_bias = aux_masks(rows, p)
        q_wide = jnp.concatenate(
            [
                stack_pair(queries[:, cols], low_half),
                jnp.where(for_scores | for_bias, aux2, zero),
            ],
            axis=1,
        )
        d_wide = jnp.concatenate(
            [
                stack_pair(payload[:, cols], low_half),
                jnp.where(for_delta, aux2, zero),
            ],
            axis=1,
        )
        total = None
        for b in range(-1, n_blocks):
            if b < 0:
                key, value, ends = prefix_k[:, cols], prefix_v[:, cols], prefix_tail
            elif far:
                if n == 0:
                    for copy in arriving[b]:
                        copy.wait()
                key, value, ends = keys[b, :, here], values[b, :, here], tail
            else:
                key, value, ends = all_keys[b][:, cols], all_values[b][:, cols], tail
            probs = jnp.exp(dot(q_wide, jnp.concatenate([key, ends], axis=1), NT))
            products = dot(d_wide, jnp.concatenate([value, ends], axis=1), NT)
            term = dot((probs * products).astype(BF16), key)
            total = term if total is None else total + term
        both = jnp.where(low_half, total[0:rows], total[rows : 2 * rows])
        grad_ref[:, here] = (both * 0.125).astype(BF16)
    chosen_cols = slice(chosen[0] * LANES, (chosen[-1] + 1) * LANES)
    out[...] = base[...] + dot(grad_ref[...], wq[:, chosen_cols], NT)


def tall(parts, cols):
    return jnp.concatenate([part[:, cols] for part in parts], axis=0)


def key_terms(sets, q_block, d_block, aux, p):
    k_wide, v_wide = [], []
    for key, value, left_out in sets:
        low_half = lane_iota(key.shape[0]) < HEAD_DIM
        for_scores, for_delta, for_bias = aux_masks(key.shape[0], p)
        tail = jnp.where(for_scores, -1.0, 0.0)
        if left_out is not None:
            tail = jnp.where(for_bias & left_out, masked_score, tail)
        k_wide.append(jnp.concatenate([stack_pair(key, low_half), tail.astype(BF16)], axis=1))
        tail = jnp.where(for_delta, -1.0, 0.0).astype(BF16)
        v_wide.append(jnp.concatenate([stack_pair(value, low_half), tail], axis=1))
    k_wide, v_wide = jnp.concatenate(k_wide, axis=0), jnp.concatenate(v_wide, axis=0)
    probs = jnp.exp(dot(k_wide, jnp.concatenate([q_block, aux], axis=1), NT))
    products = dot(v_wide, jnp.concatenate([d_block, aux], axis=1), NT)
    value_total = dot(probs.astype(BF16), d_block)
    key_total = dot((probs * products).astype(BF16), q_block)
    terms, at = [], 0
    for key, _, _ in sets:
        rows = key.shape[0]
        low_half = lane_iota(rows) < HEAD_DIM
        for total in (key_total, value_total):
            upper, lower = total[at : at + rows], total[at + rows : at + 2 * rows]
            terms.append(jnp.where(low_half, upper, lower))
        at += 2 * rows
    return terms


def own_grad_kernel(pairs, *refs):
    keys, values, side_keys, side_values, queries, payload, prefix_k, prefix_v, mask = refs[:9]
    *outs, out, sent = refs[9:]
    width = queries.shape[1]
    slots = prefix_k.shape[0]
    aux = payload[:, width : width + LANES]
    left_out = jnp.concatenate([mask[...], mask[...]], axis=0) > 0.5
    for p in range(pairs):
        cols = lanes_of(p)
        sets = [
            (keys[:, cols], values[:, cols], None),
            (side_keys[:, cols], side_values[:, cols], None),
            (prefix_k[:, cols], prefix_v[:, cols], left_out),
        ]
        terms = key_terms(sets, queries[:, cols], payload[:, cols], aux, p)
        for ref, term in zip(outs, terms):
            ref[:, cols] = term
        out[0:slots, cols] = terms[4].astype(BF16)
        out[slots : 2 * slots, cols] = terms[5].astype(BF16)
    sent[...] = out[part_of(out.shape[0], "seq", 2, 1), :]


def part_of(height, axis, parts, flip):
    at = lax.rem(lax.axis_index(axis), parts)
    other = jnp.int32(0)
    for bit in range(parts.bit_length() - 1):
        digit = lax.rem(at // (1 << bit), 2)
        other = other + (1 << bit) * (1 - digit if (flip >> bit) % 2 else digit)
    return pl.ds(pl.multiple_of(other * (height // parts), 16), height // parts)


def scatter_kernel(axis, parts, then, terms, *refs):
    got, out, sent = refs[: parts - 1], refs[parts - 1], refs[parts:]
    total = terms[part_of(terms.shape[0], axis, parts, 0), :].astype(F32)
    for ref in got:
        total = total + ref[...].astype(F32)
    out[...] = total.astype(out.dtype)
    for i, ref in enumerate(sent):
        ref[...] = out[part_of(out.shape[0], then, len(sent) + 1, i + 1), :]


def add_kernel(terms, *refs):
    total = terms[...].astype(F32)
    for ref in refs[:-1]:
        total = total + ref[...].astype(F32)
    refs[-1][...] = total.astype(BF16)


def join_kernel(axis, parts, terms, *refs):
    out = refs[-1]
    for flip, ref in enumerate((terms,) + refs[:-1]):
        out[part_of(out.shape[0], axis, parts, flip), :] = ref[...]


def join_last_kernel(slot_count, terms, got, key_out, value_out):
    lower = lax.rem(lax.axis_index("seq"), 2) == 0
    for out, mine in ((key_out, lower), (value_out, jnp.logical_not(lower))):
        rows = jnp.where(mine, terms[...].astype(F32), got[...].astype(F32))
        out[...] = rows[0:slot_count, :]


def key_grad_kernel(pairs, n_sets, n_queries, send, *refs):
    refs = list(refs)

    def take(count):
        got = refs[:count]
        del refs[:count]
        return got

    key_sets = [take(2) for _ in range(n_sets)]
    q_refs, (pay,) = take(n_queries), take(1)
    before, outs = take(2 * n_sets), take(1 if send else 2 * n_sets)
    width = pay.shape[1] - LANES
    aux = pay[:, width : width + LANES]
    for p in range(pairs):
        cols = lanes_of(p)
        sets = [(keys[:, cols], values[:, cols], None) for keys, values in key_sets]
        terms = key_terms(sets, tall(q_refs, cols), pay[:, cols], aux, p)
        terms = [term + ref[:, cols] for term, ref in zip(terms, before)]
        if send:
            outs[0][:, cols] = terms[0].astype(BF16)
            outs[0][:, lanes_of(pairs + p)] = terms[1].astype(BF16)
        else:
            for ref, term in zip(outs, terms):
                ref[:, cols] = term


def input_grad_kernel(key_terms_ref, value_terms_ref, came, partial, wk, wv, out):
    width = out.shape[1]
    key_low = (key_terms_ref[...] + came[:, 0:width].astype(F32)).astype(BF16)
    value_low = (value_terms_ref[...] + came[:, width : 2 * width].astype(F32)).astype(BF16)
    total = partial[...] + dot(key_low, wk[...], NT) + dot(value_low, wv[...], NT)
    out[...] = total.astype(BF16)


def after(value, *others):
    return lax.optimization_barrier((value, *others))[0]


def sum_steps(dp, seq, slots, width, slot_count):
    def rows_out(count):
        return Out((count, width), BF16)

    dp_flips, part = range(1, dp), slots // dp
    last = [Out((slot_count, width), F32, "auto")] * 2
    return [
        (
            ("seq", [1]),
            functools.partial(scatter_kernel, "seq", 2, "dp"),
            [rows_out(slots)] + [rows_out(part)] * (dp - 1),
        ),
        (("dp", dp_flips), functools.partial(scatter_kernel, "dp", dp, ""), [rows_out(part)]),
        (("seq", range(2, seq, 2)), add_kernel, [rows_out(part)]),
        (("dp", dp_flips), functools.partial(join_kernel, "dp", dp), [rows_out(slots)]),
        (("seq", [1]), functools.partial(join_last_kernel, slot_count), last),
    ]


def per_device(
    hidden_in,
    task_ids,
    prefix_keys,
    prefix_values,
    query_weight,
    query_bias,
    key_weight,
    key_bias,
    value_weight,
    value_bias,
    out_weight,
    out_bias,
    norm1_gain,
    norm1_bias,
    up_weight,
    up_bias,
    down_weight,
    down_bias,
    norm2_gain,
    norm2_bias,
    out_grad,
):
    rows, width = hidden_in.shape
    pairs = width // LANES
    ff = up_weight.shape[1]
    seq = lax.axis_size("seq")
    chips = seq // 2
    slot_count = prefix_keys.shape[0]
    slots = -(-slot_count // LANES) * LANES
    loop = [*range(0, chips, 2), *range(1, chips, 2)[::-1]]
    ring = [
        (2 * loop[i] + c, 2 * loop[(i + 1) % chips] + c) for i in range(chips) for c in range(2)
    ]
    swap = [(i, i ^ 1) for i in range(seq)]

    half = rows // 2

    wide = (rows, width)

    def ring_hop(block):
        return lax.ppermute(block, "seq", ring)

    def swapped(block):
        return lax.ppermute(block, "seq", swap)

    def walk(block, use, done, between, ahead):
        here, flying = block, ring_hop(block)
        for hop in range(chips):
            if hop:
                here = after(flying, done[-1], *ahead(hop))
                if hop < chips - 1:
                    flying = ring_hop(here)
            use(hop, after(here, done[-1]))
            between.get(hop, lambda: None)()

    def walk_in_halves(block, use, done):
        halves = block[0 : rows // 2], block[rows // 2 : rows]
        flying = [ring_hop(half) for half in halves]
        other = swapped(after(block, *halves))
        hops = 2 * chips - 2
        use(0, [block])
        parts = [other]
        for step in range(hops):
            here = after(flying.pop(0), done[-1])
            if step < hops - 2:
                flying.append(ring_hop(here))
            use(step + 1, [after(part, done[-1], here) for part in parts])
            parts = [here, swapped(here)]
        use(hops + 1, [after(part, done[-1]) for part in parts])

    state = [Out((pairs, 2 * rows, LANES), F32), Out(wide, F32), Out(wide, F32)]
    far = seq > 8
    q_list, k_list, v_list, attended, held, masks, late_parts = [], [], [], [], [], [], []
    near_weights = []

    def attend(step, parts):
        late = step >= seq // 2
        kinds = (1, 2) if late or step == 1 else (0, 1, 2)
        weights = [near_weights[i] for i in kinds] if step else []
        shapes = [(parts[0].shape[0], width) if i == 0 else wide for i in kinds]
        rows_out = [Out(shape, BF16, "hbm" if far else "vmem") for shape in shapes]
        scratch = [(shape, BF16) for shape in shapes] if far else []
        scratch += [pltpu.SemaphoreType.DMA((9,))]
        early = {2: [out_weight, up_weight], 4: [down_weight]}.get(step, [])
        kernel = functools.partial(fwd_kernel, len(parts), step == 0, far, kinds, pairs, len(early))
        if step == 0:
            got = call(
                kernel,
                rows_out
                + [Out((pairs, 2 * rows, LANES), BF16, "vmem")]
                + [Out((slots, width), BF16)] * 2
                + [Out((slots, LANES), F32)]
                + [Out((width, width), BF16)] * 3
                + [Out((3, width), F32)]
                + state,
                [Arg(part) for part in parts]
                + [Arg(w, "hbm") for w in (query_weight, key_weight, value_weight)]
                + [Arg(v) for v in (query_bias, key_bias, value_bias, prefix_keys, prefix_values)]
                + [Arg(task_ids, "smem")],
                10 * rows * width * width, "attend_first", scratch, lazy=True,
            )
            masks[:] = got[6:7]
            near_weights[:] = got[7:10]
            held[:] = got[3:6] + got[10:14]
        else:
            got = call(
                kernel,
                rows_out + state,
                [Arg(part, "auto") for part in parts]
                + [Arg(w, "vmem") for w in weights + held[3:4] + held[0:1] + held[4:7] + early],
                8 * rows * width * width, "attend_%d" % len(parts), scratch, lazy=True,
            )
            held[4:7] = got[len(kinds) : len(kinds) + 3]
        if late:
            late_parts.append(parts[0])
        elif step != 1:
            q_list.append(got[0])
        k_list.append(got[len(kinds) - 2])
        v_list.append(got[len(kinds) - 1])
        attended.append(k_list[-1])

    walk_in_halves(hidden_in, attend, attended)
    prefix_k, prefix_v, state_now = held[1], held[2], held[4:7]
    q0, key_pairs = q_list[0], [k_list[0], v_list[0], k_list[1], v_list[1]]
    layer_out, res_grad, payload = call(
        functools.partial(middle_kernel, pairs, 4),
        [Out(wide, BF16, "auto"), Out(wide, F32), Out((rows, width + LANES), BF16)],
        [Arg(hidden_in)]
        + [Arg(a, "vmem") for a in state_now]
        + [Arg(a) for a in (out_grad, out_bias, norm1_gain, norm1_bias)]
        + [Arg(a) for a in (up_bias, down_bias, norm2_gain, norm2_bias)]
        + [Arg(a, "vmem") for a in (out_weight, up_weight, down_weight)],
        8 * rows * width * ff, "middle", [((rows, ff), BF16)], spare=12 * 1024 * 1024, lazy=True,
    )
    near_rows = "copy" if far else "vmem"
    prefix = [Arg(prefix_k, "vmem"), Arg(prefix_v, "vmem")]
    sums = sum_steps(lax.axis_size("dp"), seq, slots, width, slot_count)
    trading, pending, done = [], [], [res_grad]

    def trade():
        if sums:
            (axis, flips), _, _ = sums[0]
            kept, sent = trading[0], trading[1:] or trading[:1] * len(flips)
            partners = [[(i, i ^ f) for i in range(lax.axis_size(axis))] for f in flips]
            pending[:] = [lax.ppermute(b, axis, p) for b, p in zip(sent, partners)]

    def exchange():
        _, job, outs = sums.pop(0)
        got = [trading[0]] + [after(g, done[-1]) for g in pending]
        pending[:] = []
        return job, outs, [Arg(a, "auto") for a in got]

    partial_now = [res_grad]

    def query_grads(first_pair, each):
        chosen = tuple(range(first_pair, first_pair + each))
        scratch = [((rows, each * LANES), BF16)]
        if far:
            scratch += [((seq, rows, each * LANES), BF16)] * 2 + [pltpu.SemaphoreType.DMA((2 * seq,))]
        partial_now[:] = call(
            functools.partial(query_grad_kernel, seq, far, chosen),
            [Out(wide, F32)],
            [Arg(masks[0], "vmem"), Arg(q0, near_rows), Arg(after(payload, done[-1]), "vmem")]
            + [Arg(partial_now[0], "vmem"), Arg(query_weight, "vmem")]
            + prefix
            + [Arg(a, "hbm" if far else "vmem") for a in k_list + v_list],
            24 * rows * rows * seq * each * LANES, "query_grad_%d" % first_pair, scratch,
        )
        done.append(partial_now[0])

    key_state = []

    def key_grads(hop, part):
        near_keys = [Arg(a, near_rows) for a in key_pairs]
        if hop == 0:
            got = call(
                functools.partial(own_grad_kernel, pairs),
                [Out(wide, F32)] * 4 + [Out((2 * slots, width), BF16), Out((slots, width), BF16)],
                near_keys
                + [Arg(q0, near_rows), Arg(part, "vmem"), *prefix, Arg(masks[0], "vmem")],
                80 * rows * rows * width, "own_grads",
            )
            key_state[:], trading[:] = got[:4], got[4:]
            done.append(key_state[0])
            return trade()
        q_blocks = [Arg(a, near_rows) for a in q_rows(hop)]

        def terms(sets, send, side=None):
            return call(
                functools.partial(key_grad_kernel, pairs, len(sets), len(q_blocks), send),
                [Out((rows, 2 * width), BF16)] if send else [Out(wide, F32)] * (2 * len(sets)),
                [near_keys[2 * i + j] for i in sets for j in range(2)]
                + q_blocks
                + [Arg(part, "auto")]
                + [Arg(key_state[2 * i + j], "vmem") for i in sets for j in range(2)],
                32 * rows * rows * width * len(sets), "key_grad_%d" % len(sets), side=side,
            )

        if hop < chips - 1:
            side = exchange() if hop == 2 else None
            got = terms((0, 1), False, side)
            if side is not None:
                got, trading[:] = got
                trade()
            key_state[:] = got
            done.append(key_state[0])
            return
        (sending,) = terms((1,), True)
        done.append(sending)
        came = swapped(sending)
        near_keys[0] = Arg(after(near_keys[0].array, sending), near_rows)
        own = terms((0,), False)
        done.append(own[0])
        key_state[:], trading[:] = call(
            input_grad_kernel,
            [Out(wide, BF16, "auto")],
            [Arg(a, "vmem") for a in own]
            + [Arg(after(came, own[0]), "auto")]
            + [Arg(a, "vmem") for a in (partial_now[0], key_weight, value_weight)],
            4 * rows * width * width, "input_grad", side=exchange(),
        )

    def settle():
        job, outs, args = exchange()
        trading[:] = call(job, outs, args, 0, "settle")
        done.append(trading[0])
        trade()

    def q_rows(hop):
        early = (len(q_list) - 1) // 2
        return q_list[2 * hop - 1 : 2 * hop + 1] if hop <= early else late_list[hop - early - 1 :][:1]

    late_list = []

    def late_queries():
        for i in range(0, len(late_parts), 2):
            (block,) = call(
                late_queries_kernel,
                [Out(wide, BF16)],
                [Arg(after(part, done[-1]), "auto") for part in late_parts[i : i + 2]]
                + [Arg(query_weight, "vmem"), Arg(held[3], "vmem")],
                2 * rows * width * width, "late_queries",
            )
            late_list.append(block)
            done.append(block)

    between = {
        0: lambda: (query_grads(0, 1), settle(), late_queries(), settle()),
        1: lambda: query_grads(1, 5),
        2: lambda: (query_grads(6, 2), settle()),
    }
    walk(payload, key_grads, done, between, lambda hop: pending if hop == 2 else [])
    (result,) = key_state
    return (layer_out, result, *trading)


def solution(mesh):
    rows = P(("dp", "seq"), None)
    return jax.shard_map(
        per_device,
        mesh=mesh,
        in_specs=(rows, P("dp")) + (P(),) * 18 + (rows,),
        out_specs=(rows, rows, P(), P()),
        check_vma=False,
    )
```

```python
import functools
from typing import Any, NamedTuple

import jax
import jax.numpy as jnp
from jax import lax
from jax.experimental import pallas as pl
from jax.experimental.pallas import tpu as pltpu
from jax.sharding import PartitionSpec as P

HEAD_DIM = 64
LANES = 128
F32 = jnp.float32
BF16 = jnp.bfloat16
eps_norm = 1e-05
masked_score = -1e30
root_half = 0.7071067811865476
inv_root_tau = 0.3989422804014327
MARGIN = 4 * 1024 * 1024
COST = 0.05
NT = (((1,), (1,)), ((), ()))
NN = (((1,), (0,)), ((), ()))


def dot(left, right, dims=NN):
    return lax.dot_general(left, right, dims, preferred_element_type=F32)


def lane_iota(rows):
    return lax.broadcasted_iota(jnp.int32, (rows, LANES), 1)


def stack_pair(block, low_half):
    zero = jnp.zeros_like(block)
    return jnp.concatenate(
        [jnp.where(low_half, block, zero), jnp.where(low_half, zero, block)], axis=0
    )


def lanes_of(p):
    return slice(p * LANES, (p + 1) * LANES)


def row_of(ref):
    return ref[...].astype(F32).reshape(1, -1)


def start_copies(pairs_of_refs, sems, at=0):
    copies = [
        pltpu.make_async_copy(src, dst, sems.at[at + i]) for i, (src, dst) in enumerate(pairs_of_refs)
    ]
    for copy in copies:
        copy.start()
    return copies


def project_rows(parts, weights, biases, kinds, outs, arriving=()):
    for n, (i, weight, out) in enumerate(zip(kinds, weights, outs)):
        if arriving:
            arriving[n].wait()
        at = 0
        for part in parts[:1] if i == 0 else parts:
            here = slice(at, at + part.shape[0])
            at += part.shape[0]
            block = (dot(part[...], weight[...]) + biases[i : i + 1, :]).astype(BF16)
            out[here, :] = block * jnp.asarray(0.125, BF16) if i == 0 else block


def late_queries_kernel(upper, lower, weight, biases, out):
    half = upper.shape[0]
    project_rows([upper], [weight], biases, (0,), [out.at[0:half, :]])
    project_rows([lower], [weight], biases, (0,), [out.at[half : 2 * half, :]])


def fwd_kernel(n_parts, first, far, kinds, pairs, unused, ready, *refs):
    refs = list(refs)

    def take(count):
        got = refs[:count]
        del refs[:count]
        return got

    parts = take(n_parts)
    if first:
        weights_far, vectors, (prefix_keys, prefix_values, task) = take(3), take(3), take(3)
    else:
        weights, (biases,) = take(len(kinds)), take(1)
        stacked_in, top_in, sum_in, acc_in = take(4)
    take(unused)
    rows_out = take(len(kinds))
    if first:
        stacked_out, prefix_k, prefix_v, left_out = take(4)
        weights, (biases,) = take(3), take(1)
    top_out, sum_out, acc_out = take(3)
    here_out = take(len(kinds)) if far else rows_out
    q_out, k_out, v_out = here_out if first else ([None] + list(here_out))[-3:]
    (sems,) = take(1)
    rows = acc_out.shape[0]
    low_half = lane_iota(rows) < HEAD_DIM
    arriving = start_copies(zip(weights_far, weights), sems, 3) if first else []
    ready()
    if first:
        for i, vector in enumerate(vectors):
            biases[i : i + 1, :] = row_of(vector)
        slot_count = prefix_keys.shape[0]
        prefix_k[...] = jnp.zeros_like(prefix_k)
        prefix_v[...] = jnp.zeros_like(prefix_v)
        prefix_k[0:slot_count, :] = prefix_keys[...]
        prefix_v[0:slot_count, :] = prefix_values[...]
        kept = jnp.where(task[0] == 0, 20, jnp.where(task[0] == 1, 64, slot_count))
        slot = lax.broadcasted_iota(jnp.int32, (1, prefix_k.shape[0]), 1)
        slot_bias = jnp.where(slot < kept, 0.0, masked_score)
        slot = lax.broadcasted_iota(jnp.int32, left_out.shape, 0)
        left_out[...] = jnp.where(slot < kept, 0.0, 1.0)

    def attend(p, stacked, sources, before):
        cols = lanes_of(p)
        tiles = []
        for key, value, bias in sources:
            score = dot(stacked, key, NT)
            if bias is not None:
                score = score + bias
            tiles.append([score[:, i : i + LANES] for i in range(0, score.shape[1], LANES)])
        top = functools.reduce(jnp.maximum, sum(tiles, []))
        top = jnp.broadcast_to(jnp.max(top, axis=1, keepdims=True), top.shape)
        if before is not None:
            old = before[0][p]
            top = jnp.maximum(top, old)
        top_out[p] = top
        total = None
        for (key, value, bias), group in zip(sources, tiles):
            probs = jnp.concatenate([jnp.exp(tile - top).astype(BF16) for tile in group], axis=1)
            wide = jnp.concatenate([value, jnp.ones_like(value)], axis=1)
            term = dot(probs, wide)
            total = term if total is None else total + term
        acc = jnp.where(low_half, total[0:rows, 0:LANES], total[rows:, 0:LANES])
        sums = jnp.where(low_half, total[0:rows, LANES:], total[rows:, LANES:])
        if before is not None:
            alpha = jnp.exp(old - top)
            alpha = jnp.where(low_half, alpha[0:rows], alpha[rows:])
            sums = sums + before[1][:, cols] * alpha
            acc = acc + before[2][:, cols] * alpha
        sum_out[:, cols] = sums
        acc_out[:, cols] = acc

    project_rows(parts, weights, biases, kinds, here_out, arriving)
    leaving = start_copies(zip(here_out, rows_out), sems) if far else []
    for p in range(pairs):
        cols = lanes_of(p)
        sources = [(k_out[:, cols], v_out[:, cols], None)]
        if first:
            stacked = stack_pair(q_out[:, cols], low_half)
            stacked_out[p] = stacked
            sources.append((prefix_k[:, cols], prefix_v[:, cols], slot_bias))
            attend(p, stacked, sources, None)
        else:
            attend(p, stacked_in[p], sources, (top_in, sum_in, acc_in))
    for copy in leaving:
        copy.wait()


def size_of(shape, kind):
    n = jnp.dtype(kind).itemsize
    for dim in shape:
        n *= dim
    return n


class Arg(NamedTuple):
    array: Any
    how: str = "copy"


class Out(NamedTuple):
    shape: tuple
    kind: Any
    how: str = "vmem"


def call(kernel, outs, args, flops, name, scratch=(), side=None, spare=MARGIN, lazy=False, alias=None):
    outs, args, scratch = list(outs), list(args), list(scratch)
    n_args, n_outs = len(args), len(outs)
    if side is not None:
        side_kernel, side_outs, side_args = side
        args += side_args
        outs += side_outs
    copied = [i for i, a in enumerate(args) if a.how == "copy"]
    held = sum(size_of(a.array.shape, a.array.dtype) for a in args if a.how in ("copy", "auto"))
    held += sum(size_of(o.shape, o.kind) for o in outs if o.how == "auto")
    held += sum(size_of(*o) for o in scratch if isinstance(o, tuple))
    spaces = {
        "vmem": pltpu.VMEM,
        "auto": pltpu.VMEM,
        "copy": pltpu.HBM,
        "hbm": pltpu.HBM,
        "smem": pltpu.SMEM,
    }

    def placed(arg):
        if arg.how in ("vmem", "hbm", "copy"):
            return pltpu.with_memory_space_constraint(arg.array, spaces[arg.how])
        return arg.array

    own = [(args[i].array.shape, args[i].array.dtype) for i in copied]
    if copied:
        own.append(pltpu.SemaphoreType.DMA((len(copied),)))

    def body(*refs):
        ins = list(refs[: len(args)])
        results = refs[len(args) : len(args) + len(outs)]
        extra = refs[len(args) + len(outs) :]
        if copied:
            sems = extra[len(copied)]
            copies = start_copies([(ins[i], extra[n]) for n, i in enumerate(copied)], sems)
            for n, i in enumerate(copied):
                ins[i] = extra[n]

        def ready():
            if copied:
                for copy in copies:
                    copy.wait()

        if side is not None:
            side_kernel(*ins[n_args:], *results[n_outs:])
        if lazy:
            kernel(ready, *ins[:n_args], *results[:n_outs], *extra[len(own) :])
        else:
            ready()
            kernel(*ins[:n_args], *results[:n_outs], *extra[len(own) :])

    n_bytes = sum(size_of(a.array.shape, a.array.dtype) for a in args if a.how != "vmem")
    got = pl.pallas_call(
        body,
        out_shape=[
            (pltpu.VMEM if o.how == "vmem" else pltpu.HBM)(o.shape, o.kind) for o in outs
        ],
        in_specs=[pl.BlockSpec(memory_space=spaces[a.how]) for a in args],
        out_specs=[pl.BlockSpec(memory_space=spaces[o.how]) for o in outs],
        scratch_shapes=[pltpu.VMEM(*o) if isinstance(o, tuple) else o for o in own + scratch],
        input_output_aliases=alias or {},
        compiler_params=pltpu.CompilerParams(vmem_limit_bytes=held + spare),
        cost_estimate=pl.CostEstimate(
            flops=int(flops * COST), bytes_accessed=int(n_bytes * COST), transcendentals=0
        ),
        name=name,
    )(*[placed(a) for a in args])
    return (got[:n_outs], got[n_outs:]) if side is not None else got


def norm_forward(values, gain, shift):
    center = values - jnp.mean(values, axis=-1, keepdims=True)
    inv_spread = lax.rsqrt(jnp.mean(center * center, axis=-1, keepdims=True) + eps_norm)
    normed = center * inv_spread
    return (normed * gain + shift, normed, inv_spread)


def norm_backward(upstream, normed, inv_spread, gain):
    scaled = upstream * gain
    return inv_spread * (
        scaled
        - jnp.mean(scaled, axis=-1, keepdims=True)
        - normed * jnp.mean(scaled * normed, axis=-1, keepdims=True)
    )


def middle_kernel(
    pairs, n_up, ready, hidden, m_in, l_in, acc_in, grad, bo, g1, s1, up_bias, down_bias, g2, s2,
    wo, *refs,
):
    up, down, layer_out, res_out, pay_out, slope_ref = refs
    rows, width = hidden.shape
    chunk = up.shape[1] // n_up
    low_half = lane_iota(rows) < HEAD_DIM
    lane = lane_iota(rows)
    vec = row_of
    sums = l_in[...]
    attended = acc_in[...] / sums
    branch = dot(attended.astype(BF16), wo[...])
    ready()
    residual = hidden[...].astype(F32) + branch + vec(bo)
    first_norm, first_normed, first_spread = norm_forward(residual, vec(g1), vec(s1))
    first_low = first_norm.astype(BF16)
    ffn = jnp.zeros((rows, width), F32)
    up_row = row_of(up_bias)
    for c in range(n_up):
        cols = slice(c * chunk, (c + 1) * chunk)
        pre = dot(first_low, up[:, cols]) + up_row[:, cols]
        phi = 0.5 * (1.0 + lax.erf(pre * root_half))
        slope_ref[:, cols] = (phi + pre * jnp.exp(-0.5 * pre * pre) * inv_root_tau).astype(BF16)
        ffn = ffn + dot((pre * phi).astype(BF16), down[cols, :])
    layer, second_normed, second_spread = norm_forward(
        first_norm + ffn + vec(down_bias), vec(g2), vec(s2)
    )
    layer_out[...] = layer.astype(BF16)
    sum_grad = norm_backward(grad[...].astype(F32), second_normed, second_spread, vec(g2))
    sum_low = sum_grad.astype(BF16)
    first_grad = sum_grad
    for c in range(n_up):
        cols = slice(c * chunk, (c + 1) * chunk)
        pre_grad = dot(sum_low, down[cols, :], NT) * slope_ref[:, cols]
        first_grad = first_grad + dot(pre_grad.astype(BF16), up[:, cols], NT)
    res_grad = norm_backward(first_grad, first_normed, first_spread, vec(g1))
    res_out[...] = res_grad
    upstream = dot(res_grad.astype(BF16), wo[...], NT).astype(BF16)
    log_sums = jnp.log(sums)
    lse = jnp.zeros((rows, LANES), F32)
    product = upstream.astype(F32) * attended
    delta = jnp.zeros((rows, LANES), F32)
    for p in range(pairs):
        block = product[:, lanes_of(p)]
        for e in range(2):
            keep = low_half if e == 0 else jnp.logical_not(low_half)
            part = jnp.sum(jnp.where(keep, block, 0.0), axis=1, keepdims=True)
            delta = jnp.where(lane == p + 8 * e, part, delta)
            at = p * LANES + e * HEAD_DIM
            head_lse = m_in[p, e * rows : (e + 1) * rows, :] + log_sums[:, at : at + 1]
            lse = jnp.where(lane == p + 8 * e, head_lse, lse)

    def pieces(values, count):
        got = []
        for _ in range(count):
            low = values.astype(BF16).astype(F32)
            got.append(low)
            values = values - low
        return got

    aux = jnp.where(lane == LANES - 1, 1.0, 0.0)
    for i, piece in enumerate(pieces(lse, 3) + pieces(delta, 2)):
        moved = piece if i == 0 else pltpu.roll(piece, 16 * i, 1)
        aux = jnp.where((lane >= 16 * i) & (lane < 16 * i + 16), moved, aux)
    payload = jnp.concatenate([upstream, aux.astype(BF16)], axis=1)
    pay_out[...] = payload


def aux_masks(rows, p):
    lane = lane_iota(2 * rows)
    side = jnp.where(lax.broadcasted_iota(jnp.int32, (2 * rows, LANES), 0) < rows, 0, 8)
    own = lax.rem(lane, 16) == p + side
    return own & (lane < 48), own & (lane >= 48) & (lane < 80), lane == LANES - 1


def query_grad_kernel(n_blocks, far, chosen, *refs):
    mask, queries, payload, base, wq, prefix_k, prefix_v = refs[:7]
    all_keys = refs[7 : 7 + n_blocks]
    all_values = refs[7 + n_blocks : 7 + 2 * n_blocks]
    out, grad_ref, *own = refs[7 + 2 * n_blocks :]
    rows, width = queries.shape
    span = pl.ds(chosen[0] * LANES, len(chosen) * LANES)
    arriving = []
    if far:
        keys, values, sems = own
        for b in range(n_blocks):
            moves = [
                (all_keys[b].at[:, span], keys.at[b]),
                (all_values[b].at[:, span], values.at[b]),
            ]
            arriving.append(start_copies(moves, sems, 2 * b))
    slots = prefix_k.shape[0]
    low_half = lane_iota(rows) < HEAD_DIM
    aux = payload[:, width : width + LANES]
    aux2 = jnp.concatenate([aux, aux], axis=0)
    zero = jnp.zeros_like(aux2)

    def minus_ones(count):
        return jnp.where(lane_iota(count) < 80, -1.0, 0.0)

    left_out = (lane_iota(slots) == LANES - 1) & (mask[...] > 0.5)
    prefix_tail = jnp.where(left_out, masked_score, minus_ones(slots)).astype(BF16)
    tail = minus_ones(rows).astype(BF16)
    for n, p in enumerate(chosen):
        cols, here = lanes_of(p), lanes_of(n)
        for_scores, for_delta, for_bias = aux_masks(rows, p)
        q_wide = jnp.concatenate(
            [
                stack_pair(queries[:, cols], low_half),
                jnp.where(for_scores | for_bias, aux2, zero),
            ],
            axis=1,
        )
        d_wide = jnp.concatenate(
            [
                stack_pair(payload[:, cols], low_half),
                jnp.where(for_delta, aux2, zero),
            ],
            axis=1,
        )
        total = None
        for b in range(-1, n_blocks):
            if b < 0:
                key, value, ends = prefix_k[:, cols], prefix_v[:, cols], prefix_tail
            elif far:
                if n == 0:
                    for copy in arriving[b]:
                        copy.wait()
                key, value, ends = keys[b, :, here], values[b, :, here], tail
            else:
                key, value, ends = all_keys[b][:, cols], all_values[b][:, cols], tail
            probs = jnp.exp(dot(q_wide, jnp.concatenate([key, ends], axis=1), NT))
            products = dot(d_wide, jnp.concatenate([value, ends], axis=1), NT)
            term = dot((probs * products).astype(BF16), key)
            total = term if total is None else total + term
        both = jnp.where(low_half, total[0:rows], total[rows : 2 * rows])
        grad_ref[:, here] = (both * 0.125).astype(BF16)
    chosen_cols = slice(chosen[0] * LANES, (chosen[-1] + 1) * LANES)
    out[...] = base[...] + dot(grad_ref[...], wq[:, chosen_cols], NT)


def tall(parts, cols):
    return jnp.concatenate([part[:, cols] for part in parts], axis=0)


def key_terms(sets, q_block, d_block, aux, p):
    k_wide, v_wide = [], []
    for key, value, left_out in sets:
        low_half = lane_iota(key.shape[0]) < HEAD_DIM
        for_scores, for_delta, for_bias = aux_masks(key.shape[0], p)
        tail = jnp.where(for_scores, -1.0, 0.0)
        if left_out is not None:
            tail = jnp.where(for_bias & left_out, masked_score, tail)
        k_wide.append(jnp.concatenate([stack_pair(key, low_half), tail.astype(BF16)], axis=1))
        tail = jnp.where(for_delta, -1.0, 0.0).astype(BF16)
        v_wide.append(jnp.concatenate([stack_pair(value, low_half), tail], axis=1))
    k_wide, v_wide = jnp.concatenate(k_wide, axis=0), jnp.concatenate(v_wide, axis=0)
    probs = jnp.exp(dot(k_wide, jnp.concatenate([q_block, aux], axis=1), NT))
    products = dot(v_wide, jnp.concatenate([d_block, aux], axis=1), NT)
    value_total = dot(probs.astype(BF16), d_block)
    key_total = dot((probs * products).astype(BF16), q_block)
    terms, at = [], 0
    for key, _, _ in sets:
        rows = key.shape[0]
        low_half = lane_iota(rows) < HEAD_DIM
        for total in (key_total, value_total):
            upper, lower = total[at : at + rows], total[at + rows : at + 2 * rows]
            terms.append(jnp.where(low_half, upper, lower))
        at += 2 * rows
    return terms


def own_grad_kernel(pairs, *refs):
    keys, values, side_keys, side_values, queries, payload, prefix_k, prefix_v, mask = refs[:9]
    *outs, out, sent = refs[9:]
    width = queries.shape[1]
    slots = prefix_k.shape[0]
    aux = payload[:, width : width + LANES]
    left_out = jnp.concatenate([mask[...], mask[...]], axis=0) > 0.5
    for p in range(pairs):
        cols = lanes_of(p)
        sets = [
            (keys[:, cols], values[:, cols], None),
            (side_keys[:, cols], side_values[:, cols], None),
            (prefix_k[:, cols], prefix_v[:, cols], left_out),
        ]
        terms = key_terms(sets, queries[:, cols], payload[:, cols], aux, p)
        for ref, term in zip(outs, terms):
            ref[:, cols] = term
        out[0:slots, cols] = terms[4].astype(BF16)
        out[slots : 2 * slots, cols] = terms[5].astype(BF16)
    sent[...] = out[part_of(out.shape[0], "seq", 2, 1), :]


def part_of(height, axis, parts, flip):
    at = lax.rem(lax.axis_index(axis), parts)
    other = jnp.int32(0)
    for bit in range(parts.bit_length() - 1):
        digit = lax.rem(at // (1 << bit), 2)
        other = other + (1 << bit) * (1 - digit if (flip >> bit) % 2 else digit)
    return pl.ds(pl.multiple_of(other * (height // parts), 16), height // parts)


def scatter_kernel(axis, parts, then, terms, *refs):
    got, out, sent = refs[: parts - 1], refs[parts - 1], refs[parts:]
    total = terms[part_of(terms.shape[0], axis, parts, 0), :].astype(F32)
    for ref in got:
        total = total + ref[...].astype(F32)
    out[...] = total.astype(out.dtype)
    for i, ref in enumerate(sent):
        ref[...] = out[part_of(out.shape[0], then, len(sent) + 1, i + 1), :]


def add_kernel(terms, *refs):
    total = terms[...].astype(F32)
    for ref in refs[:-1]:
        total = total + ref[...].astype(F32)
    refs[-1][...] = total.astype(BF16)


def join_kernel(axis, parts, terms, *refs):
    out = refs[-1]
    for flip, ref in enumerate((terms,) + refs[:-1]):
        out[part_of(out.shape[0], axis, parts, flip), :] = ref[...]


def join_last_kernel(slot_count, terms, got, key_out, value_out):
    lower = lax.rem(lax.axis_index("seq"), 2) == 0
    for out, mine in ((key_out, lower), (value_out, jnp.logical_not(lower))):
        rows = jnp.where(mine, terms[...].astype(F32), got[...].astype(F32))
        out[...] = rows[0:slot_count, :]


def key_grad_kernel(pairs, n_sets, n_queries, send, *refs):
    refs = list(refs)

    def take(count):
        got = refs[:count]
        del refs[:count]
        return got

    key_sets = [take(2) for _ in range(n_sets)]
    q_refs, (pay,) = take(n_queries), take(1)
    before, outs = take(2 * n_sets), take(1 if send else 2 * n_sets)
    width = pay.shape[1] - LANES
    aux = pay[:, width : width + LANES]
    for p in range(pairs):
        cols = lanes_of(p)
        sets = [(keys[:, cols], values[:, cols], None) for keys, values in key_sets]
        terms = key_terms(sets, tall(q_refs, cols), pay[:, cols], aux, p)
        terms = [term + ref[:, cols] for term, ref in zip(terms, before)]
        if send:
            outs[0][:, cols] = terms[0].astype(BF16)
            outs[0][:, lanes_of(pairs + p)] = terms[1].astype(BF16)
        else:
            for ref, term in zip(outs, terms):
                ref[:, cols] = term


def input_grad_kernel(key_terms_ref, value_terms_ref, came, partial, wk, wv, out):
    width = out.shape[1]
    key_low = (key_terms_ref[...] + came[:, 0:width].astype(F32)).astype(BF16)
    value_low = (value_terms_ref[...] + came[:, width : 2 * width].astype(F32)).astype(BF16)
    total = partial[...] + dot(key_low, wk[...], NT) + dot(value_low, wv[...], NT)
    out[...] = total.astype(BF16)


def after(value, *others):
    return lax.optimization_barrier((value, *others))[0]


def sum_steps(dp, seq, slots, width, slot_count):
    def rows_out(count):
        return Out((count, width), BF16)

    dp_flips, part = range(1, dp), slots // dp
    last = [Out((slot_count, width), F32, "auto")] * 2
    return [
        (
            ("seq", [1]),
            functools.partial(scatter_kernel, "seq", 2, "dp"),
            [rows_out(slots)] + [rows_out(part)] * (dp - 1),
        ),
        (("dp", dp_flips), functools.partial(scatter_kernel, "dp", dp, ""), [rows_out(part)]),
        (("seq", range(2, seq, 2)), add_kernel, [rows_out(part)]),
        (("dp", dp_flips), functools.partial(join_kernel, "dp", dp), [rows_out(slots)]),
        (("seq", [1]), functools.partial(join_last_kernel, slot_count), last),
    ]


def per_device(
    hidden_in,
    task_ids,
    prefix_keys,
    prefix_values,
    query_weight,
    query_bias,
    key_weight,
    key_bias,
    value_weight,
    value_bias,
    out_weight,
    out_bias,
    norm1_gain,
    norm1_bias,
    up_weight,
    up_bias,
    down_weight,
    down_bias,
    norm2_gain,
    norm2_bias,
    out_grad,
):
    rows, width = hidden_in.shape
    pairs = width // LANES
    ff = up_weight.shape[1]
    seq = lax.axis_size("seq")
    chips = seq // 2
    slot_count = prefix_keys.shape[0]
    slots = -(-slot_count // LANES) * LANES
    loop = [*range(0, chips, 2), *range(1, chips, 2)[::-1]]
    ring = [
        (2 * loop[i] + c, 2 * loop[(i + 1) % chips] + c) for i in range(chips) for c in range(2)
    ]
    swap = [(i, i ^ 1) for i in range(seq)]

    half = rows // 2

    wide = (rows, width)

    def ring_hop(block):
        return lax.ppermute(block, "seq", ring)

    def swapped(block):
        return lax.ppermute(block, "seq", swap)

    def walk(block, use, done, between, ahead):
        here, flying = block, ring_hop(block)
        for hop in range(chips):
            if hop:
                here = after(flying, done[-1], *ahead(hop))
                if hop < chips - 1:
                    flying = ring_hop(here)
            use(hop, after(here, done[-1]))
            between.get(hop, lambda: None)()

    def walk_in_halves(block, use, done):
        halves = block[0 : rows // 2], block[rows // 2 : rows]
        flying = [ring_hop(half) for half in halves]
        other = swapped(after(block, *halves))
        hops = 2 * chips - 2
        use(0, [block])
        parts = [other]
        for step in range(hops):
            here = after(flying.pop(0), done[-1])
            if step < hops - 2:
                flying.append(ring_hop(here))
            use(step + 1, [after(part, done[-1], here) for part in parts])
            parts = [here, swapped(here)]
        use(hops + 1, [after(part, done[-1]) for part in parts])

    state = [Out((pairs, 2 * rows, LANES), F32), Out(wide, F32), Out(wide, F32)]
    far = seq > 8
    q_list, k_list, v_list, attended, held, masks, late_parts = [], [], [], [], [], [], []
    near_weights = []

    def attend(step, parts):
        late = step > 1
        kinds = (1, 2) if late or step == 1 else (0, 1, 2)
        weights = [near_weights[i] for i in kinds] if step else []
        shapes = [(parts[0].shape[0], width) if i == 0 else wide for i in kinds]
        rows_out = [Out(shape, BF16, "hbm" if far else "vmem") for shape in shapes]
        scratch = [(shape, BF16) for shape in shapes] if far else []
        scratch += [pltpu.SemaphoreType.DMA((9,))]
        early = {2: [out_weight, up_weight], 4: [down_weight]}.get(step, [])
        kernel = functools.partial(fwd_kernel, len(parts), step == 0, far, kinds, pairs, len(early))
        if step == 0:
            got = call(
                kernel,
                rows_out
                + [Out((pairs, 2 * rows, LANES), BF16, "vmem")]
                + [Out((slots, width), BF16)] * 2
                + [Out((slots, LANES), F32)]
                + [Out((width, width), BF16)] * 3
                + [Out((3, width), F32)]
                + state,
                [Arg(part) for part in parts]
                + [Arg(w, "hbm") for w in (query_weight, key_weight, value_weight)]
                + [Arg(v) for v in (query_bias, key_bias, value_bias, prefix_keys, prefix_values)]
                + [Arg(task_ids, "smem")],
                10 * rows * width * width, "attend_first", scratch, lazy=True,
            )
            masks[:] = got[6:7]
            near_weights[:] = got[7:10]
            held[:] = got[3:6] + got[10:14]
        else:
            got = call(
                kernel,
                rows_out + state,
                [Arg(part, "auto") for part in parts]
                + [Arg(w, "vmem") for w in weights + held[3:4] + held[0:1] + held[4:7] + early],
                8 * rows * width * width, "attend_%d" % len(parts), scratch, lazy=True,
            )
            held[4:7] = got[len(kinds) : len(kinds) + 3]
        if late:
            late_parts.append(parts[0])
        elif step != 1:
            q_list.append(got[0])
        k_list.append(got[len(kinds) - 2])
        v_list.append(got[len(kinds) - 1])
        attended.append(k_list[-1])

    walk_in_halves(hidden_in, attend, attended)
    prefix_k, prefix_v, state_now = held[1], held[2], held[4:7]
    q0, key_pairs = q_list[0], [k_list[0], v_list[0], k_list[1], v_list[1]]
    layer_out, res_grad, payload = call(
        functools.partial(middle_kernel, pairs, 4),
        [Out(wide, BF16, "auto"), Out(wide, F32), Out((rows, width + LANES), BF16)],
        [Arg(hidden_in)]
        + [Arg(a, "vmem") for a in state_now]
        + [Arg(a) for a in (out_grad, out_bias, norm1_gain, norm1_bias)]
        + [Arg(a) for a in (up_bias, down_bias, norm2_gain, norm2_bias)]
        + [Arg(a, "vmem") for a in (out_weight, up_weight, down_weight)],
        8 * rows * width * ff, "middle", [((rows, ff), BF16)], spare=12 * 1024 * 1024, lazy=True,
    )
    near_rows = "copy" if far else "vmem"
    prefix = [Arg(prefix_k, "vmem"), Arg(prefix_v, "vmem")]
    sums = sum_steps(lax.axis_size("dp"), seq, slots, width, slot_count)
    trading, pending, done = [], [], [res_grad]

    def trade():
        if sums:
            (axis, flips), _, _ = sums[0]
            kept, sent = trading[0], trading[1:] or trading[:1] * len(flips)
            partners = [[(i, i ^ f) for i in range(lax.axis_size(axis))] for f in flips]
            pending[:] = [lax.ppermute(b, axis, p) for b, p in zip(sent, partners)]

    def exchange():
        _, job, outs = sums.pop(0)
        got = [trading[0]] + [after(g, done[-1]) for g in pending]
        pending[:] = []
        return job, outs, [Arg(a, "auto") for a in got]

    partial_now = [res_grad]

    def query_grads(first_pair, each):
        chosen = tuple(range(first_pair, first_pair + each))
        scratch = [((rows, each * LANES), BF16)]
        if far:
            scratch += [((seq, rows, each * LANES), BF16)] * 2 + [pltpu.SemaphoreType.DMA((2 * seq,))]
        partial_now[:] = call(
            functools.partial(query_grad_kernel, seq, far, chosen),
            [Out(wide, F32)],
            [Arg(masks[0], "vmem"), Arg(q0, near_rows), Arg(after(payload, done[-1]), "vmem")]
            + [Arg(partial_now[0], "vmem"), Arg(query_weight, "vmem")]
            + prefix
            + [Arg(a, "hbm" if far else "vmem") for a in k_list + v_list],
            24 * rows * rows * seq * each * LANES, "query_grad_%d" % first_pair, scratch,
        )
        done.append(partial_now[0])

    key_state = []

    def key_grads(hop, part):
        near_keys = [Arg(a, near_rows) for a in key_pairs]
        if hop == 0:
            got = call(
                functools.partial(own_grad_kernel, pairs),
                [Out(wide, F32)] * 4 + [Out((2 * slots, width), BF16), Out((slots, width), BF16)],
                near_keys
                + [Arg(q0, near_rows), Arg(part, "vmem"), *prefix, Arg(masks[0], "vmem")],
                80 * rows * rows * width, "own_grads",
            )
            key_state[:], trading[:] = got[:4], got[4:]
            done.append(key_state[0])
            return trade()
        q_blocks = [Arg(a, near_rows) for a in q_rows(hop)]

        def terms(sets, send, side=None):
            return call(
                functools.partial(key_grad_kernel, pairs, len(sets), len(q_blocks), send),
                [Out((rows, 2 * width), BF16)] if send else [Out(wide, F32)] * (2 * len(sets)),
                [near_keys[2 * i + j] for i in sets for j in range(2)]
                + q_blocks
                + [Arg(part, "auto")]
                + [Arg(key_state[2 * i + j], "vmem") for i in sets for j in range(2)],
                32 * rows * rows * width * len(sets), "key_grad_%d" % len(sets), side=side,
            )

        if hop < chips - 1:
            side = exchange() if hop == 2 else None
            got = terms((0, 1), False, side)
            if side is not None:
                got, trading[:] = got
                trade()
            key_state[:] = got
            done.append(key_state[0])
            return
        (sending,) = terms((1,), True)
        done.append(sending)
        came = swapped(sending)
        near_keys[0] = Arg(after(near_keys[0].array, sending), near_rows)
        own = terms((0,), False)
        done.append(own[0])
        key_state[:], trading[:] = call(
            input_grad_kernel,
            [Out(wide, BF16, "auto")],
            [Arg(a, "vmem") for a in own]
            + [Arg(after(came, own[0]), "auto")]
            + [Arg(a, "vmem") for a in (partial_now[0], key_weight, value_weight)],
            4 * rows * width * width, "input_grad", side=exchange(),
        )

    def settle():
        job, outs, args = exchange()
        trading[:] = call(job, outs, args, 0, "settle")
        done.append(trading[0])
        trade()

    def q_rows(hop):
        early = (len(q_list) - 1) // 2
        return q_list[2 * hop - 1 : 2 * hop + 1] if hop <= early else late_list[hop - early - 1 :][:1]

    late_list = []

    def late_queries():
        for i in range(0, len(late_parts), 2):
            (block,) = call(
                late_queries_kernel,
                [Out(wide, BF16)],
                [Arg(after(part, done[-1]), "auto") for part in late_parts[i : i + 2]]
                + [Arg(query_weight, "vmem"), Arg(held[3], "vmem")],
                2 * rows * width * width, "late_queries",
            )
            late_list.append(block)
            done.append(block)

    between = {
        0: lambda: (query_grads(0, 1), settle(), late_queries(), settle()),
        1: lambda: query_grads(1, 5),
        2: lambda: (query_grads(6, 2), settle()),
    }
    walk(payload, key_grads, done, between, lambda hop: pending if hop == 2 else [])
    (result,) = key_state
    return (layer_out, result, *trading)


def solution(mesh):
    rows = P(("dp", "seq"), None)
    return jax.shard_map(
        per_device,
        mesh=mesh,
        in_specs=(rows, P("dp")) + (P(),) * 18 + (rows,),
        out_specs=(rows, rows, P(), P()),
        check_vma=False,
    )
```

```python
import functools
from typing import Any, NamedTuple

import jax
import jax.numpy as jnp
from jax import lax
from jax.experimental import pallas as pl
from jax.experimental.pallas import tpu as pltpu
from jax.sharding import PartitionSpec as P

HEAD_DIM = 64
LANES = 128
F32 = jnp.float32
BF16 = jnp.bfloat16
eps_norm = 1e-05
masked_score = -1e30
root_half = 0.7071067811865476
inv_root_tau = 0.3989422804014327
MARGIN = 4 * 1024 * 1024
COST = 0.05
NT = (((1,), (1,)), ((), ()))
NN = (((1,), (0,)), ((), ()))


def dot(left, right, dims=NN):
    return lax.dot_general(left, right, dims, preferred_element_type=F32)


def lane_iota(rows):
    return lax.broadcasted_iota(jnp.int32, (rows, LANES), 1)


def stack_pair(block, low_half):
    zero = jnp.zeros_like(block)
    return jnp.concatenate(
        [jnp.where(low_half, block, zero), jnp.where(low_half, zero, block)], axis=0
    )


def lanes_of(p):
    return slice(p * LANES, (p + 1) * LANES)


def row_of(ref):
    return ref[...].astype(F32).reshape(1, -1)


def start_copies(pairs_of_refs, sems, at=0):
    copies = [
        pltpu.make_async_copy(src, dst, sems.at[at + i]) for i, (src, dst) in enumerate(pairs_of_refs)
    ]
    for copy in copies:
        copy.start()
    return copies


def project_rows(parts, weights, biases, kinds, outs, arriving=()):
    for n, (i, weight, out) in enumerate(zip(kinds, weights, outs)):
        if arriving:
            arriving[n].wait()
        at = 0
        for part in parts[:1] if i == 0 else parts:
            here = slice(at, at + part.shape[0])
            at += part.shape[0]
            block = (dot(part[...], weight[...]) + biases[i : i + 1, :]).astype(BF16)
            out[here, :] = block * jnp.asarray(0.125, BF16) if i == 0 else block


def late_queries_kernel(upper, lower, weight, biases, out):
    half = upper.shape[0]
    project_rows([upper], [weight], biases, (0,), [out.at[0:half, :]])
    project_rows([lower], [weight], biases, (0,), [out.at[half : 2 * half, :]])


def fwd_kernel(n_parts, first, far, kinds, pairs, unused, ready, *refs):
    refs = list(refs)

    def take(count):
        got = refs[:count]
        del refs[:count]
        return got

    parts = take(n_parts)
    if first:
        weights_far, vectors, (prefix_keys, prefix_values, task) = take(3), take(3), take(3)
    else:
        weights, (biases,) = take(len(kinds)), take(1)
        stacked_in, top_in, sum_in, acc_in = take(4)
    take(unused)
    rows_out = take(len(kinds))
    if first:
        stacked_out, prefix_k, prefix_v, left_out = take(4)
        weights, (biases,) = take(3), take(1)
    top_out, sum_out, acc_out = take(3)
    here_out = take(len(kinds)) if far else rows_out
    q_out, k_out, v_out = here_out if first else ([None] + list(here_out))[-3:]
    (sems,) = take(1)
    rows = acc_out.shape[0]
    low_half = lane_iota(rows) < HEAD_DIM
    arriving = start_copies(zip(weights_far, weights), sems, 3) if first else []
    ready()
    if first:
        for i, vector in enumerate(vectors):
            biases[i : i + 1, :] = row_of(vector)
        slot_count = prefix_keys.shape[0]
        prefix_k[...] = jnp.zeros_like(prefix_k)
        prefix_v[...] = jnp.zeros_like(prefix_v)
        prefix_k[0:slot_count, :] = prefix_keys[...]
        prefix_v[0:slot_count, :] = prefix_values[...]
        kept = jnp.where(task[0] == 0, 20, jnp.where(task[0] == 1, 64, slot_count))
        slot = lax.broadcasted_iota(jnp.int32, (1, prefix_k.shape[0]), 1)
        slot_bias = jnp.where(slot < kept, 0.0, masked_score)
        slot = lax.broadcasted_iota(jnp.int32, left_out.shape, 0)
        left_out[...] = jnp.where(slot < kept, 0.0, 1.0)

    def attend(p, stacked, sources, before):
        cols = lanes_of(p)
        tiles = []
        for key, value, bias in sources:
            score = dot(stacked, key, NT)
            if bias is not None:
                score = score + bias
            tiles.append([score[:, i : i + LANES] for i in range(0, score.shape[1], LANES)])
        top = functools.reduce(jnp.maximum, sum(tiles, []))
        top = jnp.broadcast_to(jnp.max(top, axis=1, keepdims=True), top.shape)
        if before is not None:
            old = before[0][p]
            top = jnp.maximum(top, old)
        top_out[p] = top
        total = None
        for (key, value, bias), group in zip(sources, tiles):
            probs = jnp.concatenate([jnp.exp(tile - top).astype(BF16) for tile in group], axis=1)
            wide = jnp.concatenate([value, jnp.ones_like(value)], axis=1)
            term = dot(probs, wide)
            total = term if total is None else total + term
        acc = jnp.where(low_half, total[0:rows, 0:LANES], total[rows:, 0:LANES])
        sums = jnp.where(low_half, total[0:rows, LANES:], total[rows:, LANES:])
        if before is not None:
            alpha = jnp.exp(old - top)
            alpha = jnp.where(low_half, alpha[0:rows], alpha[rows:])
            sums = sums + before[1][:, cols] * alpha
            acc = acc + before[2][:, cols] * alpha
        sum_out[:, cols] = sums
        acc_out[:, cols] = acc

    project_rows(parts, weights, biases, kinds, here_out, arriving)
    leaving = start_copies(zip(here_out, rows_out), sems) if far else []
    for p in range(pairs):
        cols = lanes_of(p)
        sources = [(k_out[:, cols], v_out[:, cols], None)]
        if first:
            stacked = stack_pair(q_out[:, cols], low_half)
            stacked_out[p] = stacked
            sources.append((prefix_k[:, cols], prefix_v[:, cols], slot_bias))
            attend(p, stacked, sources, None)
        else:
            attend(p, stacked_in[p], sources, (top_in, sum_in, acc_in))
    for copy in leaving:
        copy.wait()


def size_of(shape, kind):
    n = jnp.dtype(kind).itemsize
    for dim in shape:
        n *= dim
    return n


class Arg(NamedTuple):
    array: Any
    how: str = "copy"


class Out(NamedTuple):
    shape: tuple
    kind: Any
    how: str = "vmem"


def call(kernel, outs, args, flops, name, scratch=(), side=None, spare=MARGIN, lazy=False, alias=None):
    outs, args, scratch = list(outs), list(args), list(scratch)
    n_args, n_outs = len(args), len(outs)
    if side is not None:
        side_kernel, side_outs, side_args = side
        args += side_args
        outs += side_outs
    copied = [i for i, a in enumerate(args) if a.how == "copy"]
    held = sum(size_of(a.array.shape, a.array.dtype) for a in args if a.how in ("copy", "auto"))
    held += sum(size_of(o.shape, o.kind) for o in outs if o.how == "auto")
    held += sum(size_of(*o) for o in scratch if isinstance(o, tuple))
    spaces = {
        "vmem": pltpu.VMEM,
        "auto": pltpu.VMEM,
        "copy": pltpu.HBM,
        "hbm": pltpu.HBM,
        "smem": pltpu.SMEM,
    }

    def placed(arg):
        if arg.how in ("vmem", "hbm", "copy"):
            return pltpu.with_memory_space_constraint(arg.array, spaces[arg.how])
        return arg.array

    own = [(args[i].array.shape, args[i].array.dtype) for i in copied]
    if copied:
        own.append(pltpu.SemaphoreType.DMA((len(copied),)))

    def body(*refs):
        ins = list(refs[: len(args)])
        results = refs[len(args) : len(args) + len(outs)]
        extra = refs[len(args) + len(outs) :]
        if copied:
            sems = extra[len(copied)]
            copies = start_copies([(ins[i], extra[n]) for n, i in enumerate(copied)], sems)
            for n, i in enumerate(copied):
                ins[i] = extra[n]

        def ready():
            if copied:
                for copy in copies:
                    copy.wait()

        if side is not None:
            side_kernel(*ins[n_args:], *results[n_outs:])
        if lazy:
            kernel(ready, *ins[:n_args], *results[:n_outs], *extra[len(own) :])
        else:
            ready()
            kernel(*ins[:n_args], *results[:n_outs], *extra[len(own) :])

    n_bytes = sum(size_of(a.array.shape, a.array.dtype) for a in args if a.how != "vmem")
    got = pl.pallas_call(
        body,
        out_shape=[
            (pltpu.VMEM if o.how == "vmem" else pltpu.HBM)(o.shape, o.kind) for o in outs
        ],
        in_specs=[pl.BlockSpec(memory_space=spaces[a.how]) for a in args],
        out_specs=[pl.BlockSpec(memory_space=spaces[o.how]) for o in outs],
        scratch_shapes=[pltpu.VMEM(*o) if isinstance(o, tuple) else o for o in own + scratch],
        input_output_aliases=alias or {},
        compiler_params=pltpu.CompilerParams(vmem_limit_bytes=held + spare),
        cost_estimate=pl.CostEstimate(
            flops=int(flops * COST), bytes_accessed=int(n_bytes * COST), transcendentals=0
        ),
        name=name,
    )(*[placed(a) for a in args])
    return (got[:n_outs], got[n_outs:]) if side is not None else got


def norm_forward(values, gain, shift):
    center = values - jnp.mean(values, axis=-1, keepdims=True)
    inv_spread = lax.rsqrt(jnp.mean(center * center, axis=-1, keepdims=True) + eps_norm)
    normed = center * inv_spread
    return (normed * gain + shift, normed, inv_spread)


def norm_backward(upstream, normed, inv_spread, gain):
    scaled = upstream * gain
    return inv_spread * (
        scaled
        - jnp.mean(scaled, axis=-1, keepdims=True)
        - normed * jnp.mean(scaled * normed, axis=-1, keepdims=True)
    )


def middle_kernel(
    pairs, n_up, ready, hidden, m_in, l_in, acc_in, grad, bo, g1, s1, up_bias, down_bias, g2, s2,
    wo, *refs,
):
    up, down, layer_out, res_out, pay_out, slope_ref = refs
    rows, width = hidden.shape
    chunk = up.shape[1] // n_up
    low_half = lane_iota(rows) < HEAD_DIM
    lane = lane_iota(rows)
    vec = row_of
    sums = l_in[...]
    attended = acc_in[...] / sums
    branch = dot(attended.astype(BF16), wo[...])
    ready()
    residual = hidden[...].astype(F32) + branch + vec(bo)
    first_norm, first_normed, first_spread = norm_forward(residual, vec(g1), vec(s1))
    first_low = first_norm.astype(BF16)
    ffn = jnp.zeros((rows, width), F32)
    up_row = row_of(up_bias)
    for c in range(n_up):
        cols = slice(c * chunk, (c + 1) * chunk)
        pre = dot(first_low, up[:, cols]) + up_row[:, cols]
        phi = 0.5 * (1.0 + lax.erf(pre * root_half))
        slope_ref[:, cols] = (phi + pre * jnp.exp(-0.5 * pre * pre) * inv_root_tau).astype(BF16)
        ffn = ffn + dot((pre * phi).astype(BF16), down[cols, :])
    layer, second_normed, second_spread = norm_forward(
        first_norm + ffn + vec(down_bias), vec(g2), vec(s2)
    )
    layer_out[...] = layer.astype(BF16)
    sum_grad = norm_backward(grad[...].astype(F32), second_normed, second_spread, vec(g2))
    sum_low = sum_grad.astype(BF16)
    first_grad = sum_grad
    for c in range(n_up):
        cols = slice(c * chunk, (c + 1) * chunk)
        pre_grad = dot(sum_low, down[cols, :], NT) * slope_ref[:, cols]
        first_grad = first_grad + dot(pre_grad.astype(BF16), up[:, cols], NT)
    res_grad = norm_backward(first_grad, first_normed, first_spread, vec(g1))
    res_out[...] = res_grad
    upstream = dot(res_grad.astype(BF16), wo[...], NT).astype(BF16)
    log_sums = jnp.log(sums)
    lse = jnp.zeros((rows, LANES), F32)
    product = upstream.astype(F32) * attended
    delta = jnp.zeros((rows, LANES), F32)
    for p in range(pairs):
        block = product[:, lanes_of(p)]
        for e in range(2):
            keep = low_half if e == 0 else jnp.logical_not(low_half)
            part = jnp.sum(jnp.where(keep, block, 0.0), axis=1, keepdims=True)
            delta = jnp.where(lane == p + 8 * e, part, delta)
            at = p * LANES + e * HEAD_DIM
            head_lse = m_in[p, e * rows : (e + 1) * rows, :] + log_sums[:, at : at + 1]
            lse = jnp.where(lane == p + 8 * e, head_lse, lse)

    def pieces(values, count):
        got = []
        for _ in range(count):
            low = values.astype(BF16).astype(F32)
            got.append(low)
            values = values - low
        return got

    aux = jnp.where(lane == LANES - 1, 1.0, 0.0)
    for i, piece in enumerate(pieces(lse, 3) + pieces(delta, 2)):
        moved = piece if i == 0 else pltpu.roll(piece, 16 * i, 1)
        aux = jnp.where((lane >= 16 * i) & (lane < 16 * i + 16), moved, aux)
    payload = jnp.concatenate([upstream, aux.astype(BF16)], axis=1)
    pay_out[...] = payload


def aux_masks(rows, p):
    lane = lane_iota(2 * rows)
    side = jnp.where(lax.broadcasted_iota(jnp.int32, (2 * rows, LANES), 0) < rows, 0, 8)
    own = lax.rem(lane, 16) == p + side
    return own & (lane < 48), own & (lane >= 48) & (lane < 80), lane == LANES - 1


def query_grad_kernel(n_blocks, far, chosen, *refs):
    mask, queries, payload, base, wq, prefix_k, prefix_v = refs[:7]
    all_keys = refs[7 : 7 + n_blocks]
    all_values = refs[7 + n_blocks : 7 + 2 * n_blocks]
    out, grad_ref, *own = refs[7 + 2 * n_blocks :]
    rows, width = queries.shape
    span = pl.ds(chosen[0] * LANES, len(chosen) * LANES)
    arriving = []
    if far:
        keys, values, sems = own
        for b in range(n_blocks):
            moves = [
                (all_keys[b].at[:, span], keys.at[b]),
                (all_values[b].at[:, span], values.at[b]),
            ]
            arriving.append(start_copies(moves, sems, 2 * b))
    slots = prefix_k.shape[0]
    low_half = lane_iota(rows) < HEAD_DIM
    aux = payload[:, width : width + LANES]
    aux2 = jnp.concatenate([aux, aux], axis=0)
    zero = jnp.zeros_like(aux2)

    def minus_ones(count):
        return jnp.where(lane_iota(count) < 80, -1.0, 0.0)

    left_out = (lane_iota(slots) == LANES - 1) & (mask[...] > 0.5)
    prefix_tail = jnp.where(left_out, masked_score, minus_ones(slots)).astype(BF16)
    tail = minus_ones(rows).astype(BF16)
    for n, p in enumerate(chosen):
        cols, here = lanes_of(p), lanes_of(n)
        for_scores, for_delta, for_bias = aux_masks(rows, p)
        q_wide = jnp.concatenate(
            [
                stack_pair(queries[:, cols], low_half),
                jnp.where(for_scores | for_bias, aux2, zero),
            ],
            axis=1,
        )
        d_wide = jnp.concatenate(
            [
                stack_pair(payload[:, cols], low_half),
                jnp.where(for_delta, aux2, zero),
            ],
            axis=1,
        )
        total = None
        for b in range(-1, n_blocks):
            if b < 0:
                key, value, ends = prefix_k[:, cols], prefix_v[:, cols], prefix_tail
            elif far:
                if n == 0:
                    for copy in arriving[b]:
                        copy.wait()
                key, value, ends = keys[b, :, here], values[b, :, here], tail
            else:
                key, value, ends = all_keys[b][:, cols], all_values[b][:, cols], tail
            probs = jnp.exp(dot(q_wide, jnp.concatenate([key, ends], axis=1), NT))
            products = dot(d_wide, jnp.concatenate([value, ends], axis=1), NT)
            term = dot((probs * products).astype(BF16), key)
            total = term if total is None else total + term
        both = jnp.where(low_half, total[0:rows], total[rows : 2 * rows])
        grad_ref[:, here] = (both * 0.125).astype(BF16)
    chosen_cols = slice(chosen[0] * LANES, (chosen[-1] + 1) * LANES)
    out[...] = base[...] + dot(grad_ref[...], wq[:, chosen_cols], NT)


def tall(parts, cols):
    return jnp.concatenate([part[:, cols] for part in parts], axis=0)


def key_terms(sets, q_block, d_block, aux, p):
    k_wide, v_wide = [], []
    for key, value, left_out in sets:
        low_half = lane_iota(key.shape[0]) < HEAD_DIM
        for_scores, for_delta, for_bias = aux_masks(key.shape[0], p)
        tail = jnp.where(for_scores, -1.0, 0.0)
        if left_out is not None:
            tail = jnp.where(for_bias & left_out, masked_score, tail)
        k_wide.append(jnp.concatenate([stack_pair(key, low_half), tail.astype(BF16)], axis=1))
        tail = jnp.where(for_delta, -1.0, 0.0).astype(BF16)
        v_wide.append(jnp.concatenate([stack_pair(value, low_half), tail], axis=1))
    k_wide, v_wide = jnp.concatenate(k_wide, axis=0), jnp.concatenate(v_wide, axis=0)
    probs = jnp.exp(dot(k_wide, jnp.concatenate([q_block, aux], axis=1), NT))
    products = dot(v_wide, jnp.concatenate([d_block, aux], axis=1), NT)
    value_total = dot(probs.astype(BF16), d_block)
    key_total = dot((probs * products).astype(BF16), q_block)
    terms, at = [], 0
    for key, _, _ in sets:
        rows = key.shape[0]
        low_half = lane_iota(rows) < HEAD_DIM
        for total in (key_total, value_total):
            upper, lower = total[at : at + rows], total[at + rows : at + 2 * rows]
            terms.append(jnp.where(low_half, upper, lower))
        at += 2 * rows
    return terms


def own_grad_kernel(pairs, *refs):
    keys, values, side_keys, side_values, queries, payload, prefix_k, prefix_v, mask = refs[:9]
    *outs, out, sent = refs[9:]
    width = queries.shape[1]
    slots = prefix_k.shape[0]
    aux = payload[:, width : width + LANES]
    left_out = jnp.concatenate([mask[...], mask[...]], axis=0) > 0.5
    for p in range(pairs):
        cols = lanes_of(p)
        sets = [
            (keys[:, cols], values[:, cols], None),
            (side_keys[:, cols], side_values[:, cols], None),
            (prefix_k[:, cols], prefix_v[:, cols], left_out),
        ]
        terms = key_terms(sets, queries[:, cols], payload[:, cols], aux, p)
        for ref, term in zip(outs, terms):
            ref[:, cols] = term
        out[0:slots, cols] = terms[4].astype(BF16)
        out[slots : 2 * slots, cols] = terms[5].astype(BF16)
    sent[...] = out[part_of(out.shape[0], "seq", 2, 1), :]


def part_of(height, axis, parts, flip):
    at = lax.rem(lax.axis_index(axis), parts)
    other = jnp.int32(0)
    for bit in range(parts.bit_length() - 1):
        digit = lax.rem(at // (1 << bit), 2)
        other = other + (1 << bit) * (1 - digit if (flip >> bit) % 2 else digit)
    return pl.ds(pl.multiple_of(other * (height // parts), 16), height // parts)


def scatter_kernel(axis, parts, then, terms, *refs):
    got, out, sent = refs[: parts - 1], refs[parts - 1], refs[parts:]
    total = terms[part_of(terms.shape[0], axis, parts, 0), :].astype(F32)
    for ref in got:
        total = total + ref[...].astype(F32)
    out[...] = total.astype(out.dtype)
    for i, ref in enumerate(sent):
        ref[...] = out[part_of(out.shape[0], then, len(sent) + 1, i + 1), :]


def add_kernel(terms, *refs):
    total = terms[...].astype(F32)
    for ref in refs[:-1]:
        total = total + ref[...].astype(F32)
    refs[-1][...] = total.astype(BF16)


def join_kernel(axis, parts, terms, *refs):
    out = refs[-1]
    for flip, ref in enumerate((terms,) + refs[:-1]):
        out[part_of(out.shape[0], axis, parts, flip), :] = ref[...]


def join_last_kernel(slot_count, terms, got, key_out, value_out):
    lower = lax.rem(lax.axis_index("seq"), 2) == 0
    for out, mine in ((key_out, lower), (value_out, jnp.logical_not(lower))):
        rows = jnp.where(mine, terms[...].astype(F32), got[...].astype(F32))
        out[...] = rows[0:slot_count, :]


def key_grad_kernel(pairs, n_sets, n_queries, send, *refs):
    refs = list(refs)

    def take(count):
        got = refs[:count]
        del refs[:count]
        return got

    key_sets = [take(2) for _ in range(n_sets)]
    q_refs, (pay,) = take(n_queries), take(1)
    before, outs = take(2 * n_sets), take(1 if send else 2 * n_sets)
    width = pay.shape[1] - LANES
    aux = pay[:, width : width + LANES]
    for p in range(pairs):
        cols = lanes_of(p)
        sets = [(keys[:, cols], values[:, cols], None) for keys, values in key_sets]
        terms = key_terms(sets, tall(q_refs, cols), pay[:, cols], aux, p)
        terms = [term + ref[:, cols] for term, ref in zip(terms, before)]
        if send:
            outs[0][:, cols] = terms[0].astype(BF16)
            outs[0][:, lanes_of(pairs + p)] = terms[1].astype(BF16)
        else:
            for ref, term in zip(outs, terms):
                ref[:, cols] = term


def input_grad_kernel(key_terms_ref, value_terms_ref, came, partial, wk, wv, out):
    width = out.shape[1]
    key_low = (key_terms_ref[...] + came[:, 0:width].astype(F32)).astype(BF16)
    value_low = (value_terms_ref[...] + came[:, width : 2 * width].astype(F32)).astype(BF16)
    total = partial[...] + dot(key_low, wk[...], NT) + dot(value_low, wv[...], NT)
    out[...] = total.astype(BF16)


def after(value, *others):
    return lax.optimization_barrier((value, *others))[0]


def sum_steps(dp, seq, slots, width, slot_count):
    def rows_out(count):
        return Out((count, width), BF16)

    dp_flips, part = range(1, dp), slots // dp
    last = [Out((slot_count, width), F32, "auto")] * 2
    return [
        (
            ("seq", [1]),
            functools.partial(scatter_kernel, "seq", 2, "dp"),
            [rows_out(slots)] + [rows_out(part)] * (dp - 1),
        ),
        (("dp", dp_flips), functools.partial(scatter_kernel, "dp", dp, ""), [rows_out(part)]),
        (("seq", range(2, seq, 2)), add_kernel, [rows_out(part)]),
        (("dp", dp_flips), functools.partial(join_kernel, "dp", dp), [rows_out(slots)]),
        (("seq", [1]), functools.partial(join_last_kernel, slot_count), last),
    ]


def per_device(
    hidden_in,
    task_ids,
    prefix_keys,
    prefix_values,
    query_weight,
    query_bias,
    key_weight,
    key_bias,
    value_weight,
    value_bias,
    out_weight,
    out_bias,
    norm1_gain,
    norm1_bias,
    up_weight,
    up_bias,
    down_weight,
    down_bias,
    norm2_gain,
    norm2_bias,
    out_grad,
):
    rows, width = hidden_in.shape
    pairs = width // LANES
    ff = up_weight.shape[1]
    seq = lax.axis_size("seq")
    chips = seq // 2
    slot_count = prefix_keys.shape[0]
    slots = -(-slot_count // LANES) * LANES
    loop = [*range(0, chips, 2), *range(1, chips, 2)[::-1]]
    ring = [
        (2 * loop[i] + c, 2 * loop[(i + 1) % chips] + c) for i in range(chips) for c in range(2)
    ]
    swap = [(i, i ^ 1) for i in range(seq)]

    half = rows // 2

    wide = (rows, width)

    def ring_hop(block):
        return lax.ppermute(block, "seq", ring)

    def swapped(block):
        return lax.ppermute(block, "seq", swap)

    def walk(block, use, done, between, ahead):
        here, flying = block, ring_hop(block)
        for hop in range(chips):
            if hop:
                here = after(flying, done[-1], *ahead(hop))
                if hop < chips - 1:
                    flying = ring_hop(here)
            use(hop, after(here, done[-1]))
            between.get(hop, lambda: None)()

    def walk_in_halves(block, use, done):
        halves = block[0 : rows // 2], block[rows // 2 : rows]
        flying = [ring_hop(half) for half in halves]
        other = swapped(after(block, *halves))
        hops = 2 * chips - 2
        use(0, [block])
        parts = [other]
        for step in range(hops):
            here = after(flying.pop(0), done[-1])
            if step < hops - 2:
                flying.append(ring_hop(here))
            use(step + 1, [after(part, done[-1], here) for part in parts])
            parts = [here, swapped(here)]
        use(hops + 1, [after(part, done[-1]) for part in parts])

    state = [Out((pairs, 2 * rows, LANES), F32), Out(wide, F32), Out(wide, F32)]
    far = seq > 8
    q_list, k_list, v_list, attended, held, masks, late_parts = [], [], [], [], [], [], []
    near_weights = []

    def attend(step, parts):
        late = step > 1
        kinds = (1, 2) if late or step == 1 else (0, 1, 2)
        weights = [near_weights[i] for i in kinds] if step else []
        shapes = [(parts[0].shape[0], width) if i == 0 else wide for i in kinds]
        rows_out = [Out(shape, BF16, "hbm" if far else "vmem") for shape in shapes]
        scratch = [(shape, BF16) for shape in shapes] if far else []
        scratch += [pltpu.SemaphoreType.DMA((9,))]
        early = {2: [out_weight, up_weight], 4: [down_weight]}.get(step, [])
        kernel = functools.partial(fwd_kernel, len(parts), step == 0, far, kinds, pairs, len(early))
        if step == 0:
            got = call(
                kernel,
                rows_out
                + [Out((pairs, 2 * rows, LANES), BF16, "vmem")]
                + [Out((slots, width), BF16)] * 2
                + [Out((slots, LANES), F32)]
                + [Out((width, width), BF16)] * 3
                + [Out((3, width), F32)]
                + state,
                [Arg(part) for part in parts]
                + [Arg(w, "hbm") for w in (query_weight, key_weight, value_weight)]
                + [Arg(v) for v in (query_bias, key_bias, value_bias, prefix_keys, prefix_values)]
                + [Arg(task_ids, "smem")],
                10 * rows * width * width, "attend_first", scratch, lazy=True,
            )
            masks[:] = got[6:7]
            near_weights[:] = got[7:10]
            held[:] = got[3:6] + got[10:14]
        else:
            got = call(
                kernel,
                rows_out + state,
                [Arg(part, "auto") for part in parts]
                + [Arg(w, "vmem") for w in weights + held[3:4] + held[0:1] + held[4:7] + early],
                8 * rows * width * width, "attend_%d" % len(parts), scratch, lazy=True,
            )
            held[4:7] = got[len(kinds) : len(kinds) + 3]
        if late:
            late_parts.append(parts[0])
        elif step != 1:
            q_list.append(got[0])
        k_list.append(got[len(kinds) - 2])
        v_list.append(got[len(kinds) - 1])
        attended.append(k_list[-1])

    walk_in_halves(hidden_in, attend, attended)
    prefix_k, prefix_v, state_now = held[1], held[2], held[4:7]
    q0, key_pairs = q_list[0], [k_list[0], v_list[0], k_list[1], v_list[1]]
    layer_out, res_grad, payload = call(
        functools.partial(middle_kernel, pairs, 4),
        [Out(wide, BF16, "auto"), Out(wide, F32), Out((rows, width + LANES), BF16)],
        [Arg(hidden_in)]
        + [Arg(a, "vmem") for a in state_now]
        + [Arg(a) for a in (out_grad, out_bias, norm1_gain, norm1_bias)]
        + [Arg(a) for a in (up_bias, down_bias, norm2_gain, norm2_bias)]
        + [Arg(a, "vmem") for a in (out_weight, up_weight, down_weight)],
        8 * rows * width * ff, "middle", [((rows, ff), BF16)], spare=12 * 1024 * 1024, lazy=True,
    )
    near_rows = "copy" if far else "vmem"
    prefix = [Arg(prefix_k, "vmem"), Arg(prefix_v, "vmem")]
    sums = sum_steps(lax.axis_size("dp"), seq, slots, width, slot_count)
    trading, pending, done = [], [], [res_grad]

    def trade():
        if sums:
            (axis, flips), _, _ = sums[0]
            kept, sent = trading[0], trading[1:] or trading[:1] * len(flips)
            partners = [[(i, i ^ f) for i in range(lax.axis_size(axis))] for f in flips]
            pending[:] = [lax.ppermute(b, axis, p) for b, p in zip(sent, partners)]

    def exchange():
        _, job, outs = sums.pop(0)
        got = [trading[0]] + [after(g, done[-1]) for g in pending]
        pending[:] = []
        return job, outs, [Arg(a, "auto") for a in got]

    partial_now = [res_grad]

    def query_grads(first_pair, each):
        chosen = tuple(range(first_pair, first_pair + each))
        scratch = [((rows, each * LANES), BF16)]
        if far:
            scratch += [((seq, rows, each * LANES), BF16)] * 2 + [pltpu.SemaphoreType.DMA((2 * seq,))]
        partial_now[:] = call(
            functools.partial(query_grad_kernel, seq, far, chosen),
            [Out(wide, F32)],
            [Arg(masks[0], "vmem"), Arg(q0, near_rows), Arg(after(payload, done[-1]), "vmem")]
            + [Arg(partial_now[0], "vmem"), Arg(query_weight, "vmem")]
            + prefix
            + [Arg(a, "hbm" if far else "vmem") for a in k_list + v_list],
            24 * rows * rows * seq * each * LANES, "query_grad_%d" % first_pair, scratch,
        )
        done.append(partial_now[0])

    key_state = []

    def key_grads(hop, part):
        near_keys = [Arg(a, near_rows) for a in key_pairs]
        if hop == 0:
            got = call(
                functools.partial(own_grad_kernel, pairs),
                [Out(wide, F32)] * 4 + [Out((2 * slots, width), BF16), Out((slots, width), BF16)],
                near_keys
                + [Arg(q0, near_rows), Arg(part, "vmem"), *prefix, Arg(masks[0], "vmem")],
                80 * rows * rows * width, "own_grads",
            )
            key_state[:], trading[:] = got[:4], got[4:]
            done.append(key_state[0])
            return trade()
        q_blocks = [Arg(a, near_rows) for a in q_rows(hop)]

        def terms(sets, send, side=None):
            return call(
                functools.partial(key_grad_kernel, pairs, len(sets), len(q_blocks), send),
                [Out((rows, 2 * width), BF16)] if send else [Out(wide, F32)] * (2 * len(sets)),
                [near_keys[2 * i + j] for i in sets for j in range(2)]
                + q_blocks
                + [Arg(part, "auto")]
                + [Arg(key_state[2 * i + j], "vmem") for i in sets for j in range(2)],
                32 * rows * rows * width * len(sets), "key_grad_%d" % len(sets), side=side,
            )

        if hop < chips - 1:
            side = exchange() if hop == 2 else None
            got = terms((0, 1), False, side)
            if side is not None:
                got, trading[:] = got
                trade()
            key_state[:] = got
            done.append(key_state[0])
            return
        (sending,) = terms((1,), True)
        done.append(sending)
        came = swapped(sending)
        near_keys[0] = Arg(after(near_keys[0].array, sending), near_rows)
        own = terms((0,), False)
        done.append(own[0])
        key_state[:], trading[:] = call(
            input_grad_kernel,
            [Out(wide, BF16, "auto")],
            [Arg(a, "vmem") for a in own]
            + [Arg(after(came, own[0]), "auto")]
            + [Arg(a, "vmem") for a in (partial_now[0], key_weight, value_weight)],
            4 * rows * width * width, "input_grad", side=exchange(),
        )

    def settle():
        job, outs, args = exchange()
        trading[:] = call(job, outs, args, 0, "settle")
        done.append(trading[0])
        trade()

    def q_rows(hop):
        early = (len(q_list) - 1) // 2
        return q_list[2 * hop - 1 : 2 * hop + 1] if hop <= early else late_list[hop - early - 1 :][:1]

    late_list = []

    def late_queries(first, last):
        for i in range(first, last, 2):
            (block,) = call(
                late_queries_kernel,
                [Out(wide, BF16)],
                [Arg(after(part, done[-1]), "auto") for part in late_parts[i : i + 2]]
                + [Arg(query_weight, "vmem"), Arg(held[3], "vmem")],
                2 * rows * width * width, "late_queries",
            )
            late_list.append(block)
            done.append(block)

    between = {
        0: lambda: (
            late_queries(0, 4),
            settle(),
            late_queries(4, len(late_parts)),
            settle(),
        ),
        1: lambda: query_grads(0, 5),
        2: lambda: (query_grads(5, 3), settle()),
    }
    walk(payload, key_grads, done, between, lambda hop: pending if hop == 2 else [])
    (result,) = key_state
    return (layer_out, result, *trading)


def solution(mesh):
    rows = P(("dp", "seq"), None)
    return jax.shard_map(
        per_device,
        mesh=mesh,
        in_specs=(rows, P("dp")) + (P(),) * 18 + (rows,),
        out_specs=(rows, rows, P(), P()),
        check_vma=False,
    )
```
